256 devices in a mesh: dp: 64 (over z, x, core), mp: 4 (over y).
Axes of the slice: x: 4, y: 4, z: 8, core: 2. Of those that a mesh axis runs over, the one named last changes fastest.
Arguments:
- view_a: bfloat16 [20480, 4096], P('dp', 'mp'), may hold values from -80 to 80
- view_b: bfloat16 [20480, 4096], P('dp', 'mp'), may hold values from -80 to 80
Outputs:
- grad_a: bfloat16 [20480, 4096], P('dp', 'mp')
- grad_b: bfloat16 [20480, 4096], P('dp', 'mp')
- loss: float32 [], replicated
The draws below stay inside these ranges and needn't reach their ends.
All inputs are finite; a program needn't handle non-finite values.
Results may differ from the reference program's by a relative error of at most 0.0035.
The reference program's roundings to bfloat16 on the way (of `slope16`) count: a program that leaves them out, or rounds other values in their place, can miss the bound.
Values may be sent and summed in bfloat16 or wider, within the bound.
A program may use at most 64 MiB of HBM per device.

```python
import math
import jax
import jax.numpy as jnp
from jax import lax

D = 4096
FRAMES = 20480


def rising(growth):
    position = jnp.arange(FRAMES, dtype=jnp.float32) / max(FRAMES - 1, 1)
    return (1.0 + growth * position)[:, None]


def common(key, first_half, second_half, row_top, row_growth):
    first_key = jax.random.fold_in(key, 101)
    second_key = jax.random.fold_in(key, 102)
    order_key = jax.random.fold_in(key, 103)
    left_key = jax.random.fold_in(key, 104)
    right_key = jax.random.fold_in(key, 105)
    row_key = jax.random.fold_in(key, 106)
    share_key = jax.random.fold_in(key, 107)
    integer_field = jax.random.randint(first_key, (FRAMES, D), -first_half, first_half + 1) + jax.random.randint(second_key, (FRAMES, D), -second_half, second_half + 1)
    integer_field = integer_field.astype(jnp.float32)
    feature_order = jax.random.permutation(order_key, D)
    first_size = 1 << (D.bit_length() - 1) // 2
    second_size = D // first_size
    left_mix = jax.random.randint(left_key, (first_size, first_size), -3, 4).astype(jnp.float32)
    right_mix = jax.random.randint(right_key, (second_size, second_size), -3, 4).astype(jnp.float32)
    mixed_grid = integer_field[:, feature_order].reshape(FRAMES, first_size, second_size)
    mixed_grid = jnp.einsum('fpq,pr->frq', mixed_grid, left_mix, precision=lax.Precision.HIGHEST)
    mixed_grid = jnp.einsum('frq,qs->frs', mixed_grid, right_mix, precision=lax.Precision.HIGHEST)
    latent = integer_field * (1.0 / 16.0) + mixed_grid.reshape(FRAMES, D) * (0.7 / (64.0 * math.sqrt(D)))
    position = jnp.arange(FRAMES, dtype=jnp.float32) / max(FRAMES - 1, 1)
    row_scale = jnp.exp(jax.random.uniform(row_key, (FRAMES, 1), jnp.float32, 0.0, row_top)) * jnp.sqrt(1.0 + row_growth * position)[:, None]
    trend_share = jax.random.uniform(share_key, (1, D), jnp.float32, -0.3, 0.3)
    return (latent * row_scale, trend_share)


def draw_view_a(key, part):
    latent, trend_share = common(key, 16, 16, 1.1, 2.0)
    trend = rising(2.0)
    key = jax.random.fold_in(key, 1)
    feature_scale = jnp.exp(jax.random.uniform(key, (1, D), jnp.float32, -1.0, 0.8))
    values = feature_scale * (latent + trend_share * trend)
    return jnp.clip(values, -78.0, 78.0).astype(jnp.bfloat16)


def draw_view_b(key, part):
    latent, trend_share = common(key, 16, 16, 1.1, 2.0)
    trend = rising(2.0)
    key = jax.random.fold_in(key, 2)
    scale_key, noise_key, level_key = jax.random.split(key, 3)
    feature_scale = jnp.exp(jax.random.uniform(scale_key, (1, D), jnp.float32, -1.0, 0.8))
    noise_level = jnp.exp(jax.random.uniform(level_key, (1, D), jnp.float32, -2.5, 0.0))
    noise = jax.random.truncated_normal(noise_key, -4.0, 4.0, (FRAMES, D), jnp.float32)
    values = feature_scale * (latent + noise_level * noise + trend_share * trend)
    return jnp.clip(values, -78.0, 78.0).astype(jnp.bfloat16)


def setup_inputs(seed: int = 0) -> dict:
    streams_of = jax.random.split(jax.random.key(seed), 3)
    return {
        "view_a": draw_view_a(jax.random.fold_in(streams_of[2], 71), 0),
        "view_b": draw_view_b(jax.random.fold_in(streams_of[2], 71), 0),
    }


epsilon = 1e-05
off_weight = 0.0051

def standard(view):
    values = view.astype(jnp.float32)
    center = lax.optimization_barrier(jnp.mean(values, axis=0))
    spread = lax.optimization_barrier(jnp.mean((values - center) ** 2, axis=0))
    inv_std = lax.rsqrt(spread + epsilon)
    return ((values - center) * inv_std, inv_std)

def backward(back, normed, inv_std):
    return (inv_std * (back - lax.optimization_barrier(jnp.mean(back, axis=0)) - normed * lax.optimization_barrier(jnp.mean(back * normed, axis=0)))).astype(jnp.bfloat16)

def reference(view_a, view_b):
    normed_a, inv_a = standard(view_a)
    normed_b, inv_b = standard(view_b)
    normed_a16 = normed_a.astype(jnp.bfloat16)
    normed_b16 = normed_b.astype(jnp.bfloat16)
    corr = lax.dot_general(normed_a16, normed_b16, (((0,), (0,)), ((), ())), preferred_element_type=jnp.float32) / FRAMES
    index = jnp.arange(D, dtype=jnp.int32)
    diagonal = index[:, None] == index[None, :]
    loss = jnp.sum(jnp.where(diagonal, (1.0 - corr) ** 2, off_weight * corr * corr))
    slope16 = jnp.where(diagonal, -2.0 * (1.0 - corr), 2.0 * off_weight * corr).astype(jnp.bfloat16)
    back_a = lax.dot_general(normed_b16, slope16, (((1,), (1,)), ((), ())), preferred_element_type=jnp.float32)
    back_b = jnp.dot(normed_a16, slope16, preferred_element_type=jnp.float32)
    return (backward(back_a, normed_a, inv_a), backward(back_b, normed_b, inv_b), loss)
```

```python
import functools

import jax
import jax.numpy as jnp
from jax import lax
from jax.experimental import pallas as pl
from jax.experimental.pallas import tpu as pltpu
from jax.sharding import PartitionSpec as P

epsilon = 1e-05
off_weight = 0.0051

MESH = pl.DeviceIdType.MESH
f32 = jnp.float32
bf16 = jnp.bfloat16

SHIFT = (0, 1, 3, 2)
SLOT = (0, 1, 3, 2)


tiny = 1e-37


def encode(v):
    q = v * v
    q = q * q
    return jnp.where(v < 0.0, -q, q).astype(bf16)


def decode(y):
    y = y.astype(f32)
    q = jnp.abs(y)
    q = q * lax.rsqrt(jnp.maximum(q, tiny))
    q = q * lax.rsqrt(jnp.maximum(q, tiny))
    return jnp.where(y < 0.0, -q, q)


def kernel(
    nx, nz, ny, total,
    a_ref, b_ref, ga_ref, gb_ref, loss_ref,
    na16, nb16, na, nat, nb, part, slope, back_a, part_b, sum_b, full_b,
    stat_c, stat_x, stat_z, diag_c, diag_x, diag_z,
    mean_b16, extra_y, extra_c, extra_a, row_acc,
    rx_p1, rx_m1, rx_p2, rx_m2, rz_p1, rz_m1, rz_p2, rz_m2,
    sx_p1, sx_m1, sx_p2, sx_m2, sz_p1, sz_m1, sz_p2, sz_m2,
    ry_p1, ry_m1, ry_p2, ry_m2, sy_p1, sy_m1, sy_p2, sy_m2, recv_a,
    send_sems, recv_sems,
):
    frames, width = a_ref.shape
    both = 2 * frames
    half = width // 2
    quarter = half // 2
    slots = ny
    dp = lax.axis_index("dp")
    m = lax.axis_index("mp")
    c = lax.rem(dp, 2)
    x = lax.rem(dp // 2, nx)
    z = dp // (2 * nx)

    def device(dc=0, dx=0, dz=0, dy=0):
        there = (lax.rem(z + dz, nz) * nx + lax.rem(x + dx, nx)) * 2
        there = there + (1 - c if dc else c)
        return (there, lax.rem(m + dy, ny))

    partner = device(dc=1)
    peers_x = [device(dx=k) for k in range(1, nx)]
    peers_z = [device(dz=k) for k in range(1, nz)]
    peers_y = [device(dy=k) for k in range(1, ny)]
    everyone = [partner] + peers_x + peers_z + peers_y

    barrier = pltpu.get_barrier_semaphore()
    for peer in everyone:
        pl.semaphore_signal(barrier, inc=1, device_id=peer, device_id_type=MESH)

    started = []

    def send(src, dst, peer):
        at = len(started)
        copy = pltpu.make_async_remote_copy(
            src_ref=src,
            dst_ref=dst,
            send_sem=send_sems.at[at],
            recv_sem=recv_sems.at[at],
            device_id=peer,
            device_id_type=MESH,
        )
        copy.start()
        started.append(copy)
        return copy

    def exchange(buf, mine, peers):
        copies = [send(buf.at[mine], buf.at[mine], peer) for peer in peers]
        for copy in copies:
            copy.wait_recv()

    def column_sum(fn):
        step = 64
        def body(i, acc):
            return acc + jnp.sum(fn(pl.ds(i * step, step)), axis=0, keepdims=True)
        return lax.fori_loop(0, frames // step, body, jnp.zeros((1, width), f32))

    for view, ref in enumerate((a_ref, b_ref)):
        center = column_sum(lambda rows: ref[rows, :].astype(f32)) / frames
        def deviation(rows, ref=ref, center=center):
            dev = ref[rows, :].astype(f32) - center
            return dev * dev
        stat_c[c, 0, view : view + 1, :] = center
        stat_c[c, 1, view : view + 1, :] = column_sum(deviation)

    pl.semaphore_wait(barrier, len(everyone))

    def merge(buf, members, count):
        center = sum(buf[i, 0] for i in range(members)) * (1.0 / members)
        spread = sum(buf[i, 1] for i in range(members))
        shift = sum((buf[i, 0] - center) ** 2 for i in range(members))
        return center, spread + count * shift

    exchange(stat_c, c, [partner])
    stat_x[x, 0], stat_x[x, 1] = merge(stat_c, 2, float(frames))
    exchange(stat_x, x, peers_x)
    stat_z[z, 0], stat_z[z, 1] = merge(stat_x, nx, float(frames * 2))
    exchange(stat_z, z, peers_z)
    center, spread = merge(stat_z, nz, float(frames * 2 * nx))
    inv = lax.rsqrt(spread / total + epsilon)
    center_a, center_b = center[0:1], center[1:2]
    inv_a, inv_b = inv[0:1], inv[1:2]

    def standardize(i, acc):
        step = 64
        rows = pl.ds(pl.multiple_of(i * step, step), step)
        wide_a = (a_ref[rows, :].astype(f32) - center_a) * inv_a
        wide_b = (b_ref[rows, :].astype(f32) - center_b) * inv_b
        short_a, short_b = wide_a.astype(bf16), wide_b.astype(bf16)
        here = pl.ds(pl.multiple_of(c * frames + i * step, step), step)
        na16[rows, :] = short_a
        nb16[rows, :] = short_b
        back_a16, back_b16 = short_a.astype(f32), short_b.astype(f32)
        terms = (back_a16, back_b16, back_a16 * back_b16, wide_a * back_b16, wide_b * back_a16)
        return tuple(s + jnp.sum(t, axis=0, keepdims=True) for s, t in zip(acc, terms))

    sums = lax.fori_loop(0, frames // 64, standardize, (jnp.zeros((1, width), f32),) * 5)
    diag_c[c, 0, 0:1, :] = sums[0]
    diag_c[c, 0, 1:2, :] = sums[1]
    diag_c[c, 1, 0:1, :] = sums[2]
    diag_c[c, 1, 1:2, :] = jnp.zeros((1, width), f32)
    diag_c[c, 2, 0:1, :] = sums[3]
    diag_c[c, 2, 1:2, :] = sums[4]

    own_frames = pl.ds(pl.multiple_of(c * frames, 64), frames)
    other_frames = pl.ds(pl.multiple_of((1 - c) * frames, 64), frames)
    own_half = pl.ds(pl.multiple_of(c * half, 128), half)
    other_half = pl.ds(pl.multiple_of((1 - c) * half, 128), half)
    swap_b = send(nb16.at[:, other_half], nb.at[0, own_frames, :], partner)
    swap_a = send(na16, na.at[own_frames, :], partner)
    na[own_frames, :] = na16[...]
    nb[0, own_frames, :] = nb16[:, own_half]
    swap_b.wait_recv()

    up, down = device(dy=1), device(dy=ny - 1)
    first = [send(nb.at[0], nb.at[2], up), send(nb.at[0], nb.at[1], down)]
    swap_a.wait_recv()
    for i in range(width // 128):
        cols = pl.ds(i * 128, 128)
        nat[cols, :] = jnp.transpose(na[:, cols].astype(f32)).astype(bf16)

    exchange(diag_c, c, [partner])
    diag_x[x] = sum(diag_c[i] for i in range(2))
    exchange(diag_x, x, peers_x)
    diag_z[z] = sum(diag_x[i] for i in range(nx))
    exchange(diag_z, z, peers_z)
    diag = sum(diag_z[i] for i in range(nz)) / total
    mean_a16, mean_own_b16 = diag[0, 0:1], diag[0, 1:2]
    corr_ii = diag[1, 0:1]
    cross_a, cross_b = diag[2, 0:1], diag[2, 1:2]
    slope_ii = (-2.0 * (1.0 - corr_ii)).astype(bf16).astype(f32)

    def pick(row):
        return jnp.where(c == 0, row[:, :half], row[:, half:])

    mean_b16[0] = pick(mean_own_b16)
    share_b = [send(mean_b16.at[0], mean_b16.at[SLOT[ny - k]], peers_y[k - 1]) for k in range(1, ny)]

    for copy in first:
        copy.wait_recv()
    low, high = pl.ds(0, frames), pl.ds(frames, frames)
    second = [
        send(nb.at[2, low], nb.at[3, low], up),
        send(nb.at[1, high], nb.at[3, high], down),
    ]

    def correlate(p):
        def body(i, _):
            rows = pl.ds(pl.multiple_of(i * 256, 256), 256)
            part[p, rows, :] = jnp.dot(
                nat[rows, :], nb[p], preferred_element_type=f32
            )
            return 0
        lax.fori_loop(0, width // 256, body, 0)

    for p in range(3):
        correlate(p)
    for copy in second:
        copy.wait_recv()
    correlate(3)

    left, right = pl.ds(0, quarter), pl.ds(quarter, quarter)
    every = pl.ds(0, half)

    def sweep(group, rows, fn):
        first, count = group
        step = min(rows, 32)
        def body(i, _):
            p = first + i // (rows // step)
            at = lax.rem(i, rows // step) * step
            fn(p, pl.multiple_of(at, 16), step)
            return 0
        lax.fori_loop(0, count * (rows // step), body, 0)

    def reduce_chain(group, base, rows, n, at, plus, minus, off, bufs):
        out_p1, out_m1, out_p2, out_m2, in_p1, in_m1, in_p2, in_m2 = bufs
        far = n // 2
        some = pl.ds(*group)
        window = pl.ds(off, rows)

        def pack(s, source, cols, out1, out2, in1, in2):
            def fn(p, r, step):
                there = pl.ds(pl.multiple_of(source + r, 16), step)
                here = pl.ds(pl.multiple_of(off + r, 16), step)
                if s == 1:
                    out1[p, here, :] = encode(part[p, there, cols])
                    return
                if s > 2:
                    out2[s - 2, p, here, :] = encode(part[p, there, :] + decode(in2[s - 3, p, here, :]))
                    return
                rest = right if cols is left else left
                out2[0, p, here, cols] = encode(part[p, there, cols] + decode(in1[p, here, :]))
                out2[0, p, here, rest] = encode(part[p, there, rest])
            sweep(group, rows, fn)

        for s in range(1, far + 1):
            distance = far + 1 - s
            pack(s, base + lax.rem(at + distance, n) * rows, left, out_p1, out_p2, in_p1, in_p2)
            pack(s, base + lax.rem(at + n - distance, n) * rows, right, out_m1, out_m2, in_m1, in_m2)
            def view(first, later):
                return first.at[some, window] if s == 1 else later.at[s - 2, some, window]
            go = [
                send(view(out_p1, out_p2), view(in_p1, in_p2), plus),
                send(view(out_m1, out_m2), view(in_m1, in_m2), minus),
            ]
            yield
            for copy in go:
                copy.wait_recv()

        def finish(p, r, step):
            there = pl.ds(pl.multiple_of(base + at * rows + r, 16), step)
            here = pl.ds(pl.multiple_of(off + r, 16), step)
            part[p, there, :] += decode(in_p2[far - 2, p, here, :]) + decode(in_m2[far - 2, p, here, :])
        sweep(group, rows, finish)

    def gather_chain(base, rows, n, at, plus, minus):
        far = n // 2
        for s in range(1, far + 1):
            cols_p, cols_m = (left, right) if s == far else (every, every)
            from_p = base + lax.rem(at + n - (s - 1), n) * rows
            from_m = base + lax.rem(at + (s - 1), n) * rows
            there_p = pl.ds(pl.multiple_of(from_p, 16), rows)
            there_m = pl.ds(pl.multiple_of(from_m, 16), rows)
            ref_p = slope.at[:, there_p, cols_p]
            ref_m = slope.at[:, there_m, cols_m]
            go = [send(ref_p, ref_p, plus), send(ref_m, ref_m, minus)]
            yield
            for copy in go:
                copy.wait_recv()

    def in_turn(chains):
        live = list(chains)
        while live:
            for chain in list(live):
                if next(chain, live) is live:
                    live.remove(chain)

    plus_x, minus_x = device(dx=1), device(dx=nx - 1)
    plus_z, minus_z = device(dz=1), device(dz=nz - 1)
    top = width // 2
    rows_x, rows_z, rows_o = top // nx, top // nz, top // (nx * nz)
    base_x = x * rows_x
    base_z = top + z * rows_z

    bufs_x = (sx_p1, sx_m1, sx_p2, sx_m2, rx_p1, rx_m1, rx_p2, rx_m2)
    bufs_z = (sz_p1, sz_m1, sz_p2, sz_m2, rz_p1, rz_m1, rz_p2, rz_m2)

    def one_way(group):
        yield from reduce_chain(group, 0, rows_x, nx, x, plus_x, minus_x, 0, bufs_x)
        yield from reduce_chain(group, base_x, rows_o, nz, z, plus_z, minus_z, rows_z, bufs_z)

    def other_way(group):
        yield from reduce_chain(group, top, rows_z, nz, z, plus_z, minus_z, 0, bufs_z)
        yield from reduce_chain(group, base_z, rows_o, nx, x, plus_x, minus_x, rows_x, bufs_x)

    in_turn([one_way((0, slots)), other_way((0, slots))])

    own_x = base_x + z * rows_o
    own_z = base_z + x * rows_o
    row_ids = lax.broadcasted_iota(jnp.int32, (rows_o, half), 0)
    col_ids = lax.broadcasted_iota(jnp.int32, (rows_o, half), 1)
    for base in (own_x, own_z):
        rows = pl.ds(pl.multiple_of(base, 16), rows_o)
        for p in range(slots):
            corr = part[p, rows, :] / total
            value = 2.0 * off_weight * corr
            if p == 0:
                value = jnp.where(row_ids + base == col_ids + c * half, 0.0, value)
            slope[p, rows, :] = value.astype(bf16)

    def one_way():
        yield from gather_chain(base_x, rows_o, nz, z, plus_z, minus_z)
        yield from gather_chain(0, rows_x, nx, x, plus_x, minus_x)

    def other_way():
        yield from gather_chain(base_z, rows_o, nx, x, plus_x, minus_x)
        yield from gather_chain(top, rows_z, nz, z, plus_z, minus_z)

    in_turn([one_way(), other_way()])
    for copy in share_b:
        copy.wait_recv()

    scale = 1.0 / (2.0 * off_weight)
    row_acc[...] = jnp.zeros_like(row_acc)
    loss_here = jnp.zeros((1, half), f32)
    loss_diag = jnp.sum((1.0 - pick(corr_ii)) ** 2, axis=1, keepdims=True)
    ext_a = jnp.broadcast_to(mean_a16, (16, width)).astype(bf16)
    mean_a = jnp.zeros((16, width), f32)
    inner_b = []
    mean_b = []
    for p in range(slots):
        def body(i, acc, p=p):
            rows = pl.ds(pl.multiple_of(i * 32, 32), 32)
            s = slope[p, rows, :].astype(f32)
            s = s * s
            row_acc[rows, :] += sum(s[:, k * 128 : (k + 1) * 128] for k in range(half // 128))
            return acc + jnp.sum(s, axis=0, keepdims=True)
        square = lax.fori_loop(0, width // 32, body, jnp.zeros((1, half), f32))
        inner_b.append(square * scale)
        loss_here = loss_here + square
        mean_b.append(jnp.dot(ext_a, slope[p], preferred_element_type=f32)[0:1])
        ext_b = jnp.broadcast_to(mean_b16[p], (16, half)).astype(bf16)
        mean_a = mean_a + lax.dot_general(
            ext_b, slope[p], (((1,), (1,)), ((), ())), preferred_element_type=f32)
    loss_off = jnp.sum(loss_here, axis=1, keepdims=True) * (off_weight * scale * scale)
    loss_row = jnp.broadcast_to(loss_off + loss_diag, (1, half))
    for p in range(slots):
        block = extra_y.at[ny + p] if p else extra_y.at[m]
        block[0:1, :] = mean_b[p]
        block[1:2, :] = inner_b[p]
        block[2:3, :] = loss_row
        block[3:4, :] = jnp.zeros((1, half), f32)
    share_y = [
        send(extra_y.at[ny + SLOT[k]], extra_y.at[m], peers_y[k - 1]) for k in range(1, ny)
    ]
    inner_a = jnp.sum(jnp.transpose(row_acc[...]), axis=0, keepdims=True) * scale
    extra_a[c, 0:1, :] = mean_a[0:1]
    extra_a[c, 1:2, :] = inner_a
    share_a = send(extra_a.at[c], extra_a.at[c], partner)

    def back_to_b(p):
        def body(i, _):
            cols = pl.ds(pl.multiple_of(i * 256, 256), 256)
            part_b[p, :, cols] = jnp.dot(
                na[...], slope[p, :, cols], preferred_element_type=f32
            )
            return 0
        lax.fori_loop(0, half // 256, body, 0)

    back_to_b(3)
    def first_y(i, _):
        here = pl.ds(pl.multiple_of(i * 32, 32), 32)
        there = pl.ds(pl.multiple_of(i * 32 + frames, 32), 32)
        sy_p1[here, :] = encode(part_b[3, here, :])
        sy_m1[here, :] = encode(part_b[3, there, :])
        return 0

    lax.fori_loop(0, frames // 32, first_y, 0)
    far = [send(sy_p1, ry_p1, up), send(sy_m1, ry_m1, down)]
    back_to_b(1)
    back_to_b(2)

    def back_to_a(i, _):
        cols = pl.ds(pl.multiple_of(i * 256, 256), 256)
        acc = None
        for p in range(slots):
            term = lax.dot_general(
                nb[p], slope[p, cols, :], (((1,), (1,)), ((), ())), preferred_element_type=f32)
            acc = term if acc is None else acc + term
        back_a[:, cols] = acc
        return 0

    for copy in far:
        copy.wait_recv()

    def second_y(i, _):
        here = pl.ds(pl.multiple_of(i * 32, 32), 32)
        there = pl.ds(pl.multiple_of(i * 32 + frames, 32), 32)
        sy_p2[here, :] = encode(part_b[1, here, :] + decode(ry_p1[here, :]))
        sy_p2[there, :] = encode(part_b[1, there, :])
        sy_m2[here, :] = encode(part_b[2, here, :])
        sy_m2[there, :] = encode(part_b[2, there, :] + decode(ry_m1[here, :]))
        return 0

    lax.fori_loop(0, frames // 32, second_y, 0)
    near = [send(sy_p2, ry_p2, up), send(sy_m2, ry_m2, down)]
    lax.fori_loop(0, width // 256, back_to_a, 0)
    swap_back = send(back_a.at[other_frames, :], recv_a, partner)
    back_to_b(0)
    for copy in near:
        copy.wait_recv()

    def add_last(i, _):
        rows = pl.ds(pl.multiple_of(i * 32, 32), 32)
        sum_b[rows, :] = (
            part_b[0, rows, :] + decode(ry_p2[rows, :]) + decode(ry_m2[rows, :])
        )
        return 0

    lax.fori_loop(0, both // 32, add_last, 0)
    swap_b2 = send(sum_b.at[other_frames, :], full_b.at[:, own_half], partner)
    for copy in share_y:
        copy.wait_recv()
    extra_c[c] = sum(extra_y[i] for i in range(ny))
    share_c = send(extra_c.at[c], extra_c.at[c], partner)
    full_b[:, own_half] = sum_b[own_frames, :]

    share_a.wait_recv()
    last_a = extra_a[0] + extra_a[1]
    mean_a = last_a[0:1] + mean_own_b16 * slope_ii
    inner_a = last_a[1:2] + cross_a * slope_ii
    swap_back.wait_recv()

    def finish_a(i, _):
        rows = pl.ds(pl.multiple_of(i * 32, 32), 32)
        here = pl.ds(pl.multiple_of(c * frames + i * 32, 32), 32)
        wide = (a_ref[rows, :].astype(f32) - center_a) * inv_a
        back = back_a[here, :] + recv_a[rows, :] + slope_ii * nb16[rows, :].astype(f32)
        ga_ref[rows, :] = (inv_a * (back - mean_a - wide * inner_a)).astype(bf16)
        return 0

    lax.fori_loop(0, frames // 32, finish_a, 0)

    share_c.wait_recv()
    mean_b = jnp.concatenate([extra_c[0, 0:1], extra_c[1, 0:1]], axis=1) + mean_a16 * slope_ii
    inner_b = jnp.concatenate([extra_c[0, 1:2], extra_c[1, 1:2]], axis=1) + cross_b * slope_ii
    loss_ref[...] = jnp.broadcast_to(extra_c[0, 2:3, :128] + extra_c[1, 2:3, :128], (8, 128))
    swap_b2.wait_recv()

    def finish_b(i, _):
        rows = pl.ds(pl.multiple_of(i * 32, 32), 32)
        wide = (b_ref[rows, :].astype(f32) - center_b) * inv_b
        back = full_b[rows, :] + slope_ii * na16[rows, :].astype(f32)
        gb_ref[rows, :] = (inv_b * (back - mean_b - wide * inner_b)).astype(bf16)
        return 0

    lax.fori_loop(0, frames // 32, finish_b, 0)
    for copy in started:
        copy.wait_send()


def solution(mesh):
    ny = mesh.shape["mp"]
    members = mesh.shape["dp"]
    nx = ny
    nz = members // (2 * nx)

    def per_device(view_a, view_b):
        frames, width = view_a.shape
        both, half = 2 * frames, width // 2
        quarter = half // 2
        top = width // 2
        rows_x, rows_z, rows_o = top // nx, top // nz, top // (nx * nz)
        vmem = pltpu.VMEM
        rings = []
        scratch = [
            vmem((frames, width), bf16),
            vmem((frames, width), bf16),
            vmem((both, width), bf16),
            vmem((width, both), bf16),
            vmem((ny, both, half), bf16),
            vmem((ny, width, half), f32),
            vmem((ny, width, half), bf16),
            vmem((both, width), f32),
            vmem((ny, both, half), f32),
            vmem((both, half), f32),
            vmem((frames, width), f32),
            vmem((2, 2, 2, width), f32),
            vmem((nx, 2, 2, width), f32),
            vmem((nz, 2, 2, width), f32),
            vmem((2, 3, 2, width), f32),
            vmem((nx, 3, 2, width), f32),
            vmem((nz, 3, 2, width), f32),
            vmem((ny, 1, half), f32),
            vmem((2 * ny, 4, half), f32),
            vmem((2, 4, half), f32),
            vmem((2, 2, width), f32),
            vmem((width, 128), f32),
        ]
        for rows, n in ((rows_x + rows_o, nx), (rows_z + rows_o, nz)):
            ring = [vmem((ny, rows, quarter), bf16)] * 2 + [vmem((n // 2 - 1, ny, rows, half), bf16)] * 2
            rings.append(ring)
        ring_y = [vmem((frames, half), bf16)] * 2 + [vmem((both, half), bf16)] * 2
        scratch += rings[0] + rings[1] + rings[0] + rings[1] + ring_y + ring_y + [
            vmem((frames, width), f32),
            pltpu.SemaphoreType.DMA((110,)),
            pltpu.SemaphoreType.DMA((110,)),
        ]
        grad_a, grad_b, loss = pl.pallas_call(
            functools.partial(kernel, nx, nz, ny, float(frames * members)),
            out_shape=(
                jax.ShapeDtypeStruct((frames, width), bf16),
                jax.ShapeDtypeStruct((frames, width), bf16),
                jax.ShapeDtypeStruct((8, 128), f32),
            ),
            in_specs=[pl.BlockSpec(memory_space=vmem)] * 2,
            out_specs=[pl.BlockSpec(memory_space=vmem)] * 3,
            scratch_shapes=scratch,
            compiler_params=pltpu.CompilerParams(
                collective_id=0, has_side_effects=True, vmem_limit_bytes=56 * 1024 * 1024
            ),
            cost_estimate=pl.CostEstimate(
                flops=3 * 2 * both * width * half * ny, bytes_accessed=4 * frames * width * 2,
                transcendentals=0),
        )(view_a, view_b)
        return grad_a, grad_b, loss[0, 0]

    placed = P("dp", "mp")
    return jax.shard_map(
        per_device,
        mesh=mesh,
        in_specs=(placed, placed),
        out_specs=(placed, placed, P()),
        check_vma=False,
    )
```

```python
import functools

import jax
import jax.numpy as jnp
from jax import lax
from jax.experimental import pallas as pl
from jax.experimental.pallas import tpu as pltpu
from jax.sharding import PartitionSpec as P

epsilon = 1e-05
off_weight = 0.0051

MESH = pl.DeviceIdType.MESH
f32 = jnp.float32
bf16 = jnp.bfloat16

SHIFT = (0, 1, 3, 2)
SLOT = (0, 1, 3, 2)


tiny = 1e-37


def encode(v):
    q = v * v
    q = q * q
    return jnp.where(v < 0.0, -q, q).astype(bf16)


def decode(y):
    y = y.astype(f32)
    q = jnp.abs(y)
    q = q * lax.rsqrt(jnp.maximum(q, tiny))
    q = q * lax.rsqrt(jnp.maximum(q, tiny))
    return jnp.where(y < 0.0, -q, q)


def kernel(
    nx, nz, ny, total,
    a_ref, b_ref, ga_ref, gb_ref, loss_ref,
    nb16, na, nat, nb, part, slope, back_a, part_b, sum_b, full_b,
    stat_c, stat_x, stat_z, diag_c, diag_x, diag_z, diag_f,
    mean_b16, square, extra_y, extra_c, extra_a, row_acc,
    rx_p1, rx_m1, rx_p2, rx_m2, rz_p1, rz_m1, rz_p2, rz_m2,
    sx_p1, sx_m1, sx_p2, sx_m2, sz_p1, sz_m1, sz_p2, sz_m2,
    ry_p1, ry_m1, ry_p2, ry_m2, sy_p1, sy_m1, sy_p2, sy_m2, recv_a,
    send_sems, recv_sems,
):
    frames, width = a_ref.shape
    both = 2 * frames
    half = width // 2
    slots = ny
    dp = lax.axis_index("dp")
    m = lax.axis_index("mp")
    c = lax.rem(dp, 2)
    x = lax.rem(dp // 2, nx)
    z = dp // (2 * nx)

    def device(dc=0, dx=0, dz=0, dy=0):
        there = (lax.rem(z + dz, nz) * nx + lax.rem(x + dx, nx)) * 2
        there = there + (1 - c if dc else c)
        return (there, lax.rem(m + dy, ny))

    partner = device(dc=1)
    peers_x = [device(dx=k) for k in range(1, nx)]
    peers_z = [device(dz=k) for k in range(1, nz)]
    peers_y = [device(dy=k) for k in range(1, ny)]
    everyone = [partner] + peers_x + peers_z + peers_y

    barrier = pltpu.get_barrier_semaphore()
    for peer in everyone:
        pl.semaphore_signal(barrier, inc=1, device_id=peer, device_id_type=MESH)

    started = []

    def send(src, dst, peer):
        at = len(started)
        copy = pltpu.make_async_remote_copy(
            src_ref=src,
            dst_ref=dst,
            send_sem=send_sems.at[at],
            recv_sem=recv_sems.at[at],
            device_id=peer,
            device_id_type=MESH,
        )
        copy.start()
        started.append(copy)
        return copy

    def arrive(copies):
        for copy in copies:
            copy.wait_recv()

    def spread_to(buf, mine, peers):
        return [send(buf.at[mine], buf.at[mine], peer) for peer in peers]

    def column_sum(fn):
        step = 64
        def body(i, acc):
            return acc + jnp.sum(fn(pl.ds(i * step, step)), axis=0, keepdims=True)
        return lax.fori_loop(0, frames // step, body, jnp.zeros((1, width), f32))

    for view, ref in enumerate((a_ref, b_ref)):
        center = column_sum(lambda rows: ref[rows, :].astype(f32)) / frames
        def deviation(rows, ref=ref, center=center):
            dev = ref[rows, :].astype(f32) - center
            return dev * dev
        stat_c[c, 0, view : view + 1, :] = center
        stat_c[c, 1, view : view + 1, :] = column_sum(deviation)

    pl.semaphore_wait(barrier, len(everyone))

    def merge(buf, members, count):
        center = sum(buf[i, 0] for i in range(members)) * (1.0 / members)
        spread = sum(buf[i, 1] for i in range(members))
        shift = sum((buf[i, 0] - center) ** 2 for i in range(members))
        return center, spread + count * shift

    arrive(spread_to(stat_c, c, [partner]))
    stat_x[x, 0], stat_x[x, 1] = merge(stat_c, 2, float(frames))
    arrive(spread_to(stat_x, x, peers_x))
    stat_z[z, 0], stat_z[z, 1] = merge(stat_x, nx, float(frames * 2))
    arrive(spread_to(stat_z, z, peers_z))
    center, spread = merge(stat_z, nz, float(frames * 2 * nx))
    inv = lax.rsqrt(spread / total + epsilon)
    center_a, center_b = center[0:1], center[1:2]
    inv_a, inv_b = inv[0:1], inv[1:2]

    own, other = pl.ds(0, frames), pl.ds(frames, frames)
    own_half = pl.ds(pl.multiple_of(c * half, 128), half)
    other_half = pl.ds(pl.multiple_of((1 - c) * half, 128), half)

    def standardize(src, dst, center, inv):
        def body(i, _):
            rows = pl.ds(pl.multiple_of(i * 32, 32), 32)
            dst[rows, :] = ((src[rows, :].astype(f32) - center) * inv).astype(bf16)
            return 0
        lax.fori_loop(0, frames // 32, body, 0)

    standardize(b_ref, nb16, center_b, inv_b)
    swap_b = send(nb16.at[:, other_half], nb.at[0, other], partner)
    nb[0, own, :] = nb16[:, own_half]
    up, down = device(dy=1), device(dy=ny - 1)
    first = [send(nb.at[0, own], nb.at[2, own], up)]
    standardize(a_ref, na, center_a, inv_a)
    swap_a = send(na.at[own], na.at[other], partner)
    swap_b.wait_recv()
    first.append(send(nb.at[0, other], nb.at[1, other], down))

    def diagonal():
        def body(i, acc):
            rows = pl.ds(pl.multiple_of(i * 32, 32), 32)
            wide_a = (a_ref[rows, :].astype(f32) - center_a) * inv_a
            wide_b = (b_ref[rows, :].astype(f32) - center_b) * inv_b
            short_a, short_b = na[rows, :].astype(f32), nb16[rows, :].astype(f32)
            terms = (short_a, short_b, short_a * short_b, wide_a * short_b, wide_b * short_a)
            return tuple(s + jnp.sum(t, axis=0, keepdims=True) for s, t in zip(acc, terms))
        sums = lax.fori_loop(0, frames // 32, body, (jnp.zeros((1, width), f32),) * 5)
        for at, value in enumerate(sums[:3] + (jnp.zeros((1, width), f32),) + sums[3:]):
            diag_c[c, at // 2, at % 2 : at % 2 + 1, :] = value
        copies = spread_to(diag_c, c, [partner])
        yield
        arrive(copies)
        diag_x[x] = jnp.where(
            c == 0, diag_c[0, :, :, :half] + diag_c[1, :, :, :half],
            diag_c[0, :, :, half:] + diag_c[1, :, :, half:])
        copies = spread_to(diag_x, x, peers_x)
        yield
        arrive(copies)
        diag_z[z] = sum(diag_x[i] for i in range(nx))
        copies = spread_to(diag_z, z, peers_z)
        yield
        arrive(copies)
        diag_f[c] = sum(diag_z[i] for i in range(nz)) / total
        mean_b16[0] = diag_f[c, 0, 1:2]
        copies = spread_to(diag_f, c, [partner])
        copies += [send(mean_b16.at[0], mean_b16.at[SLOT[ny - k]], peers_y[k - 1]) for k in range(1, ny)]
        yield
        arrive(copies)
        mean_a = jnp.concatenate([diag_f[0, 0, 0:1], diag_f[1, 0, 0:1]], axis=1)
        na[pl.ds(both, 16), :] = jnp.broadcast_to(mean_a, (16, width)).astype(bf16)
        for p in range(slots):
            nb[p, pl.ds(both, 16), :] = jnp.broadcast_to(mean_b16[p], (16, half)).astype(bf16)

    def correlate(p):
        def body(i, _):
            rows = pl.ds(pl.multiple_of(i * 256, 256), 256)
            part[p, rows, :] = jnp.dot(nat[rows, :], nb[p, :both, :], preferred_element_type=f32)
            return 0
        lax.fori_loop(0, width // 256, body, 0)

    def sweep(group, rows, fn):
        first, count, _, columns = group
        step = min(rows, 32)
        turns = count * (rows // step)
        per = min(turns, max(1, 16384 // (step * columns)))
        def body(i, _):
            stores = []
            for u in range(per):
                k = i * per + u
                p = first + k // (rows // step)
                r = k % (rows // step) * step if isinstance(k, int) else lax.rem(k, rows // step) * step
                stores += fn(p, r, step)
            for ref, at, value in stores:
                ref[at] = value
            return 0
        if turns == per:
            body(0, 0)
        else:
            lax.fori_loop(0, turns // per, body, 0)

    def strip(base, step):
        return pl.ds(base if isinstance(base, int) else pl.multiple_of(base, 16), step)

    def reduce_chain(group, base, rows, n, at, plus, minus, off, bufs):
        out_p1, out_m1, out_p2, out_m2, in_p1, in_m1, in_p2, in_m2 = bufs
        far = n // 2
        first, count, column, columns = group
        some, window, every = pl.ds(first, count), pl.ds(off, rows), pl.ds(column, columns)
        left, right = pl.ds(column, columns // 2), pl.ds(column + columns // 2, columns // 2)
        short = pl.ds(column // 2, columns // 2)

        def pack(s, source, cols, out1, out2, in1, in2):
            rest = right if cols is left else left
            def fn(p, r, step):
                there = strip(source + r, step)
                here = strip(off + r, step)
                if s == 1:
                    return [(out1, (p, here, short), encode(part[p, there, cols]))]
                if s > 2:
                    value = encode(part[p, there, every] + decode(in2[s - 3, p, here, every]))
                    return [(out2, (s - 2, p, here, every), value)]
                value = encode(part[p, there, cols] + decode(in1[p, here, short]))
                return [
                    (out2, (0, p, here, cols), value),
                    (out2, (0, p, here, rest), encode(part[p, there, rest])),
                ]
            return fn

        for s in range(1, far + 1):
            distance = far + 1 - s
            go_p = pack(s, base + lax.rem(at + distance, n) * rows, left, out_p1, out_p2, in_p1, in_p2)
            go_m = pack(s, base + lax.rem(at + n - distance, n) * rows, right, out_m1, out_m2, in_m1, in_m2)
            sweep(group, rows, lambda p, r, step: go_p(p, r, step) + go_m(p, r, step))
            def view(ref1, ref2):
                return ref1.at[some, window, short] if s == 1 else ref2.at[s - 2, some, window, every]
            go = [
                send(view(out_p1, out_p2), view(in_p1, in_p2), plus),
                send(view(out_m1, out_m2), view(in_m1, in_m2), minus),
            ]
            yield
            arrive(go)

        def finish(p, r, step):
            there = strip(base + at * rows + r, step)
            here = strip(off + r, step)
            value = part[p, there, every] + decode(in_p2[far - 2, p, here, every])
            return [(part, (p, there, every), value + decode(in_m2[far - 2, p, here, every]))]
        sweep(group, rows, finish)

    def gather_chain(group, base, rows, n, at, plus, minus):
        far = n // 2
        first, count, column, columns = group
        some, every = pl.ds(first, count), pl.ds(column, columns)
        left, right = pl.ds(column, columns // 2), pl.ds(column + columns // 2, columns // 2)
        for s in range(1, far + 1):
            cols_p, cols_m = (left, right) if s == far else (every, every)
            from_p = base + lax.rem(at + n - (s - 1), n) * rows
            from_m = base + lax.rem(at + (s - 1), n) * rows
            ref_p = slope.at[some, strip(from_p, rows), cols_p]
            ref_m = slope.at[some, strip(from_m, rows), cols_m]
            go = [send(ref_p, ref_p, plus), send(ref_m, ref_m, minus)]
            yield
            arrive(go)

    plus_x, minus_x = device(dx=1), device(dx=nx - 1)
    plus_z, minus_z = device(dz=1), device(dz=nz - 1)
    top = width // 2
    rows_x, rows_z, rows_o = top // nx, top // nz, top // (nx * nz)
    base_x = x * rows_x
    base_z = top + z * rows_z
    bufs_x = (sx_p1, sx_m1, sx_p2, sx_m2, rx_p1, rx_m1, rx_p2, rx_m2)
    bufs_z = (sz_p1, sz_m1, sz_p2, sz_m2, rz_p1, rz_m1, rz_p2, rz_m2)

    def slopes(group, base):
        first, count, column, columns = group
        rows, cols = strip(base, rows_o), pl.ds(column, columns)
        row_ids = lax.broadcasted_iota(jnp.int32, (rows_o, columns), 0) + base
        col_ids = lax.broadcasted_iota(jnp.int32, (rows_o, columns), 1) + (c * half + column)
        for p in range(first, first + count):
            value = 2.0 * off_weight * (part[p, rows, cols] / total)
            if p == 0:
                value = jnp.where(row_ids == col_ids, 0.0, value)
            slope[p, rows, cols] = value.astype(bf16)

    def one_way(group):
        yield from reduce_chain(group, 0, rows_x, nx, x, plus_x, minus_x, 0, bufs_x)
        yield from reduce_chain(group, base_x, rows_o, nz, z, plus_z, minus_z, rows_z, bufs_z)
        slopes(group, base_x + z * rows_o)
        yield from gather_chain(group, base_x, rows_o, nz, z, plus_z, minus_z)
        yield from gather_chain(group, 0, rows_x, nx, x, plus_x, minus_x)

    def other_way(group):
        yield from reduce_chain(group, top, rows_z, nz, z, plus_z, minus_z, 0, bufs_z)
        yield from reduce_chain(group, base_z, rows_o, nx, x, plus_x, minus_x, rows_x, bufs_x)
        slopes(group, base_z + x * rows_o)
        yield from gather_chain(group, base_z, rows_o, nx, x, plus_x, minus_x)
        yield from gather_chain(group, top, rows_z, nz, z, plus_z, minus_z)

    def step_all(live):
        for chain in list(live):
            if next(chain, live) is live:
                live.remove(chain)

    def to_b(group):
        first, count, column, columns = group
        for p in range(first, first + count):
            def body(i, _, p=p):
                cols = pl.ds(pl.multiple_of(column + i * 256, 256), 256)
                part_b[p, :, cols] = jnp.dot(na[...], slope[p, :, cols], preferred_element_type=f32)
                return 0
            if columns == 256:
                cols = pl.ds(column, 256)
                part_b[p, :, cols] = jnp.dot(na[...], slope[p, :, cols], preferred_element_type=f32)
            else:
                lax.fori_loop(0, columns // 256, body, 0)

    begun = []

    def to_a(group):
        first, count, column, columns = group
        cols = pl.ds(column, columns)
        fresh = not begun
        begun.append(group)
        def body(i, _):
            rows = pl.ds(pl.multiple_of(i * 256, 256), 256)
            acc = None if fresh else back_a[:, rows]
            for p in range(first, first + count):
                term = lax.dot_general(
                    nb[p, :, cols], slope[p, rows, cols], (((1,), (1,)), ((), ())),
                    preferred_element_type=f32)
                acc = term if acc is None else acc + term
            back_a[:, rows] = acc
            return 0
        lax.fori_loop(0, width // 256, body, 0)

    def squares(group):
        first, count, column, columns = group
        cols = pl.ds(column, columns)
        for p in range(first, first + count):
            def body(i, acc, p=p):
                rows = pl.ds(pl.multiple_of(i * 32, 32), 32)
                s = slope[p, rows, cols].astype(f32)
                s = s * s
                row_acc[rows, :] += sum(s[:, k * 128 : (k + 1) * 128] for k in range(columns // 128))
                return acc + jnp.sum(s, axis=0, keepdims=True)
            square[p, :, cols] = lax.fori_loop(0, width // 32, body, jnp.zeros((1, columns), f32))

    def whole(group):
        live = [one_way(group), other_way(group)]
        while live:
            step_all(live)
            if live:
                yield

    far_y, near_y = [], []

    def group_own():
        yield from whole(GROUP_OWN)
        squares(GROUP_OWN)
        to_b(GROUP_OWN)
        to_a(GROUP_OWN)

    def group_far():
        yield from whole(GROUP_FAR)
        to_b(GROUP_FAR)
        def body(i, _):
            here = pl.ds(pl.multiple_of(i * 32, 32), 32)
            there = pl.ds(pl.multiple_of(i * 32 + frames, 32), 32)
            sy_p1[here, :] = encode(part_b[3, here, :])
            sy_m1[here, :] = encode(part_b[3, there, :])
            return 0
        lax.fori_loop(0, frames // 32, body, 0)
        far_y.extend([send(sy_p1, ry_p1, up), send(sy_m1, ry_m1, down)])
        to_a(GROUP_FAR)
        squares(GROUP_FAR)

    def group_near(group):
        yield from whole(group)
        to_b(group)
        if not near_y:
            arrive(far_y)
        cols = pl.ds(group[2], group[3])
        def body(i, _):
            here = pl.ds(pl.multiple_of(i * 32, 32), 32)
            there = pl.ds(pl.multiple_of(i * 32 + frames, 32), 32)
            plus_near = encode(part_b[1, here, cols] + decode(ry_p1[here, cols]))
            plus_rest = encode(part_b[1, there, cols])
            minus_rest = encode(part_b[2, here, cols])
            minus_near = encode(part_b[2, there, cols] + decode(ry_m1[here, cols]))
            sy_p2[here, cols] = plus_near
            sy_p2[there, cols] = plus_rest
            sy_m2[here, cols] = minus_rest
            sy_m2[there, cols] = minus_near
            return 0
        lax.fori_loop(0, frames // 32, body, 0)
        near_y.append([
            send(sy_p2.at[:, cols], ry_p2.at[:, cols], up),
            send(sy_m2.at[:, cols], ry_m2.at[:, cols], down),
        ])
        to_a(group)
        squares(group)

    GROUP_OWN, GROUP_FAR = (0, 1, 0, half), (3, 1, 0, half)
    NEAR = [(1, 2, 0, half // 2), (1, 2, half // 2, half // 2)]

    row_acc[...] = jnp.zeros_like(row_acc)
    diag_chain = diagonal()
    swap_a.wait_recv()
    for i in range(width // 128):
        cols = pl.ds(i * 128, 128)
        nat[cols, :] = jnp.transpose(na[:both, cols].astype(f32)).astype(bf16)
    correlate(0)
    live = [group_own()]
    step_all(live)
    next(diag_chain)
    arrive(first)
    second = [
        send(nb.at[2, own], nb.at[3, own], up),
        send(nb.at[1, other], nb.at[3, other], down),
    ]
    third = [
        send(nb.at[0, other], nb.at[2, other], up),
        send(nb.at[0, own], nb.at[1, own], down),
    ]
    step_all(live)
    next(diag_chain)
    step_all(live)
    next(diag_chain)
    step_all(live)
    arrive(second)
    correlate(3)
    live.append(group_far())
    step_all(live)
    next(diag_chain)
    step_all(live)
    arrive(third)
    correlate(1)
    correlate(2)
    live += [group_near(group) for group in NEAR]
    step_all(live)
    next(diag_chain, None)
    while live:
        step_all(live)

    swap_back = send(back_a.at[other, :], recv_a, partner)

    scale = 1.0 / (2.0 * off_weight)
    corr_half = diag_f[c, 1, 0:1]
    loss_off = jnp.sum(sum(square[p] for p in range(slots)), axis=1, keepdims=True)
    loss_diag = jnp.sum((1.0 - corr_half) ** 2, axis=1, keepdims=True)
    loss_row = jnp.broadcast_to(loss_off * (off_weight * scale * scale) + loss_diag, (1, half))
    for p in range(slots):
        block = extra_y.at[ny + p] if p else extra_y.at[m]
        block[0:1, :] = part_b[p, both : both + 1, :]
        block[1:2, :] = square[p] * scale
        block[2:3, :] = loss_row
        block[3:4, :] = jnp.zeros((1, half), f32)
    share_y = [
        send(extra_y.at[ny + SLOT[k]], extra_y.at[m], peers_y[k - 1]) for k in range(1, ny)
    ]
    extra_a[c, 0:1, :] = back_a[both : both + 1, :]
    extra_a[c, 1:2, :] = jnp.sum(jnp.transpose(row_acc[...]), axis=0, keepdims=True) * scale
    share_a = send(extra_a.at[c], extra_a.at[c], partner)

    diag = jnp.concatenate([diag_f[0], diag_f[1]], axis=2)
    mean_a16, mean_own_b16 = diag[0, 0:1], diag[0, 1:2]
    corr_ii = diag[1, 0:1]
    cross_a, cross_b = diag[2, 0:1], diag[2, 1:2]
    slope_ii = (-2.0 * (1.0 - corr_ii)).astype(bf16).astype(f32)

    share_a.wait_recv()
    last_a = extra_a[0] + extra_a[1]
    mean_a = last_a[0:1] + mean_own_b16 * slope_ii
    inner_a = last_a[1:2] + cross_a * slope_ii
    swap_back.wait_recv()

    def finish_a(i, _):
        rows = pl.ds(pl.multiple_of(i * 32, 32), 32)
        wide = (a_ref[rows, :].astype(f32) - center_a) * inv_a
        back = back_a[rows, :] + recv_a[rows, :] + slope_ii * nb16[rows, :].astype(f32)
        ga_ref[rows, :] = (inv_a * (back - mean_a - wide * inner_a)).astype(bf16)
        return 0

    lax.fori_loop(0, frames // 32, finish_a, 0)

    arrive(share_y)
    extra_c[c] = sum(extra_y[i] for i in range(ny))
    share_c = send(extra_c.at[c], extra_c.at[c], partner)

    def add_last(base, cols):
        def body(i, _):
            rows = pl.ds(pl.multiple_of(base + i * 64, 64), 64)
            sum_b[rows, cols] = (
                part_b[0, rows, cols] + decode(ry_p2[rows, cols]) + decode(ry_m2[rows, cols])
            )
            return 0
        lax.fori_loop(0, frames // 64, body, 0)

    swap_sum = []
    for group, copies in zip(NEAR, near_y):
        arrive(copies)
        cols = pl.ds(group[2], group[3])
        there = pl.ds(pl.multiple_of(c * half + group[2], 128), group[3])
        add_last(frames, cols)
        swap_sum.append(send(sum_b.at[other, cols], full_b.at[:, there], partner))
        add_last(0, cols)
        full_b[:, there] = sum_b[own, cols]

    share_c.wait_recv()
    mean_b = jnp.concatenate([extra_c[0, 0:1], extra_c[1, 0:1]], axis=1) + mean_a16 * slope_ii
    inner_b = jnp.concatenate([extra_c[0, 1:2], extra_c[1, 1:2]], axis=1) + cross_b * slope_ii
    loss_ref[...] = jnp.broadcast_to(extra_c[0, 2:3, :128] + extra_c[1, 2:3, :128], (8, 128))
    arrive(swap_sum)

    def finish_b(i, _):
        rows = pl.ds(pl.multiple_of(i * 32, 32), 32)
        wide = (b_ref[rows, :].astype(f32) - center_b) * inv_b
        back = full_b[rows, :] + slope_ii * na[rows, :].astype(f32)
        gb_ref[rows, :] = (inv_b * (back - mean_b - wide * inner_b)).astype(bf16)
        return 0

    lax.fori_loop(0, frames // 32, finish_b, 0)
    for copy in started:
        copy.wait_send()


def solution(mesh):
    ny = mesh.shape["mp"]
    members = mesh.shape["dp"]
    nx = ny
    nz = members // (2 * nx)

    def per_device(view_a, view_b):
        frames, width = view_a.shape
        both, half = 2 * frames, width // 2
        quarter = half // 2
        top = width // 2
        rows_x, rows_z, rows_o = top // nx, top // nz, top // (nx * nz)
        vmem = pltpu.VMEM
        rings = []
        scratch = [
            vmem((frames, width), bf16),
            vmem((both + 16, width), bf16),
            vmem((width, both), bf16),
            vmem((ny, both + 16, half), bf16),
            vmem((ny, width, half), f32),
            vmem((ny, width, half), bf16),
            vmem((both + 16, width), f32),
            vmem((ny, both + 16, half), f32),
            vmem((both, half), f32),
            vmem((frames, width), f32),
            vmem((2, 2, 2, width), f32),
            vmem((nx, 2, 2, width), f32),
            vmem((nz, 2, 2, width), f32),
            vmem((2, 3, 2, width), f32),
            vmem((nx, 3, 2, half), f32),
            vmem((nz, 3, 2, half), f32),
            vmem((2, 3, 2, half), f32),
            vmem((ny, 1, half), f32),
            vmem((ny, 1, half), f32),
            vmem((2 * ny, 4, half), f32),
            vmem((2, 4, half), f32),
            vmem((2, 2, width), f32),
            vmem((width, 128), f32),
        ]
        for rows, n in ((rows_x + rows_o, nx), (rows_z + rows_o, nz)):
            ring = [vmem((ny, rows, quarter), bf16)] * 2 + [vmem((n // 2 - 1, ny, rows, half), bf16)] * 2
            rings.append(ring)
        ring_y = [vmem((frames, half), bf16)] * 2 + [vmem((both, half), bf16)] * 2
        scratch += rings[0] + rings[1] + rings[0] + rings[1] + ring_y + ring_y + [
            vmem((frames, width), f32),
            pltpu.SemaphoreType.DMA((256,)),
            pltpu.SemaphoreType.DMA((256,)),
        ]
        grad_a, grad_b, loss = pl.pallas_call(
            functools.partial(kernel, nx, nz, ny, float(frames * members)),
            out_shape=(
                jax.ShapeDtypeStruct((frames, width), bf16),
                jax.ShapeDtypeStruct((frames, width), bf16),
                jax.ShapeDtypeStruct((8, 128), f32),
            ),
            in_specs=[pl.BlockSpec(memory_space=vmem)] * 2,
            out_specs=[pl.BlockSpec(memory_space=vmem)] * 3,
            scratch_shapes=scratch,
            compiler_params=pltpu.CompilerParams(
                collective_id=0, has_side_effects=True, vmem_limit_bytes=56 * 1024 * 1024
            ),
            cost_estimate=pl.CostEstimate(
                flops=3 * 2 * both * width * half * ny, bytes_accessed=4 * frames * width * 2,
                transcendentals=0),
        )(view_a, view_b)
        return grad_a, grad_b, loss[0, 0]

    placed = P("dp", "mp")
    return jax.shard_map(
        per_device,
        mesh=mesh,
        in_specs=(placed, placed),
        out_specs=(placed, placed, P()),
        check_vma=False,
    )
```

```python
import functools

import jax
import jax.numpy as jnp
from jax import lax
from jax.experimental import pallas as pl
from jax.experimental.pallas import tpu as pltpu
from jax.sharding import PartitionSpec as P

epsilon = 1e-05
off_weight = 0.0051

MESH = pl.DeviceIdType.MESH
f32 = jnp.float32
bf16 = jnp.bfloat16

SHIFT = (0, 1, 3, 2)
SLOT = (0, 1, 3, 2)


tiny = 1e-37


def encode(v):
    q = v * v
    q = q * q
    return jnp.where(v < 0.0, -q, q).astype(bf16)


def decode(y):
    y = y.astype(f32)
    q = jnp.abs(y)
    q = q * lax.rsqrt(jnp.maximum(q, tiny))
    q = q * lax.rsqrt(jnp.maximum(q, tiny))
    return jnp.where(y < 0.0, -q, q)


def kernel(
    nx, nz, ny, total,
    a_ref, b_ref, ga_ref, gb_ref, loss_ref,
    nb16, na, nat, nb, part, slope, back_a, part_b, sum_b, full_b,
    stat_c, stat_x, stat_z, diag_c, diag_x, diag_z, diag_f,
    mean_b16, square, extra_y, extra_c, extra_a, row_acc,
    rx_p1, rx_m1, rx_p2, rx_m2, rz_p1, rz_m1, rz_p2, rz_m2,
    sx_p1, sx_m1, sx_p2, sx_m2, sz_p1, sz_m1, sz_p2, sz_m2,
    ry_p1, ry_m1, ry_p2, ry_m2, sy_p1, sy_m1, sy_p2, sy_m2, recv_a,
    send_sems, recv_sems,
):
    frames, width = a_ref.shape
    both = 2 * frames
    half = width // 2
    slots = ny
    dp = lax.axis_index("dp")
    m = lax.axis_index("mp")
    c = lax.rem(dp, 2)
    x = lax.rem(dp // 2, nx)
    z = dp // (2 * nx)

    def device(dc=0, dx=0, dz=0, dy=0):
        there = (lax.rem(z + dz, nz) * nx + lax.rem(x + dx, nx)) * 2
        there = there + (1 - c if dc else c)
        return (there, lax.rem(m + dy, ny))

    partner = device(dc=1)
    peers_x = [device(dx=k) for k in range(1, nx)]
    peers_z = [device(dz=k) for k in range(1, nz)]
    peers_y = [device(dy=k) for k in range(1, ny)]
    everyone = [partner] + peers_x + peers_z + peers_y

    barrier = pltpu.get_barrier_semaphore()
    for peer in everyone:
        pl.semaphore_signal(barrier, inc=1, device_id=peer, device_id_type=MESH)

    started, due, clock, free = [], {}, [0.0], {}

    def work(t):
        clock[0] += t

    def send(src, dst, peer, link=None):
        at = len(started)
        work(0.2)
        size = src.dtype.itemsize
        for d in src.shape:
            size *= d
        rate = 45e3 if link else 500e3
        begin = max(clock[0], free.get(link, 0.0)) if link else clock[0]
        end = begin + size / rate
        if link:
            free[link] = end
        copy = pltpu.make_async_remote_copy(
            src_ref=src,
            dst_ref=dst,
            send_sem=send_sems.at[at],
            recv_sem=recv_sems.at[at],
            device_id=peer,
            device_id_type=MESH,
        )
        copy.start()
        started.append(copy)
        due[id(copy)] = end + 1.5
        return copy

    def arrive(copies):
        for copy in copies:
            clock[0] = max(clock[0], due[id(copy)])
            copy.wait_recv()

    def spread_to(buf, mine, peers):
        return [send(buf.at[mine], buf.at[mine], peer) for peer in peers]

    def column_sum(fn):
        step = 64
        def body(i, acc):
            return acc + jnp.sum(fn(pl.ds(i * step, step)), axis=0, keepdims=True)
        return lax.fori_loop(0, frames // step, body, jnp.zeros((1, width), f32))

    for view, ref in enumerate((a_ref, b_ref)):
        center = column_sum(lambda rows: ref[rows, :].astype(f32)) / frames
        def deviation(rows, ref=ref, center=center):
            dev = ref[rows, :].astype(f32) - center
            return dev * dev
        stat_c[c, 0, view : view + 1, :] = center
        stat_c[c, 1, view : view + 1, :] = column_sum(deviation)

    pl.semaphore_wait(barrier, len(everyone))

    def merge(buf, members, count):
        center = sum(buf[i, 0] for i in range(members)) * (1.0 / members)
        spread = sum(buf[i, 1] for i in range(members))
        shift = sum((buf[i, 0] - center) ** 2 for i in range(members))
        return center, spread + count * shift

    arrive(spread_to(stat_c, c, [partner]))
    stat_x[x, 0], stat_x[x, 1] = merge(stat_c, 2, float(frames))
    arrive(spread_to(stat_x, x, peers_x))
    stat_z[z, 0], stat_z[z, 1] = merge(stat_x, nx, float(frames * 2))
    arrive(spread_to(stat_z, z, peers_z))
    center, spread = merge(stat_z, nz, float(frames * 2 * nx))
    inv = lax.rsqrt(spread / total + epsilon)
    center_a, center_b = center[0:1], center[1:2]
    inv_a, inv_b = inv[0:1], inv[1:2]

    own, other = pl.ds(0, frames), pl.ds(frames, frames)
    own_half = pl.ds(pl.multiple_of(c * half, 128), half)
    other_half = pl.ds(pl.multiple_of((1 - c) * half, 128), half)

    def standardize(src, dst, center, inv):
        def body(i, _):
            rows = pl.ds(pl.multiple_of(i * 32, 32), 32)
            dst[rows, :] = ((src[rows, :].astype(f32) - center) * inv).astype(bf16)
            return 0
        lax.fori_loop(0, frames // 32, body, 0)

    standardize(b_ref, nb16, center_b, inv_b)
    swap_b = send(nb16.at[:, other_half], nb.at[0, other], partner)
    nb[0, own, :] = nb16[:, own_half]
    up, down = device(dy=1), device(dy=ny - 1)
    first = [send(nb.at[0, own], nb.at[2, own], up, "y+")]
    standardize(a_ref, na, center_a, inv_a)
    swap_a = send(na.at[own], na.at[other], partner)
    arrive([swap_b])
    first.append(send(nb.at[0, other], nb.at[1, other], down, "y-"))

    diag_done = []

    def diagonal():
        def body(i, acc):
            rows = pl.ds(pl.multiple_of(i * 32, 32), 32)
            wide_a = (a_ref[rows, :].astype(f32) - center_a) * inv_a
            wide_b = (b_ref[rows, :].astype(f32) - center_b) * inv_b
            short_a, short_b = na[rows, :].astype(f32), nb16[rows, :].astype(f32)
            terms = (short_a, short_b, short_a * short_b, wide_a * short_b, wide_b * short_a)
            return tuple(s + jnp.sum(t, axis=0, keepdims=True) for s, t in zip(acc, terms))
        sums = lax.fori_loop(0, frames // 32, body, (jnp.zeros((1, width), f32),) * 5)
        for at, value in enumerate(sums[:3] + (jnp.zeros((1, width), f32),) + sums[3:]):
            diag_c[c, at // 2, at % 2 : at % 2 + 1, :] = value
        work(1.5)
        copies = spread_to(diag_c, c, [partner])
        yield copies
        diag_x[x] = jnp.where(
            c == 0, diag_c[0, :, :, :half] + diag_c[1, :, :, :half],
            diag_c[0, :, :, half:] + diag_c[1, :, :, half:])
        copies = spread_to(diag_x, x, peers_x)
        yield copies
        diag_z[z] = sum(diag_x[i] for i in range(nx))
        copies = spread_to(diag_z, z, peers_z)
        yield copies
        diag_f[c] = sum(diag_z[i] for i in range(nz)) / total
        mean_b16[0] = diag_f[c, 0, 1:2]
        copies = spread_to(diag_f, c, [partner])
        copies += [send(mean_b16.at[0], mean_b16.at[SLOT[ny - k]], peers_y[k - 1]) for k in range(1, ny)]
        yield copies
        mean_a = jnp.concatenate([diag_f[0, 0, 0:1], diag_f[1, 0, 0:1]], axis=1)
        na[pl.ds(both, 16), :] = jnp.broadcast_to(mean_a, (16, width)).astype(bf16)
        for p in range(slots):
            nb[p, pl.ds(both, 16), :] = jnp.broadcast_to(mean_b16[p], (16, half)).astype(bf16)
        diag_done.append(True)

    def correlate(p):
        work(1.5)
        def body(i, _):
            rows = pl.ds(pl.multiple_of(i * 256, 256), 256)
            part[p, rows, :] = jnp.dot(nat[rows, :], nb[p, :both, :], preferred_element_type=f32)
            return 0
        lax.fori_loop(0, width // 256, body, 0)

    def sweep(group, rows, fn):
        first, count, _, columns = group
        work(0.004 * rows * count * columns / 1024)
        step = min(rows, 32)
        turns = count * (rows // step)
        per = min(turns, max(1, 16384 // (step * columns)))
        def body(i, _):
            stores = []
            for u in range(per):
                k = i * per + u
                p = first + k // (rows // step)
                r = k % (rows // step) * step if isinstance(k, int) else lax.rem(k, rows // step) * step
                stores += fn(p, r, step)
            for ref, at, value in stores:
                ref[at] = value
            return 0
        if turns == per:
            body(0, 0)
        else:
            lax.fori_loop(0, turns // per, body, 0)

    def strip(base, step):
        return pl.ds(base if isinstance(base, int) else pl.multiple_of(base, 16), step)

    def reduce_chain(group, base, rows, n, at, plus, minus, axis, off, bufs):
        out_p1, out_m1, out_p2, out_m2, in_p1, in_m1, in_p2, in_m2 = bufs
        far = n // 2
        first, count, column, columns = group
        some, window, every = pl.ds(first, count), pl.ds(off, rows), pl.ds(column, columns)
        left, right = pl.ds(column, columns // 2), pl.ds(column + columns // 2, columns // 2)
        short = pl.ds(column // 2, columns // 2)

        def pack(s, source, cols, out1, out2, in1, in2):
            rest = right if cols is left else left
            def fn(p, r, step):
                there = strip(source + r, step)
                here = strip(off + r, step)
                if s == 1:
                    return [(out1, (p, here, short), encode(part[p, there, cols]))]
                if s > 2:
                    value = encode(part[p, there, every] + decode(in2[s - 3, p, here, every]))
                    return [(out2, (s - 2, p, here, every), value)]
                value = encode(part[p, there, cols] + decode(in1[p, here, short]))
                return [
                    (out2, (0, p, here, cols), value),
                    (out2, (0, p, here, rest), encode(part[p, there, rest])),
                ]
            return fn

        for s in range(1, far + 1):
            distance = far + 1 - s
            go_p = pack(s, base + lax.rem(at + distance, n) * rows, left, out_p1, out_p2, in_p1, in_p2)
            go_m = pack(s, base + lax.rem(at + n - distance, n) * rows, right, out_m1, out_m2, in_m1, in_m2)
            sweep(group, rows, lambda p, r, step: go_p(p, r, step) + go_m(p, r, step))
            def view(ref1, ref2):
                return ref1.at[some, window, short] if s == 1 else ref2.at[s - 2, some, window, every]
            go = [
                send(view(out_p1, out_p2), view(in_p1, in_p2), plus, axis + "+"),
                send(view(out_m1, out_m2), view(in_m1, in_m2), minus, axis + "-"),
            ]
            yield go

        def finish(p, r, step):
            there = strip(base + at * rows + r, step)
            here = strip(off + r, step)
            value = part[p, there, every] + decode(in_p2[far - 2, p, here, every])
            return [(part, (p, there, every), value + decode(in_m2[far - 2, p, here, every]))]
        sweep(group, rows, finish)

    def gather_chain(group, base, rows, n, at, plus, minus, axis):
        far = n // 2
        first, count, column, columns = group
        some, every = pl.ds(first, count), pl.ds(column, columns)
        left, right = pl.ds(column, columns // 2), pl.ds(column + columns // 2, columns // 2)
        for s in range(1, far + 1):
            cols_p, cols_m = (left, right) if s == far else (every, every)
            from_p = base + lax.rem(at + n - (s - 1), n) * rows
            from_m = base + lax.rem(at + (s - 1), n) * rows
            ref_p = slope.at[some, strip(from_p, rows), cols_p]
            ref_m = slope.at[some, strip(from_m, rows), cols_m]
            yield [send(ref_p, ref_p, plus, axis + "+"), send(ref_m, ref_m, minus, axis + "-")]

    plus_x, minus_x = device(dx=1), device(dx=nx - 1)
    plus_z, minus_z = device(dz=1), device(dz=nz - 1)
    rows_x, rows_z, rows_o = width // nx, width // nz, width // (nx * nz)
    base_x = x * rows_x
    base_z = z * rows_z
    bufs_x = (sx_p1, sx_m1, sx_p2, sx_m2, rx_p1, rx_m1, rx_p2, rx_m2)
    bufs_z = (sz_p1, sz_m1, sz_p2, sz_m2, rz_p1, rz_m1, rz_p2, rz_m2)

    def slopes(group, base):
        first, count, column, columns = group
        rows, cols = strip(base, rows_o), pl.ds(column, columns)
        row_ids = lax.broadcasted_iota(jnp.int32, (rows_o, columns), 0) + base
        col_ids = lax.broadcasted_iota(jnp.int32, (rows_o, columns), 1) + (c * half + column)
        for p in range(first, first + count):
            value = 2.0 * off_weight * (part[p, rows, cols] / total)
            if p == 0:
                value = jnp.where(row_ids == col_ids, 0.0, value)
            slope[p, rows, cols] = value.astype(bf16)

    def one_way(group):
        yield from reduce_chain(group, 0, rows_x, nx, x, plus_x, minus_x, "x", 0, bufs_x)
        yield from reduce_chain(group, base_x, rows_o, nz, z, plus_z, minus_z, "z", rows_z, bufs_z)
        slopes(group, base_x + z * rows_o)
        yield from gather_chain(group, base_x, rows_o, nz, z, plus_z, minus_z, "z")
        yield from gather_chain(group, 0, rows_x, nx, x, plus_x, minus_x, "x")

    def other_way(group):
        yield from reduce_chain(group, 0, rows_z, nz, z, plus_z, minus_z, "z", 0, bufs_z)
        yield from reduce_chain(group, base_z, rows_o, nx, x, plus_x, minus_x, "x", rows_x, bufs_x)
        slopes(group, base_z + x * rows_o)
        yield from gather_chain(group, base_z, rows_o, nx, x, plus_x, minus_x, "x")
        yield from gather_chain(group, 0, rows_z, nz, z, plus_z, minus_z, "z")

    live = []

    def spawn(rank, task):
        live.append([rank, len(started), task, []])

    def run():
        while live:
            best = None
            for entry in live:
                rank, _, _, wait = entry
                if callable(wait):
                    if not wait():
                        continue
                    ready = clock[0]
                else:
                    ready = max([clock[0]] + [due[id(copy)] for copy in wait])
                key = (max(ready, clock[0] + 0.2), rank)
                if best is None or key < best[0]:
                    best = (key, entry)
            entry = best[1]
            if not callable(entry[3]):
                arrive(entry[3])
            entry[3] = next(entry[2], None)
            if entry[3] is None:
                live.remove(entry)

    def group(rank, way, what, post):
        def chain():
            yield from way(what)
            yield lambda: diag_done
            yield from post
        spawn(rank, chain())

    def to_b(group):
        first, count, column, columns = group
        work(1.5 * count * columns / half)
        for p in range(first, first + count):
            def body(i, _, p=p):
                cols = pl.ds(pl.multiple_of(column + i * 256, 256), 256)
                part_b[p, :, cols] = jnp.dot(na[...], slope[p, :, cols], preferred_element_type=f32)
                return 0
            if columns == 256:
                cols = pl.ds(column, 256)
                part_b[p, :, cols] = jnp.dot(na[...], slope[p, :, cols], preferred_element_type=f32)
            else:
                lax.fori_loop(0, columns // 256, body, 0)

    begun = []

    def to_a(group):
        first, count, column, columns = group
        cols = pl.ds(column, columns)
        fresh = not begun
        work(0.5 + 1.5 * count * columns / half)
        begun.append(group)
        def body(i, _):
            rows = pl.ds(pl.multiple_of(i * 256, 256), 256)
            acc = None if fresh else back_a[:, rows]
            for p in range(first, first + count):
                term = lax.dot_general(
                    nb[p, :, cols], slope[p, rows, cols], (((1,), (1,)), ((), ())),
                    preferred_element_type=f32)
                acc = term if acc is None else acc + term
            back_a[:, rows] = acc
            return 0
        lax.fori_loop(0, width // 256, body, 0)

    def squares(group):
        first, count, column, columns = group
        work(0.6 * count * columns / half)
        cols = pl.ds(column, columns)
        for p in range(first, first + count):
            def body(i, acc, p=p):
                rows = pl.ds(pl.multiple_of(i * 32, 32), 32)
                s = slope[p, rows, cols].astype(f32)
                s = s * s
                row_acc[rows, :] += sum(s[:, k * 128 : (k + 1) * 128] for k in range(columns // 128))
                return acc + jnp.sum(s, axis=0, keepdims=True)
            square[p, :, cols] = lax.fori_loop(0, width // 32, body, jnp.zeros((1, columns), f32))

    far_ready, near_y = [], []

    def wait_far(copies):
        yield copies
        far_ready.append(True)

    def post_own():
        to_b(OWN)
        to_a(OWN)
        squares(OWN)
        yield []

    def post_far():
        to_b(FAR)
        work(1.0)
        def body(i, _):
            here = pl.ds(pl.multiple_of(i * 32, 32), 32)
            there = pl.ds(pl.multiple_of(i * 32 + frames, 32), 32)
            plus, minus = encode(part_b[3, here, :]), encode(part_b[3, there, :])
            sy_p1[here, :] = plus
            sy_m1[here, :] = minus
            return 0
        lax.fori_loop(0, frames // 32, body, 0)
        spawn(0, wait_far([send(sy_p1, ry_p1, up, "y+"), send(sy_m1, ry_m1, down, "y-")]))
        yield []
        to_a(FAR)
        squares(FAR)

    def post_near(what, out, got, into, peer, link, near, rest):
        to_b(what)
        yield lambda: far_ready
        work(1.0)
        p = what[0]
        def body(i, _):
            here = pl.ds(pl.multiple_of(i * 32, 32), 32)
            rows_n = pl.ds(pl.multiple_of(i * 32 + near, 32), 32)
            rows_r = pl.ds(pl.multiple_of(i * 32 + rest, 32), 32)
            first_half = encode(part_b[p, rows_n, :] + decode(got[here, :]))
            other_part = encode(part_b[p, rows_r, :])
            out[rows_n, :] = first_half
            out[rows_r, :] = other_part
            return 0
        lax.fori_loop(0, frames // 32, body, 0)
        near_y.append(send(out, into, peer, link))
        yield []
        to_a(what)
        squares(what)

    OWN, UP, DOWN, FAR = ((p, 1, 0, half) for p in range(slots))

    def blocks():
        yield first
        second = [
            send(nb.at[2, own], nb.at[3, own], up, "y+"),
            send(nb.at[1, other], nb.at[3, other], down, "y-"),
        ]
        third = [
            send(nb.at[0, other], nb.at[2, other], up, "y+"),
            send(nb.at[0, own], nb.at[1, own], down, "y-"),
        ]
        yield second
        correlate(3)
        group(2, one_way, FAR, post_far())
        yield third
        correlate(1)
        group(1, other_way, UP, post_near(UP, sy_p2, ry_p1, ry_p2, up, "y+", 0, frames))
        yield []
        correlate(2)
        group(1, one_way, DOWN, post_near(DOWN, sy_m2, ry_m1, ry_m2, down, "y-", frames, 0))

    row_acc[...] = jnp.zeros_like(row_acc)
    arrive([swap_a])
    for i in range(width // 128):
        cols = pl.ds(i * 128, 128)
        nat[cols, :] = jnp.transpose(na[:both, cols].astype(f32)).astype(bf16)
    work(2.0)
    correlate(0)
    spawn(0, blocks())
    group(3, one_way, OWN, post_own())
    spawn(2, diagonal())
    run()

    swap_back = send(back_a.at[other, :], recv_a, partner)

    scale = 1.0 / (2.0 * off_weight)
    corr_half = diag_f[c, 1, 0:1]
    loss_off = jnp.sum(sum(square[p] for p in range(slots)), axis=1, keepdims=True)
    loss_diag = jnp.sum((1.0 - corr_half) ** 2, axis=1, keepdims=True)
    loss_row = jnp.broadcast_to(loss_off * (off_weight * scale * scale) + loss_diag, (1, half))
    for p in range(slots):
        block = extra_y.at[ny + p] if p else extra_y.at[m]
        block[0:1, :] = part_b[p, both : both + 1, :]
        block[1:2, :] = square[p] * scale
        block[2:3, :] = loss_row
        block[3:4, :] = jnp.zeros((1, half), f32)
    share_y = [
        send(extra_y.at[ny + SLOT[k]], extra_y.at[m], peers_y[k - 1]) for k in range(1, ny)
    ]
    extra_a[c, 0:1, :] = back_a[both : both + 1, :]
    extra_a[c, 1:2, :] = jnp.sum(jnp.transpose(row_acc[...]), axis=0, keepdims=True) * scale
    share_a = send(extra_a.at[c], extra_a.at[c], partner)

    diag = jnp.concatenate([diag_f[0], diag_f[1]], axis=2)
    mean_a16, mean_own_b16 = diag[0, 0:1], diag[0, 1:2]
    corr_ii = diag[1, 0:1]
    cross_a, cross_b = diag[2, 0:1], diag[2, 1:2]
    slope_ii = (-2.0 * (1.0 - corr_ii)).astype(bf16).astype(f32)

    arrive([share_a])
    last_a = extra_a[0] + extra_a[1]
    mean_a = last_a[0:1] + mean_own_b16 * slope_ii
    inner_a = last_a[1:2] + cross_a * slope_ii
    arrive([swap_back])

    def finish_a(i, _):
        rows = pl.ds(pl.multiple_of(i * 32, 32), 32)
        wide = (a_ref[rows, :].astype(f32) - center_a) * inv_a
        back = back_a[rows, :] + recv_a[rows, :] + slope_ii * nb16[rows, :].astype(f32)
        ga_ref[rows, :] = (inv_a * (back - mean_a - wide * inner_a)).astype(bf16)
        return 0

    lax.fori_loop(0, frames // 32, finish_a, 0)

    arrive(share_y)
    extra_c[c] = sum(extra_y[i] for i in range(ny))
    share_c = send(extra_c.at[c], extra_c.at[c], partner)

    def add_last(base):
        def body(i, _):
            rows = pl.ds(pl.multiple_of(base + i * 32, 32), 32)
            sum_b[rows, :] = part_b[0, rows, :] + decode(ry_p2[rows, :]) + decode(ry_m2[rows, :])
            return 0
        lax.fori_loop(0, frames // 32, body, 0)

    arrive(near_y)
    add_last(frames)
    swap_sum = [send(sum_b.at[other, :], full_b.at[:, own_half], partner)]
    add_last(0)
    full_b[:, own_half] = sum_b[own, :]

    arrive([share_c])
    mean_b = jnp.concatenate([extra_c[0, 0:1], extra_c[1, 0:1]], axis=1) + mean_a16 * slope_ii
    inner_b = jnp.concatenate([extra_c[0, 1:2], extra_c[1, 1:2]], axis=1) + cross_b * slope_ii
    loss_ref[...] = jnp.broadcast_to(extra_c[0, 2:3, :128] + extra_c[1, 2:3, :128], (8, 128))
    arrive(swap_sum)

    def finish_b(i, _):
        rows = pl.ds(pl.multiple_of(i * 32, 32), 32)
        wide = (b_ref[rows, :].astype(f32) - center_b) * inv_b
        back = full_b[rows, :] + slope_ii * na[rows, :].astype(f32)
        gb_ref[rows, :] = (inv_b * (back - mean_b - wide * inner_b)).astype(bf16)
        return 0

    lax.fori_loop(0, frames // 32, finish_b, 0)
    for copy in started:
        copy.wait_send()


def solution(mesh):
    ny = mesh.shape["mp"]
    members = mesh.shape["dp"]
    nx = ny
    nz = members // (2 * nx)

    def per_device(view_a, view_b):
        frames, width = view_a.shape
        both, half = 2 * frames, width // 2
        quarter = half // 2
        rows_x, rows_z, rows_o = width // nx, width // nz, width // (nx * nz)
        vmem = pltpu.VMEM
        rings = []
        scratch = [
            vmem((frames, width), bf16),
            vmem((both + 16, width), bf16),
            vmem((width, both), bf16),
            vmem((ny, both + 16, half), bf16),
            vmem((ny, width, half), f32),
            vmem((ny, width, half), bf16),
            vmem((both + 16, width), f32),
            vmem((ny, both + 16, half), f32),
            vmem((both, half), f32),
            vmem((frames, width), f32),
            vmem((2, 2, 2, width), f32),
            vmem((nx, 2, 2, width), f32),
            vmem((nz, 2, 2, width), f32),
            vmem((2, 3, 2, width), f32),
            vmem((nx, 3, 2, half), f32),
            vmem((nz, 3, 2, half), f32),
            vmem((2, 3, 2, half), f32),
            vmem((ny, 1, half), f32),
            vmem((ny, 1, half), f32),
            vmem((2 * ny, 4, half), f32),
            vmem((2, 4, half), f32),
            vmem((2, 2, width), f32),
            vmem((width, 128), f32),
        ]
        for rows, n in ((rows_x + rows_o, nx), (rows_z + rows_o, nz)):
            ring = [vmem((ny, rows, quarter), bf16)] * 2 + [vmem((n // 2 - 1, ny, rows, half), bf16)] * 2
            rings.append(ring)
        ring_y = [vmem((frames, half), bf16)] * 2 + [vmem((both, half), bf16)] * 2
        scratch += rings[0] + rings[1] + rings[0] + rings[1] + ring_y + ring_y + [
            vmem((frames, width), f32),
            pltpu.SemaphoreType.DMA((160,)),
            pltpu.SemaphoreType.DMA((160,)),
        ]
        grad_a, grad_b, loss = pl.pallas_call(
            functools.partial(kernel, nx, nz, ny, float(frames * members)),
            out_shape=(
                jax.ShapeDtypeStruct((frames, width), bf16),
                jax.ShapeDtypeStruct((frames, width), bf16),
                jax.ShapeDtypeStruct((8, 128), f32),
            ),
            in_specs=[pl.BlockSpec(memory_space=vmem)] * 2,
            out_specs=[pl.BlockSpec(memory_space=vmem)] * 3,
            scratch_shapes=scratch,
            compiler_params=pltpu.CompilerParams(
                collective_id=0, has_side_effects=True, vmem_limit_bytes=56 * 1024 * 1024
            ),
            cost_estimate=pl.CostEstimate(
                flops=3 * 2 * both * width * half * ny, bytes_accessed=4 * frames * width * 2,
                transcendentals=0),
        )(view_a, view_b)
        return grad_a, grad_b, loss[0, 0]

    placed = P("dp", "mp")
    return jax.shard_map(
        per_device,
        mesh=mesh,
        in_specs=(placed, placed),
        out_specs=(placed, placed, P()),
        check_vma=False,
    )
```

```python
import functools

import jax
import jax.numpy as jnp
from jax import lax
from jax.experimental import pallas as pl
from jax.experimental.pallas import tpu as pltpu
from jax.sharding import PartitionSpec as P

epsilon = 1e-05
off_weight = 0.0051

MESH = pl.DeviceIdType.MESH
f32 = jnp.float32
bf16 = jnp.bfloat16

PIECES = ((0, 0), (0, 1), (1, 1), (2, 0), (3, 0), (3, 1), (1, 0), (2, 1))
SLOT = (0, 1, 3, 2)


tiny = 1e-37


def encode(v):
    q = v * v
    q = q * q
    return jnp.where(v < 0.0, -q, q).astype(bf16)


def decode(y):
    y = y.astype(f32)
    q = jnp.abs(y)
    q = q * lax.rsqrt(jnp.maximum(q, tiny))
    q = q * lax.rsqrt(jnp.maximum(q, tiny))
    return jnp.where(y < 0.0, -q, q)


def kernel(
    nx, nz, ny, total,
    a_ref, b_ref, ga_ref, gb_ref, loss_ref,
    nb16, na, nat, nb, part, slope, back_a, part_b, sum_b, full_b,
    stat_c, stat_x, stat_z, diag_c, diag_x, diag_z, diag_f,
    mean_b16, square, extra_y, extra_c, extra_a, row_acc,
    rx_p1, rx_m1, rx_p2, rx_m2, rz_p1, rz_m1, rz_p2, rz_m2,
    sx_p1, sx_m1, sx_p2, sx_m2, sz_p1, sz_m1, sz_p2, sz_m2,
    sy, ry, recv_a,
    send_sems, recv_sems,
):
    frames, width = a_ref.shape
    both = 2 * frames
    half = width // 2
    slots, count, piece = ny, 2 * ny, half // 2
    dp = lax.axis_index("dp")
    m = lax.axis_index("mp")
    c = lax.rem(dp, 2)
    x = lax.rem(dp // 2, nx)
    z = dp // (2 * nx)

    def device(dc=0, dx=0, dz=0, dy=0):
        there = (lax.rem(z + dz, nz) * nx + lax.rem(x + dx, nx)) * 2
        there = there + (1 - c if dc else c)
        return (there, lax.rem(m + dy, ny))

    partner = device(dc=1)
    peers_x = [device(dx=k) for k in range(1, nx)]
    peers_z = [device(dz=k) for k in range(1, nz)]
    peers_y = [device(dy=k) for k in range(1, ny)]
    everyone = [partner] + peers_x + peers_z + peers_y

    barrier = pltpu.get_barrier_semaphore()
    for peer in everyone:
        pl.semaphore_signal(barrier, inc=1, device_id=peer, device_id_type=MESH)

    started, due, clock, free = [], {}, [0.0], {}

    def work(t):
        clock[0] += t

    def send(src, dst, peer, link=None):
        at = len(started)
        work(0.2)
        size = src.dtype.itemsize
        for d in src.shape:
            size *= d
        rate = 45e3 if link else 500e3
        begin = max(clock[0], free.get(link, 0.0)) if link else clock[0]
        end = begin + size / rate
        if link:
            free[link] = end
        copy = pltpu.make_async_remote_copy(
            src_ref=src,
            dst_ref=dst,
            send_sem=send_sems.at[at],
            recv_sem=recv_sems.at[at],
            device_id=peer,
            device_id_type=MESH,
        )
        copy.start()
        started.append(copy)
        due[id(copy)] = end + 1.5
        return copy

    def arrive(copies):
        for copy in copies:
            clock[0] = max(clock[0], due[id(copy)])
            copy.wait_recv()

    def spread_to(buf, mine, peers):
        return [send(buf.at[mine], buf.at[mine], peer) for peer in peers]

    def column_sum(fn):
        step = 64
        def body(i, acc):
            return acc + jnp.sum(fn(pl.ds(i * step, step)), axis=0, keepdims=True)
        return lax.fori_loop(0, frames // step, body, jnp.zeros((1, width), f32))

    for view, ref in enumerate((a_ref, b_ref)):
        center = column_sum(lambda rows: ref[rows, :].astype(f32)) / frames
        def deviation(rows, ref=ref, center=center):
            dev = ref[rows, :].astype(f32) - center
            return dev * dev
        stat_c[c, 0, view : view + 1, :] = center
        stat_c[c, 1, view : view + 1, :] = column_sum(deviation)

    pl.semaphore_wait(barrier, len(everyone))
    work(5.0)

    def merge(buf, members, count):
        center = sum(buf[i, 0] for i in range(members)) * (1.0 / members)
        spread = sum(buf[i, 1] for i in range(members))
        shift = sum((buf[i, 0] - center) ** 2 for i in range(members))
        return center, spread + count * shift

    arrive(spread_to(stat_c, c, [partner]))
    stat_x[x, 0], stat_x[x, 1] = merge(stat_c, 2, float(frames))
    arrive(spread_to(stat_x, x, peers_x))
    stat_z[z, 0], stat_z[z, 1] = merge(stat_x, nx, float(frames * 2))
    arrive(spread_to(stat_z, z, peers_z))
    center, spread = merge(stat_z, nz, float(frames * 2 * nx))
    inv = lax.rsqrt(spread / total + epsilon)
    center_a, center_b = center[0:1], center[1:2]
    inv_a, inv_b = inv[0:1], inv[1:2]

    own, other = pl.ds(0, frames), pl.ds(frames, frames)
    own_half = pl.ds(pl.multiple_of(c * half, 128), half)
    other_half = pl.ds(pl.multiple_of((1 - c) * half, 128), half)

    def standardize(src, dst, center, inv):
        def body(i, _):
            rows = pl.ds(pl.multiple_of(i * 32, 32), 32)
            dst[rows, :] = ((src[rows, :].astype(f32) - center) * inv).astype(bf16)
            return 0
        lax.fori_loop(0, frames // 32, body, 0)

    standardize(b_ref, nb16, center_b, inv_b)
    swap_b = [
        send(
            nb16.at[:, pl.ds(pl.multiple_of((1 - c) * half + side * piece, 128), piece)],
            nb.at[side, other], partner)
        for side in range(2)
    ]
    for side in range(2):
        nb[side, own, :] = nb16[:, pl.ds(pl.multiple_of(c * half + side * piece, 128), piece)]
    up, down = device(dy=1), device(dy=ny - 1)
    first = [send(nb.at[0, own], nb.at[3, own], up, "y+"), send(nb.at[1, own], nb.at[2, own], down, "y-")]
    standardize(a_ref, na, center_a, inv_a)
    swap_a = send(na.at[own], na.at[other], partner)
    arrive(swap_b)
    first.append(send(nb.at[0, other], nb.at[3, other], up, "y+"))
    first.append(send(nb.at[1, other], nb.at[2, other], down, "y-"))

    diag_done = []

    def diagonal():
        def body(i, acc):
            rows = pl.ds(pl.multiple_of(i * 32, 32), 32)
            wide_a = (a_ref[rows, :].astype(f32) - center_a) * inv_a
            wide_b = (b_ref[rows, :].astype(f32) - center_b) * inv_b
            short_a, short_b = na[rows, :].astype(f32), nb16[rows, :].astype(f32)
            terms = (short_a, short_b, short_a * short_b, wide_a * short_b, wide_b * short_a)
            return tuple(s + jnp.sum(t, axis=0, keepdims=True) for s, t in zip(acc, terms))
        sums = lax.fori_loop(0, frames // 32, body, (jnp.zeros((1, width), f32),) * 5)
        for at, value in enumerate(sums[:3] + (jnp.zeros((1, width), f32),) + sums[3:]):
            diag_c[c, at // 2, at % 2 : at % 2 + 1, :] = value
        work(1.5)
        copies = spread_to(diag_c, c, [partner])
        yield copies
        diag_x[x] = jnp.where(
            c == 0, diag_c[0, :, :, :half] + diag_c[1, :, :, :half],
            diag_c[0, :, :, half:] + diag_c[1, :, :, half:])
        copies = spread_to(diag_x, x, peers_x)
        yield copies
        diag_z[z] = sum(diag_x[i] for i in range(nx))
        copies = spread_to(diag_z, z, peers_z)
        yield copies
        diag_f[c] = sum(diag_z[i] for i in range(nz)) / total
        mean_b16[0] = diag_f[c, 0, 1:2]
        copies = spread_to(diag_f, c, [partner])
        copies += [send(mean_b16.at[0], mean_b16.at[SLOT[ny - k]], peers_y[k - 1]) for k in range(1, ny)]
        yield copies
        mean_a = jnp.concatenate([diag_f[0, 0, 0:1], diag_f[1, 0, 0:1]], axis=1)
        na[pl.ds(both, 16), :] = jnp.broadcast_to(mean_a, (16, width)).astype(bf16)
        for p, (slot, side) in enumerate(PIECES):
            mean_b = mean_b16[slot, :, side * piece : (side + 1) * piece]
            nb[p, pl.ds(both, 16), :] = jnp.broadcast_to(mean_b, (16, piece)).astype(bf16)
        diag_done.append(True)

    def correlate(first):
        work(1.5)
        def body(i, _):
            rows = pl.ds(pl.multiple_of(i * 256, 256), 256)
            for p in (first, first + 1):
                part[p, rows, :] = jnp.dot(nat[rows, :], nb[p, :both, :], preferred_element_type=f32)
            return 0
        lax.fori_loop(0, width // 256, body, 0)

    def sweep(group, rows, fn):
        first, count, _, columns = group
        work(0.004 * rows * count * columns / 1024)
        step = min(rows, 32)
        turns = count * (rows // step)
        per = min(turns, max(1, 16384 // (step * columns)))
        def body(i, _):
            stores = []
            for u in range(per):
                k = i * per + u
                p = first + k // (rows // step)
                r = k % (rows // step) * step if isinstance(k, int) else lax.rem(k, rows // step) * step
                stores += fn(p, r, step)
            for ref, at, value in stores:
                ref[at] = value
            return 0
        if turns == per:
            body(0, 0)
        else:
            lax.fori_loop(0, turns // per, body, 0)

    def strip(base, step):
        return pl.ds(base if isinstance(base, int) else pl.multiple_of(base, 16), step)

    def reduce_chain(group, base, rows, n, at, plus, minus, axis, off, bufs):
        out_p1, out_m1, out_p2, out_m2, in_p1, in_m1, in_p2, in_m2 = bufs
        far = n // 2
        first, count, column, columns = group
        some, window, every = pl.ds(first, count), pl.ds(off, rows), pl.ds(column, columns)
        left, right = pl.ds(column, columns // 2), pl.ds(column + columns // 2, columns // 2)
        short = pl.ds(column // 2, columns // 2)

        def pack(s, source, cols, out1, out2, in1, in2):
            rest = right if cols is left else left
            def fn(p, r, step):
                there = strip(source + r, step)
                here = strip(off + r, step)
                if s == 1:
                    return [(out1, (p, here, short), encode(part[p, there, cols]))]
                if s > 2:
                    value = encode(part[p, there, every] + decode(in2[s - 3, p, here, every]))
                    return [(out2, (s - 2, p, here, every), value)]
                value = encode(part[p, there, cols] + decode(in1[p, here, short]))
                return [
                    (out2, (0, p, here, cols), value),
                    (out2, (0, p, here, rest), encode(part[p, there, rest])),
                ]
            return fn

        for s in range(1, far + 1):
            distance = far + 1 - s
            go_p = pack(s, base + lax.rem(at + distance, n) * rows, left, out_p1, out_p2, in_p1, in_p2)
            go_m = pack(s, base + lax.rem(at + n - distance, n) * rows, right, out_m1, out_m2, in_m1, in_m2)
            sweep(group, rows, lambda p, r, step: go_p(p, r, step) + go_m(p, r, step))
            def view(ref1, ref2):
                return ref1.at[some, window, short] if s == 1 else ref2.at[s - 2, some, window, every]
            go = [
                send(view(out_p1, out_p2), view(in_p1, in_p2), plus, axis + "+"),
                send(view(out_m1, out_m2), view(in_m1, in_m2), minus, axis + "-"),
            ]
            yield go

        def finish(p, r, step):
            there = strip(base + at * rows + r, step)
            here = strip(off + r, step)
            value = part[p, there, every] + decode(in_p2[far - 2, p, here, every])
            return [(part, (p, there, every), value + decode(in_m2[far - 2, p, here, every]))]
        sweep(group, rows, finish)

    def gather_chain(group, base, rows, n, at, plus, minus, axis):
        far = n // 2
        first, count, column, columns = group
        some, every = pl.ds(first, count), pl.ds(column, columns)
        left, right = pl.ds(column, columns // 2), pl.ds(column + columns // 2, columns // 2)
        for s in range(1, far + 1):
            cols_p, cols_m = (left, right) if s == far else (every, every)
            from_p = base + lax.rem(at + n - (s - 1), n) * rows
            from_m = base + lax.rem(at + (s - 1), n) * rows
            ref_p = slope.at[some, strip(from_p, rows), cols_p]
            ref_m = slope.at[some, strip(from_m, rows), cols_m]
            yield [send(ref_p, ref_p, plus, axis + "+"), send(ref_m, ref_m, minus, axis + "-")]

    plus_x, minus_x = device(dx=1), device(dx=nx - 1)
    plus_z, minus_z = device(dz=1), device(dz=nz - 1)
    rows_x, rows_z, rows_o = width // nx, width // nz, width // (nx * nz)
    base_x = x * rows_x
    base_z = z * rows_z
    bufs_x = (sx_p1, sx_m1, sx_p2, sx_m2, rx_p1, rx_m1, rx_p2, rx_m2)
    bufs_z = (sz_p1, sz_m1, sz_p2, sz_m2, rz_p1, rz_m1, rz_p2, rz_m2)

    def slopes(group, base):
        first, count, column, columns = group
        rows, cols = strip(base, rows_o), pl.ds(column, columns)
        row_ids = lax.broadcasted_iota(jnp.int32, (rows_o, columns), 0) + base
        col_ids = lax.broadcasted_iota(jnp.int32, (rows_o, columns), 1) + (c * half + column)
        for p in range(first, first + count):
            value = 2.0 * off_weight * (part[p, rows, cols] / total)
            if p < 2:
                value = jnp.where(row_ids == col_ids + p * piece, 0.0, value)
            slope[p, rows, cols] = value.astype(bf16)

    def one_way(group):
        yield from reduce_chain(group, 0, rows_x, nx, x, plus_x, minus_x, "x", 0, bufs_x)
        yield from reduce_chain(group, base_x, rows_o, nz, z, plus_z, minus_z, "z", rows_z, bufs_z)
        slopes(group, base_x + z * rows_o)
        yield from gather_chain(group, base_x, rows_o, nz, z, plus_z, minus_z, "z")
        yield from gather_chain(group, 0, rows_x, nx, x, plus_x, minus_x, "x")

    def other_way(group):
        yield from reduce_chain(group, 0, rows_z, nz, z, plus_z, minus_z, "z", 0, bufs_z)
        yield from reduce_chain(group, base_z, rows_o, nx, x, plus_x, minus_x, "x", rows_x, bufs_x)
        slopes(group, base_z + x * rows_o)
        yield from gather_chain(group, base_z, rows_o, nx, x, plus_x, minus_x, "x")
        yield from gather_chain(group, 0, rows_z, nz, z, plus_z, minus_z, "z")

    live = []

    def spawn(rank, task):
        live.append([rank, len(started), task, []])

    def run():
        while live:
            best = None
            for entry in live:
                rank, _, _, wait = entry
                if callable(wait):
                    if not wait():
                        continue
                    ready = clock[0]
                else:
                    ready = max([clock[0]] + [due[id(copy)] for copy in wait])
                key = (max(ready, clock[0] + 0.2), rank)
                if best is None or key < best[0]:
                    best = (key, entry)
            entry = best[1]
            if not callable(entry[3]):
                arrive(entry[3])
            entry[3] = next(entry[2], None)
            if entry[3] is None:
                live.remove(entry)

    def group(rank, ways, first, post):
        left = [len(ways)]
        def chain(way, what):
            yield from way(what)
            left[0] -= 1
            if not left[0]:
                yield lambda: diag_done
                yield from post
        for at, way in enumerate(ways):
            pieces = 2 // len(ways)
            spawn(rank, chain(way, (first + at * pieces, pieces, 0, piece)))

    def to_b(first):
        work(1.5)
        for p in (first, first + 1):
            part_b[p] = jnp.dot(na[...], slope[p], preferred_element_type=f32)

    begun = []

    def to_a(first):
        fresh = not begun
        work(2.0)
        begun.append(first)
        def body(i, _):
            rows = pl.ds(pl.multiple_of(i * 256, 256), 256)
            acc = None if fresh else back_a[:, rows]
            for p in (first, first + 1):
                term = lax.dot_general(
                    nb[p], slope[p, rows, :], (((1,), (1,)), ((), ())), preferred_element_type=f32)
                acc = term if acc is None else acc + term
            back_a[:, rows] = acc
            return 0
        lax.fori_loop(0, width // 256, body, 0)

    def squares(first):
        work(0.6)
        for p in (first, first + 1):
            def body(i, acc, p=p):
                rows = pl.ds(pl.multiple_of(i * 64, 64), 64)
                s = slope[p, rows, :].astype(f32)
                s = s * s
                row_acc[rows, :] += sum(s[:, k * 128 : (k + 1) * 128] for k in range(piece // 128))
                return acc + jnp.sum(s, axis=0, keepdims=True)
            square[p] = lax.fori_loop(0, width // 64, body, jnp.zeros((1, piece), f32))

    def code(out, base, extra):
        work(0.5)
        def body(i, _):
            rows = pl.ds(pl.multiple_of(i * 64, 64), 64)
            value = part_b[base, rows, :]
            if extra is not None:
                value = value + decode(ry[extra, rows, :])
            sy[out, rows, :] = encode(value)
            return 0
        lax.fori_loop(0, both // 64, body, 0)

    def gain(base, extra):
        work(0.5)
        def body(i, _):
            rows = pl.ds(pl.multiple_of(i * 64, 64), 64)
            part_b[base, rows, :] += decode(ry[extra, rows, :])
            return 0
        lax.fori_loop(0, both // 64, body, 0)

    done, last_y = [], []

    def post(first):
        to_b(first)
        if first:
            copies = []
            if first == 6:
                yield lambda: "far" in done
            for p, peer, link in ((first, up, "y+"), (first + 1, down, "y-")):
                code(p - 2, p, p - 4 if first == 6 else None)
                copies.append(send(sy.at[p - 2], ry.at[p - 2], peer, link))
            if first == 6:
                last_y.extend(copies)
            else:
                spawn(0, after_y(first, copies))
            yield []
        else:
            done.append("own")
        to_a(first)
        squares(first)

    def after_y(first, copies):
        yield copies
        if first == 4:
            done.append("far")
            return
        yield lambda: "own" in done
        gain(1, 0)
        gain(0, 1)

    def blocks():
        yield first
        second = [send(nb.at[3, :both], nb.at[4, :both], up, "y+"), send(nb.at[2, :both], nb.at[5, :both], down, "y-")]
        third = [send(nb.at[1, :both], nb.at[7, :both], up, "y+"), send(nb.at[0, :both], nb.at[6, :both], down, "y-")]
        correlate(2)
        group(RANKS[1], WAYS[1], 2, post(2))
        yield second
        correlate(4)
        group(RANKS[2], WAYS[2], 4, post(4))
        yield third
        correlate(6)
        group(RANKS[3], WAYS[3], 6, post(6))

    WAYS = [[one_way], [one_way], [other_way], [one_way]]
    RANKS = [4, 3, 2, 1]

    row_acc[...] = jnp.zeros_like(row_acc)
    arrive([swap_a])
    for i in range(width // 128):
        cols = pl.ds(i * 128, 128)
        nat[cols, :] = jnp.transpose(na[:both, cols].astype(f32)).astype(bf16)
    work(2.0)
    correlate(0)
    spawn(0, blocks())
    group(RANKS[0], WAYS[0], 0, post(0))
    spawn(2, diagonal())
    run()

    swap_back = send(back_a.at[other, :], recv_a, partner)

    scale = 1.0 / (2.0 * off_weight)
    corr_half = diag_f[c, 1, 0:1]
    loss_off = jnp.sum(sum(square[p] for p in range(count)), axis=1, keepdims=True)
    loss_diag = jnp.sum((1.0 - corr_half) ** 2, axis=1, keepdims=True)
    loss_row = jnp.broadcast_to(loss_off * (off_weight * scale * scale) + loss_diag, (1, half))
    for p in range(slots):
        block = extra_y.at[ny + p] if p else extra_y.at[m]
        left, right = PIECES.index((p, 0)), PIECES.index((p, 1))
        block[0:1, :piece] = part_b[left, both : both + 1, :]
        block[0:1, piece:] = part_b[right, both : both + 1, :]
        block[1:2, :piece] = square[left] * scale
        block[1:2, piece:] = square[right] * scale
        block[2:3, :] = loss_row
        block[3:4, :] = jnp.zeros((1, half), f32)
    share_y = [
        send(extra_y.at[ny + SLOT[k]], extra_y.at[m], peers_y[k - 1]) for k in range(1, ny)
    ]
    extra_a[c, 0:1, :] = back_a[both : both + 1, :]
    extra_a[c, 1:2, :] = jnp.sum(jnp.transpose(row_acc[...]), axis=0, keepdims=True) * scale
    share_a = send(extra_a.at[c], extra_a.at[c], partner)

    diag = jnp.concatenate([diag_f[0], diag_f[1]], axis=2)
    mean_a16, mean_own_b16 = diag[0, 0:1], diag[0, 1:2]
    corr_ii = diag[1, 0:1]
    cross_a, cross_b = diag[2, 0:1], diag[2, 1:2]
    slope_ii = (-2.0 * (1.0 - corr_ii)).astype(bf16).astype(f32)

    arrive([share_a])
    last_a = extra_a[0] + extra_a[1]
    mean_a = last_a[0:1] + mean_own_b16 * slope_ii
    inner_a = last_a[1:2] + cross_a * slope_ii
    arrive([swap_back])

    def finish_a(i, _):
        rows = pl.ds(pl.multiple_of(i * 32, 32), 32)
        wide = (a_ref[rows, :].astype(f32) - center_a) * inv_a
        back = back_a[rows, :] + recv_a[rows, :] + slope_ii * nb16[rows, :].astype(f32)
        ga_ref[rows, :] = (inv_a * (back - mean_a - wide * inner_a)).astype(bf16)
        return 0

    lax.fori_loop(0, frames // 32, finish_a, 0)

    arrive(share_y)
    extra_c[c] = sum(extra_y[i] for i in range(ny))
    share_c = send(extra_c.at[c], extra_c.at[c], partner)

    def add_last(base, dst, at):
        for side, got in ((0, 4), (1, 5)):
            cols = pl.ds(at if isinstance(at, int) else pl.multiple_of(at + side * piece, 128), piece)
            if isinstance(at, int):
                cols = pl.ds(side * piece, piece)
            def body(i, _, side=side, got=got, cols=cols):
                rows = pl.ds(pl.multiple_of(base + i * 64, 64), 64)
                here = pl.ds(pl.multiple_of(i * 64, 64), 64)
                dst[here, cols] = part_b[side, rows, :] + decode(ry[got, rows, :])
                return 0
            lax.fori_loop(0, frames // 64, body, 0)

    arrive(last_y)
    add_last(frames, sum_b, 0)
    swap_sum = [send(sum_b, full_b.at[:, own_half], partner)]
    add_last(0, full_b, c * half)

    arrive([share_c])
    mean_b = jnp.concatenate([extra_c[0, 0:1], extra_c[1, 0:1]], axis=1) + mean_a16 * slope_ii
    inner_b = jnp.concatenate([extra_c[0, 1:2], extra_c[1, 1:2]], axis=1) + cross_b * slope_ii
    loss_ref[...] = jnp.broadcast_to(extra_c[0, 2:3, :128] + extra_c[1, 2:3, :128], (8, 128))
    arrive(swap_sum)

    def finish_b(i, _):
        rows = pl.ds(pl.multiple_of(i * 32, 32), 32)
        wide = (b_ref[rows, :].astype(f32) - center_b) * inv_b
        back = full_b[rows, :] + slope_ii * na[rows, :].astype(f32)
        gb_ref[rows, :] = (inv_b * (back - mean_b - wide * inner_b)).astype(bf16)
        return 0

    lax.fori_loop(0, frames // 32, finish_b, 0)
    for copy in started:
        copy.wait_send()


def solution(mesh):
    ny = mesh.shape["mp"]
    members = mesh.shape["dp"]
    nx = ny
    nz = members // (2 * nx)

    def per_device(view_a, view_b):
        frames, width = view_a.shape
        both, half = 2 * frames, width // 2
        rows_x, rows_z, rows_o = width // nx, width // nz, width // (nx * nz)
        vmem = pltpu.VMEM
        rings = []
        count, piece = 2 * ny, half // 2
        scratch = [
            vmem((frames, width), bf16),
            vmem((both + 16, width), bf16),
            vmem((width, both), bf16),
            vmem((count, both + 16, piece), bf16),
            vmem((count, width, piece), f32),
            vmem((count, width, piece), bf16),
            vmem((both + 16, width), f32),
            vmem((count, both + 16, piece), f32),
            vmem((frames, half), f32),
            vmem((frames, width), f32),
            vmem((2, 2, 2, width), f32),
            vmem((nx, 2, 2, width), f32),
            vmem((nz, 2, 2, width), f32),
            vmem((2, 3, 2, width), f32),
            vmem((nx, 3, 2, half), f32),
            vmem((nz, 3, 2, half), f32),
            vmem((2, 3, 2, half), f32),
            vmem((ny, 1, half), f32),
            vmem((count, 1, piece), f32),
            vmem((2 * ny, 4, half), f32),
            vmem((2, 4, half), f32),
            vmem((2, 2, width), f32),
            vmem((width, 128), f32),
        ]
        for rows, n in ((rows_x + rows_o, nx), (rows_z + rows_o, nz)):
            ring = [vmem((count, rows, piece // 2), bf16)] * 2
            rings.append(ring + [vmem((n // 2 - 1, count, rows, piece), bf16)] * 2)
        scratch += rings[0] + rings[1] + rings[0] + rings[1] + [vmem((count - 2, both, piece), bf16)] * 2 + [
            vmem((frames, width), f32),
            pltpu.SemaphoreType.DMA((256,)),
            pltpu.SemaphoreType.DMA((256,)),
        ]
        grad_a, grad_b, loss = pl.pallas_call(
            functools.partial(kernel, nx, nz, ny, float(frames * members)),
            out_shape=(
                jax.ShapeDtypeStruct((frames, width), bf16),
                jax.ShapeDtypeStruct((frames, width), bf16),
                jax.ShapeDtypeStruct((8, 128), f32),
            ),
            in_specs=[pl.BlockSpec(memory_space=vmem)] * 2,
            out_specs=[pl.BlockSpec(memory_space=vmem)] * 3,
            scratch_shapes=scratch,
            compiler_params=pltpu.CompilerParams(
                collective_id=0, has_side_effects=True, vmem_limit_bytes=56 * 1024 * 1024
            ),
            cost_estimate=pl.CostEstimate(
                flops=3 * 2 * both * width * half * ny, bytes_accessed=4 * frames * width * 2,
                transcendentals=0),
        )(view_a, view_b)
        return grad_a, grad_b, loss[0, 0]

    placed = P("dp", "mp")
    return jax.shard_map(
        per_device,
        mesh=mesh,
        in_specs=(placed, placed),
        out_specs=(placed, placed, P()),
        check_vma=False,
    )
```

```python
import functools

import jax
import jax.numpy as jnp
from jax import lax
from jax.experimental import pallas as pl
from jax.experimental.pallas import tpu as pltpu
from jax.sharding import PartitionSpec as P

epsilon = 1e-05
off_weight = 0.0051

MESH = pl.DeviceIdType.MESH
f32 = jnp.float32
bf16 = jnp.bfloat16

PIECES = ((0, 0), (0, 1), (1, 1), (2, 0), (3, 0), (3, 1), (1, 0), (2, 1))
SLOT = (0, 1, 3, 2)


tiny = 1e-37


def encode(v):
    q = v * v
    q = q * q
    return jnp.where(v < 0.0, -q, q).astype(bf16)


def decode(y):
    y = y.astype(f32)
    q = jnp.abs(y)
    q = q * lax.rsqrt(jnp.maximum(q, tiny))
    q = q * lax.rsqrt(jnp.maximum(q, tiny))
    return jnp.where(y < 0.0, -q, q)


def kernel(
    nx, nz, ny, total,
    a_ref, b_ref, ga_ref, gb_ref, loss_ref,
    nb16, na, nat, raw_a, raw_b, nb, part, slope, back_a, part_b, sum_b, full_b,
    stat_x, stat_z, stat_y, diag_c, diag_x, diag_z, diag_f,
    mean_b16, square, extra_y, extra_c, extra_a, row_acc,
    rx_p1, rx_m1, rx_p2, rx_m2, rz_p1, rz_m1, rz_p2, rz_m2,
    sx_p1, sx_m1, sx_p2, sx_m2, sz_p1, sz_m1, sz_p2, sz_m2,
    sy, ry, recv_a,
    send_sems, recv_sems,
):
    frames, width = a_ref.shape
    both = 2 * frames
    half = width // 2
    slots, count, piece = ny, 2 * ny, half // 2
    dp = lax.axis_index("dp")
    m = lax.axis_index("mp")
    c = lax.rem(dp, 2)
    x = lax.rem(dp // 2, nx)
    z = dp // (2 * nx)

    def device(dc=0, dx=0, dz=0, dy=0):
        there = (lax.rem(z + dz, nz) * nx + lax.rem(x + dx, nx)) * 2
        there = there + (1 - c if dc else c)
        return (there, lax.rem(m + dy, ny))

    partner = device(dc=1)
    peers_x = [device(dx=k) for k in range(1, nx)]
    peers_z = [device(dz=k) for k in range(1, nz)]
    peers_y = [device(dy=k) for k in range(1, ny)]
    peers_cx = [device(dc=k % 2, dx=k // 2) for k in range(1, 2 * nx)]
    everyone = peers_cx + peers_z + peers_y

    barrier = pltpu.get_barrier_semaphore()
    for peer in everyone:
        pl.semaphore_signal(barrier, inc=1, device_id=peer, device_id_type=MESH)

    started, due, clock, free = [], {}, [0.0], {}

    def work(t):
        clock[0] += t

    def send(src, dst, peer, link=None):
        at = len(started)
        work(0.2)
        size = src.dtype.itemsize
        for d in src.shape:
            size *= d
        rate = 45e3 if link else 500e3
        begin = max(clock[0], free.get(link, 0.0)) if link else clock[0]
        end = begin + size / rate
        if link:
            free[link] = end
        copy = pltpu.make_async_remote_copy(
            src_ref=src,
            dst_ref=dst,
            send_sem=send_sems.at[at],
            recv_sem=recv_sems.at[at],
            device_id=peer,
            device_id_type=MESH,
        )
        copy.start()
        started.append(copy)
        due[id(copy)] = end + 1.5
        return copy

    def arrive(copies):
        for copy in copies:
            clock[0] = max(clock[0], due[id(copy)])
            copy.wait_recv()

    def spread_to(buf, mine, peers):
        return [send(buf.at[mine], buf.at[mine], peer) for peer in peers]

    own, other = pl.ds(0, frames), pl.ds(frames, frames)
    own_half = pl.ds(pl.multiple_of(c * half, 128), half)
    up, down = device(dy=1), device(dy=ny - 1)

    def piece_of(core, side):
        return pl.ds(pl.multiple_of(core * half + side * piece, 128), piece)

    for side in range(2):
        raw_b[side, own, :] = b_ref[:, piece_of(c, side)]
    pl.semaphore_wait(barrier, len(everyone))
    work(3.0)
    first = [send(raw_b.at[0, own], raw_b.at[3, own], up, "y+"), send(raw_b.at[1, own], raw_b.at[2, own], down, "y-")]
    swap_b = [send(b_ref.at[:, piece_of(1 - c, side)], raw_b.at[side, other], partner) for side in range(2)]
    swap_a = send(a_ref, raw_a, partner)

    def column_sum(fn):
        step = 64
        def body(i, acc):
            return acc + jnp.sum(fn(pl.ds(i * step, step)), axis=0, keepdims=True)
        return lax.fori_loop(0, frames // step, body, jnp.zeros((1, width), f32))

    at_cx = 2 * x + c
    for view, ref in enumerate((a_ref, b_ref)):
        center = column_sum(lambda rows: ref[rows, :].astype(f32)) / frames
        def deviation(rows, ref=ref, center=center):
            dev = ref[rows, :].astype(f32) - center
            return dev * dev
        stat_x[at_cx, 0, view : view + 1, :] = center
        stat_x[at_cx, 1, view : view + 1, :] = column_sum(deviation)
    work(2.0)

    def merge(buf, members, count):
        center = sum(buf[i, 0] for i in range(members)) * (1.0 / members)
        spread = sum(buf[i, 1] for i in range(members))
        shift = sum((buf[i, 0] - center) ** 2 for i in range(members))
        return center, spread + count * shift

    copies = spread_to(stat_x, at_cx, peers_cx)
    arrive(swap_b)
    first.append(send(raw_b.at[0, other], raw_b.at[3, other], up, "y+"))
    first.append(send(raw_b.at[1, other], raw_b.at[2, other], down, "y-"))
    arrive(copies)
    stat_z[z, 0], stat_z[z, 1] = merge(stat_x, 2 * nx, float(frames))
    copies = spread_to(stat_z, z, peers_z)
    arrive(first)
    second = [send(raw_b.at[3], raw_b.at[4], up, "y+"), send(raw_b.at[2], raw_b.at[5], down, "y-")]
    third = [send(raw_b.at[1], raw_b.at[7], up, "y+"), send(raw_b.at[0], raw_b.at[6], down, "y-")]
    arrive(copies)
    center, spread = merge(stat_z, nz, float(frames * 2 * nx))
    inv = lax.rsqrt(spread / total + epsilon)
    center_a, center_b = center[0:1], center[1:2]
    inv_a, inv_b = inv[0:1], inv[1:2]
    stat_y[0, 0:1, :] = jnp.where(c == 0, center_b[:, :half], center_b[:, half:])
    stat_y[0, 1:2, :] = jnp.where(c == 0, inv_b[:, :half], inv_b[:, half:])
    share_stat = [send(stat_y.at[0], stat_y.at[SLOT[ny - k]], peers_y[k - 1]) for k in range(1, ny)]

    def standardize(src, src_at, dst, dst_at, base, step, center, inv):
        def body(i, _):
            rows = pl.ds(pl.multiple_of(i * step, 32), step)
            there = pl.ds(pl.multiple_of(base + i * step, 32), step)
            dst[(*dst_at, there, slice(None))] = (
                (src[(*src_at, rows, slice(None))].astype(f32) - center) * inv
            ).astype(bf16)
            return 0
        return body

    def pieces_in(first):
        work(0.4)
        for p in (first, first + 1):
            slot, side = PIECES[p]
            cols = slice(side * piece, (side + 1) * piece)
            body = standardize(raw_b, (p,), nb, (p,), 0, 64, stat_y[slot, 0:1, cols], stat_y[slot, 1:2, cols])
            lax.fori_loop(0, both // 64, body, 0)

    lax.fori_loop(0, frames // 32, standardize(a_ref, (), na, (), 0, 32, center_a, inv_a), 0)
    arrive([swap_a])
    lax.fori_loop(0, frames // 32, standardize(raw_a, (), na, (), frames, 32, center_a, inv_a), 0)
    pieces_in(0)

    diag_done = []

    def diagonal():
        lax.fori_loop(0, frames // 32, standardize(b_ref, (), nb16, (), 0, 32, center_b, inv_b), 0)
        def body(i, acc):
            rows = pl.ds(pl.multiple_of(i * 32, 32), 32)
            wide_a = (a_ref[rows, :].astype(f32) - center_a) * inv_a
            wide_b = (b_ref[rows, :].astype(f32) - center_b) * inv_b
            short_a, short_b = na[rows, :].astype(f32), nb16[rows, :].astype(f32)
            terms = (short_a, short_b, short_a * short_b, wide_a * short_b, wide_b * short_a)
            return tuple(s + jnp.sum(t, axis=0, keepdims=True) for s, t in zip(acc, terms))
        sums = lax.fori_loop(0, frames // 32, body, (jnp.zeros((1, width), f32),) * 5)
        for at, value in enumerate(sums[:3] + (jnp.zeros((1, width), f32),) + sums[3:]):
            diag_c[c, at // 2, at % 2 : at % 2 + 1, :] = value
        work(1.5)
        copies = spread_to(diag_c, c, [partner])
        yield copies
        diag_x[x] = jnp.where(
            c == 0, diag_c[0, :, :, :half] + diag_c[1, :, :, :half],
            diag_c[0, :, :, half:] + diag_c[1, :, :, half:])
        copies = spread_to(diag_x, x, peers_x)
        yield copies
        diag_z[z] = sum(diag_x[i] for i in range(nx))
        copies = spread_to(diag_z, z, peers_z)
        yield copies
        diag_f[c] = sum(diag_z[i] for i in range(nz)) / total
        mean_b16[0] = diag_f[c, 0, 1:2]
        copies = spread_to(diag_f, c, [partner])
        copies += [send(mean_b16.at[0], mean_b16.at[SLOT[ny - k]], peers_y[k - 1]) for k in range(1, ny)]
        yield copies
        mean_a = jnp.concatenate([diag_f[0, 0, 0:1], diag_f[1, 0, 0:1]], axis=1)
        na[pl.ds(both, 16), :] = jnp.broadcast_to(mean_a, (16, width)).astype(bf16)
        for p, (slot, side) in enumerate(PIECES):
            mean_b = mean_b16[slot, :, side * piece : (side + 1) * piece]
            nb[p, pl.ds(both, 16), :] = jnp.broadcast_to(mean_b, (16, piece)).astype(bf16)
        diag_done.append(True)

    def correlate(first):
        work(1.5)
        def body(i, _):
            rows = pl.ds(pl.multiple_of(i * 256, 256), 256)
            for p in (first, first + 1):
                part[p, rows, :] = jnp.dot(nat[rows, :], nb[p, :both, :], preferred_element_type=f32)
            return 0
        lax.fori_loop(0, width // 256, body, 0)

    def sweep(group, rows, fn):
        first, count, _, columns = group
        work(0.004 * rows * count * columns / 1024)
        step = min(rows, 32)
        turns = count * (rows // step)
        per = min(turns, max(1, 16384 // (step * columns)))
        def body(i, _):
            stores = []
            for u in range(per):
                k = i * per + u
                p = first + k // (rows // step)
                r = k % (rows // step) * step if isinstance(k, int) else lax.rem(k, rows // step) * step
                stores += fn(p, r, step)
            for ref, at, value in stores:
                ref[at] = value
            return 0
        if turns == per:
            body(0, 0)
        else:
            lax.fori_loop(0, turns // per, body, 0)

    def strip(base, step):
        return pl.ds(base if isinstance(base, int) else pl.multiple_of(base, 16), step)

    def reduce_chain(group, base, rows, n, at, plus, minus, axis, off, bufs):
        out_p1, out_m1, out_p2, out_m2, in_p1, in_m1, in_p2, in_m2 = bufs
        far = n // 2
        first, count, column, columns = group
        some, window, every = pl.ds(first, count), pl.ds(off, rows), pl.ds(column, columns)
        left, right = pl.ds(column, columns // 2), pl.ds(column + columns // 2, columns // 2)
        short = pl.ds(column // 2, columns // 2)

        def pack(s, source, cols, out1, out2, in1, in2):
            rest = right if cols is left else left
            def fn(p, r, step):
                there = strip(source + r, step)
                here = strip(off + r, step)
                if s == 1:
                    return [(out1, (p, here, short), encode(part[p, there, cols]))]
                if s > 2:
                    value = encode(part[p, there, every] + decode(in2[s - 3, p, here, every]))
                    return [(out2, (s - 2, p, here, every), value)]
                value = encode(part[p, there, cols] + decode(in1[p, here, short]))
                return [
                    (out2, (0, p, here, cols), value),
                    (out2, (0, p, here, rest), encode(part[p, there, rest])),
                ]
            return fn

        for s in range(1, far + 1):
            distance = far + 1 - s
            go_p = pack(s, base + lax.rem(at + distance, n) * rows, left, out_p1, out_p2, in_p1, in_p2)
            go_m = pack(s, base + lax.rem(at + n - distance, n) * rows, right, out_m1, out_m2, in_m1, in_m2)
            sweep(group, rows, lambda p, r, step: go_p(p, r, step) + go_m(p, r, step))
            def view(ref1, ref2):
                return ref1.at[some, window, short] if s == 1 else ref2.at[s - 2, some, window, every]
            go = [
                send(view(out_p1, out_p2), view(in_p1, in_p2), plus, axis + "+"),
                send(view(out_m1, out_m2), view(in_m1, in_m2), minus, axis + "-"),
            ]
            yield go

        def finish(p, r, step):
            there = strip(base + at * rows + r, step)
            here = strip(off + r, step)
            value = part[p, there, every] + decode(in_p2[far - 2, p, here, every])
            return [(part, (p, there, every), value + decode(in_m2[far - 2, p, here, every]))]
        sweep(group, rows, finish)

    def gather_chain(group, base, rows, n, at, plus, minus, axis):
        far = n // 2
        first, count, column, columns = group
        some, every = pl.ds(first, count), pl.ds(column, columns)
        left, right = pl.ds(column, columns // 2), pl.ds(column + columns // 2, columns // 2)
        for s in range(1, far + 1):
            cols_p, cols_m = (left, right) if s == far else (every, every)
            from_p = base + lax.rem(at + n - (s - 1), n) * rows
            from_m = base + lax.rem(at + (s - 1), n) * rows
            ref_p = slope.at[some, strip(from_p, rows), cols_p]
            ref_m = slope.at[some, strip(from_m, rows), cols_m]
            yield [send(ref_p, ref_p, plus, axis + "+"), send(ref_m, ref_m, minus, axis + "-")]

    plus_x, minus_x = device(dx=1), device(dx=nx - 1)
    plus_z, minus_z = device(dz=1), device(dz=nz - 1)
    rows_x, rows_z, rows_o = width // nx, width // nz, width // (nx * nz)
    base_x = x * rows_x
    base_z = z * rows_z
    bufs_x = (sx_p1, sx_m1, sx_p2, sx_m2, rx_p1, rx_m1, rx_p2, rx_m2)
    bufs_z = (sz_p1, sz_m1, sz_p2, sz_m2, rz_p1, rz_m1, rz_p2, rz_m2)

    def slopes(group, base):
        first, count, column, columns = group
        rows, cols = strip(base, rows_o), pl.ds(column, columns)
        row_ids = lax.broadcasted_iota(jnp.int32, (rows_o, columns), 0) + base
        col_ids = lax.broadcasted_iota(jnp.int32, (rows_o, columns), 1) + (c * half + column)
        for p in range(first, first + count):
            value = 2.0 * off_weight * (part[p, rows, cols] / total)
            if p < 2:
                value = jnp.where(row_ids == col_ids + p * piece, 0.0, value)
            slope[p, rows, cols] = value.astype(bf16)

    def one_way(group):
        yield from reduce_chain(group, 0, rows_x, nx, x, plus_x, minus_x, "x", 0, bufs_x)
        yield from reduce_chain(group, base_x, rows_o, nz, z, plus_z, minus_z, "z", rows_z, bufs_z)
        slopes(group, base_x + z * rows_o)
        yield from gather_chain(group, base_x, rows_o, nz, z, plus_z, minus_z, "z")
        yield from gather_chain(group, 0, rows_x, nx, x, plus_x, minus_x, "x")

    def other_way(group):
        yield from reduce_chain(group, 0, rows_z, nz, z, plus_z, minus_z, "z", 0, bufs_z)
        yield from reduce_chain(group, base_z, rows_o, nx, x, plus_x, minus_x, "x", rows_x, bufs_x)
        slopes(group, base_z + x * rows_o)
        yield from gather_chain(group, base_z, rows_o, nx, x, plus_x, minus_x, "x")
        yield from gather_chain(group, 0, rows_z, nz, z, plus_z, minus_z, "z")

    live = []

    def spawn(rank, task):
        live.append([rank, len(started), task, []])

    def run():
        while live:
            best = None
            for entry in live:
                rank, _, _, wait = entry
                if callable(wait):
                    if not wait():
                        continue
                    ready = clock[0]
                else:
                    ready = max([clock[0]] + [due[id(copy)] for copy in wait])
                key = (max(ready, clock[0] + 0.2), rank)
                if best is None or key < best[0]:
                    best = (key, entry)
            entry = best[1]
            if not callable(entry[3]):
                arrive(entry[3])
            entry[3] = next(entry[2], None)
            if entry[3] is None:
                live.remove(entry)

    def group(rank, ways, first, post):
        left = [len(ways)]
        def chain(way, what):
            yield from way(what)
            left[0] -= 1
            if not left[0]:
                yield lambda: diag_done
                yield from post
        for at, way in enumerate(ways):
            pieces = 2 // len(ways)
            spawn(rank, chain(way, (first + at * pieces, pieces, 0, piece)))

    def to_b(p):
        work(0.75)
        part_b[p] = jnp.dot(na[...], slope[p], preferred_element_type=f32)

    begun = []

    def to_a(first):
        fresh = not begun
        work(2.0)
        begun.append(first)
        def body(i, _):
            rows = pl.ds(pl.multiple_of(i * 256, 256), 256)
            acc = None if fresh else back_a[:, rows]
            for p in (first, first + 1):
                term = lax.dot_general(
                    nb[p], slope[p, rows, :], (((1,), (1,)), ((), ())), preferred_element_type=f32)
                acc = term if acc is None else acc + term
            back_a[:, rows] = acc
            return 0
        lax.fori_loop(0, width // 256, body, 0)

    def squares(first):
        work(0.6)
        for p in (first, first + 1):
            def body(i, acc, p=p):
                rows = pl.ds(pl.multiple_of(i * 64, 64), 64)
                s = slope[p, rows, :].astype(f32)
                s = s * s
                row_acc[rows, :] += sum(s[:, k * 128 : (k + 1) * 128] for k in range(piece // 128))
                return acc + jnp.sum(s, axis=0, keepdims=True)
            square[p] = lax.fori_loop(0, width // 64, body, jnp.zeros((1, piece), f32))

    def code(out, base, extra):
        work(0.5)
        def body(i, _):
            rows = pl.ds(pl.multiple_of(i * 64, 64), 64)
            value = part_b[base, rows, :]
            if extra is not None:
                value = value + decode(ry[extra, rows, :])
            sy[out, rows, :] = encode(value)
            return 0
        lax.fori_loop(0, both // 64, body, 0)

    def gain(base, extra):
        work(0.5)
        def body(i, _):
            rows = pl.ds(pl.multiple_of(i * 64, 64), 64)
            part_b[base, rows, :] += decode(ry[extra, rows, :])
            return 0
        lax.fori_loop(0, both // 64, body, 0)

    done, last_y = [], []

    def post(first):
        if first:
            copies = []
            if first == 6:
                yield lambda: "far" in done
            for p, peer, link in ((first, up, "y+"), (first + 1, down, "y-")):
                to_b(p)
                code(p - 2, p, p - 4 if first == 6 else None)
                copies.append(send(sy.at[p - 2], ry.at[p - 2], peer, link))
            if first == 6:
                last_y.extend(copies)
            else:
                spawn(0, after_y(first, copies))
            yield []
        else:
            to_b(0)
            to_b(1)
            done.append("own")
        to_a(first)
        squares(first)

    def after_y(first, copies):
        yield copies
        if first == 4:
            done.append("far")
            return
        yield lambda: "own" in done
        gain(1, 0)
        gain(0, 1)

    def blocks():
        yield share_stat
        pieces_in(2)
        correlate(2)
        group(RANKS[1], WAYS[1], 2, post(2))
        yield second
        pieces_in(4)
        correlate(4)
        group(RANKS[2], WAYS[2], 4, post(4))
        yield third
        pieces_in(6)
        correlate(6)
        group(RANKS[3], WAYS[3], 6, post(6))

    WAYS = [[one_way], [one_way], [other_way], [one_way]]
    RANKS = [4, 3, 2, 1]

    row_acc[...] = jnp.zeros_like(row_acc)
    for i in range(width // 128):
        cols = pl.ds(i * 128, 128)
        nat[cols, :] = jnp.transpose(na[:both, cols].astype(f32)).astype(bf16)
    work(2.0)
    correlate(0)
    spawn(0, blocks())
    group(RANKS[0], WAYS[0], 0, post(0))
    spawn(2, diagonal())
    run()

    swap_back = send(back_a.at[other, :], recv_a, partner)

    scale = 1.0 / (2.0 * off_weight)
    corr_half = diag_f[c, 1, 0:1]
    loss_off = jnp.sum(sum(square[p] for p in range(count)), axis=1, keepdims=True)
    loss_diag = jnp.sum((1.0 - corr_half) ** 2, axis=1, keepdims=True)
    loss_row = jnp.broadcast_to(loss_off * (off_weight * scale * scale) + loss_diag, (1, half))
    for p in range(slots):
        block = extra_y.at[ny + p] if p else extra_y.at[m]
        left, right = PIECES.index((p, 0)), PIECES.index((p, 1))
        block[0:1, :piece] = part_b[left, both : both + 1, :]
        block[0:1, piece:] = part_b[right, both : both + 1, :]
        block[1:2, :piece] = square[left] * scale
        block[1:2, piece:] = square[right] * scale
        block[2:3, :] = loss_row
        block[3:4, :] = jnp.zeros((1, half), f32)
    share_y = [
        send(extra_y.at[ny + SLOT[k]], extra_y.at[m], peers_y[k - 1]) for k in range(1, ny)
    ]
    extra_a[c, 0:1, :] = back_a[both : both + 1, :]
    extra_a[c, 1:2, :] = jnp.sum(jnp.transpose(row_acc[...]), axis=0, keepdims=True) * scale
    share_a = send(extra_a.at[c], extra_a.at[c], partner)

    diag = jnp.concatenate([diag_f[0], diag_f[1]], axis=2)
    mean_a16, mean_own_b16 = diag[0, 0:1], diag[0, 1:2]
    corr_ii = diag[1, 0:1]
    cross_a, cross_b = diag[2, 0:1], diag[2, 1:2]
    slope_ii = (-2.0 * (1.0 - corr_ii)).astype(bf16).astype(f32)

    arrive([share_a])
    last_a = extra_a[0] + extra_a[1]
    mean_a = last_a[0:1] + mean_own_b16 * slope_ii
    inner_a = last_a[1:2] + cross_a * slope_ii
    arrive([swap_back])

    def finish_a(i, _):
        rows = pl.ds(pl.multiple_of(i * 32, 32), 32)
        wide = (a_ref[rows, :].astype(f32) - center_a) * inv_a
        back = back_a[rows, :] + recv_a[rows, :] + slope_ii * nb16[rows, :].astype(f32)
        ga_ref[rows, :] = (inv_a * (back - mean_a - wide * inner_a)).astype(bf16)
        return 0

    lax.fori_loop(0, frames // 32, finish_a, 0)

    arrive(share_y)
    extra_c[c] = sum(extra_y[i] for i in range(ny))
    share_c = send(extra_c.at[c], extra_c.at[c], partner)

    def add_last(base, dst, at):
        for side, got in ((0, 4), (1, 5)):
            cols = pl.ds(at if isinstance(at, int) else pl.multiple_of(at + side * piece, 128), piece)
            if isinstance(at, int):
                cols = pl.ds(side * piece, piece)
            def body(i, _, side=side, got=got, cols=cols):
                rows = pl.ds(pl.multiple_of(base + i * 64, 64), 64)
                here = pl.ds(pl.multiple_of(i * 64, 64), 64)
                dst[here, cols] = part_b[side, rows, :] + decode(ry[got, rows, :])
                return 0
            lax.fori_loop(0, frames // 64, body, 0)

    arrive(last_y)
    add_last(frames, sum_b, 0)
    swap_sum = [send(sum_b, full_b.at[:, own_half], partner)]
    add_last(0, full_b, c * half)

    arrive([share_c])
    mean_b = jnp.concatenate([extra_c[0, 0:1], extra_c[1, 0:1]], axis=1) + mean_a16 * slope_ii
    inner_b = jnp.concatenate([extra_c[0, 1:2], extra_c[1, 1:2]], axis=1) + cross_b * slope_ii
    loss_ref[...] = jnp.broadcast_to(extra_c[0, 2:3, :128] + extra_c[1, 2:3, :128], (8, 128))
    arrive(swap_sum)

    def finish_b(i, _):
        rows = pl.ds(pl.multiple_of(i * 32, 32), 32)
        wide = (b_ref[rows, :].astype(f32) - center_b) * inv_b
        back = full_b[rows, :] + slope_ii * na[rows, :].astype(f32)
        gb_ref[rows, :] = (inv_b * (back - mean_b - wide * inner_b)).astype(bf16)
        return 0

    lax.fori_loop(0, frames // 32, finish_b, 0)
    for copy in started:
        copy.wait_send()


def solution(mesh):
    ny = mesh.shape["mp"]
    members = mesh.shape["dp"]
    nx = ny
    nz = members // (2 * nx)

    def per_device(view_a, view_b):
        frames, width = view_a.shape
        both, half = 2 * frames, width // 2
        rows_x, rows_z, rows_o = width // nx, width // nz, width // (nx * nz)
        vmem = pltpu.VMEM
        rings = []
        count, piece = 2 * ny, half // 2
        scratch = [
            vmem((frames, width), bf16),
            vmem((both + 16, width), bf16),
            vmem((width, both), bf16),
            vmem((frames, width), bf16),
            vmem((count, both, piece), bf16),
            vmem((count, both + 16, piece), bf16),
            vmem((count, width, piece), f32),
            vmem((count, width, piece), bf16),
            vmem((both + 16, width), f32),
            vmem((count, both + 16, piece), f32),
            vmem((frames, half), f32),
            vmem((frames, width), f32),
            vmem((2 * nx, 2, 2, width), f32),
            vmem((nz, 2, 2, width), f32),
            vmem((ny, 2, half), f32),
            vmem((2, 3, 2, width), f32),
            vmem((nx, 3, 2, half), f32),
            vmem((nz, 3, 2, half), f32),
            vmem((2, 3, 2, half), f32),
            vmem((ny, 1, half), f32),
            vmem((count, 1, piece), f32),
            vmem((2 * ny, 4, half), f32),
            vmem((2, 4, half), f32),
            vmem((2, 2, width), f32),
            vmem((width, 128), f32),
        ]
        for rows, n in ((rows_x + rows_o, nx), (rows_z + rows_o, nz)):
            ring = [vmem((count, rows, piece // 2), bf16)] * 2
            rings.append(ring + [vmem((n // 2 - 1, count, rows, piece), bf16)] * 2)
        scratch += rings[0] + rings[1] + rings[0] + rings[1] + [vmem((count - 2, both, piece), bf16)] * 2 + [
            vmem((frames, width), f32),
            pltpu.SemaphoreType.DMA((256,)),
            pltpu.SemaphoreType.DMA((256,)),
        ]
        grad_a, grad_b, loss = pl.pallas_call(
            functools.partial(kernel, nx, nz, ny, float(frames * members)),
            out_shape=(
                jax.ShapeDtypeStruct((frames, width), bf16),
                jax.ShapeDtypeStruct((frames, width), bf16),
                jax.ShapeDtypeStruct((8, 128), f32),
            ),
            in_specs=[pl.BlockSpec(memory_space=vmem)] * 2,
            out_specs=[pl.BlockSpec(memory_space=vmem)] * 3,
            scratch_shapes=scratch,
            compiler_params=pltpu.CompilerParams(
                collective_id=0, has_side_effects=True, vmem_limit_bytes=56 * 1024 * 1024
            ),
            cost_estimate=pl.CostEstimate(
                flops=3 * 2 * both * width * half * ny, bytes_accessed=4 * frames * width * 2,
                transcendentals=0),
        )(view_a, view_b)
        return grad_a, grad_b, loss[0, 0]

    placed = P("dp", "mp")
    return jax.shard_map(
        per_device,
        mesh=mesh,
        in_specs=(placed, placed),
        out_specs=(placed, placed, P()),
        check_vma=False,
    )
```

```python
import functools

import jax
import jax.numpy as jnp
from jax import lax
from jax.experimental import pallas as pl
from jax.experimental.pallas import tpu as pltpu
from jax.sharding import PartitionSpec as P

epsilon = 1e-05
off_weight = 0.0051

MESH = pl.DeviceIdType.MESH
f32 = jnp.float32
bf16 = jnp.bfloat16

PIECES = ((0, 0), (0, 1), (1, 1), (2, 0), (3, 0), (3, 1), (1, 0), (2, 1))
SLOT = (0, 1, 3, 2)


tiny = 1e-37


def encode(v):
    return ((v * v) * (v * jnp.abs(v))).astype(bf16)


def decode(y):
    y = y.astype(f32)
    y = y * lax.rsqrt(jnp.maximum(jnp.abs(y), tiny))
    return y * lax.rsqrt(jnp.maximum(jnp.abs(y), tiny))


def kernel(
    nx, nz, ny, total,
    a_ref, b_ref, ga_ref, gb_ref, loss_ref,
    nb16, na, nat, raw_a, raw_b, nb, part, slope, back_a, part_b, sum_b, full_b,
    stat_x, stat_z, stat_y, diag_c, diag_x, diag_z, diag_f,
    mean_b16, square, extra_y, extra_c, extra_a, row_acc,
    rx_p1, rx_m1, rx_p2, rx_m2, rz_p1, rz_m1, rz_p2, rz_m2,
    sx_p1, sx_m1, sx_p2, sx_m2, sz_p1, sz_m1, sz_p2, sz_m2,
    sy, ry, recv_a,
    send_sems, recv_sems,
):
    frames, width = a_ref.shape
    both = 2 * frames
    half = width // 2
    slots, count, piece = ny, 2 * ny, half // 2
    dp = lax.axis_index("dp")
    m = lax.axis_index("mp")
    c = lax.rem(dp, 2)
    x = lax.rem(dp // 2, nx)
    z = dp // (2 * nx)

    def device(dc=0, dx=0, dz=0, dy=0):
        there = (lax.rem(z + dz, nz) * nx + lax.rem(x + dx, nx)) * 2
        there = there + (1 - c if dc else c)
        return (there, lax.rem(m + dy, ny))

    partner = device(dc=1)
    peers_x = [device(dx=k) for k in range(1, nx)]
    peers_z = [device(dz=k) for k in range(1, nz)]
    peers_y = [device(dy=k) for k in range(1, ny)]
    peers_cx = [device(dc=k % 2, dx=k // 2) for k in range(1, 2 * nx)]
    everyone = peers_cx + peers_z + peers_y

    barrier = pltpu.get_barrier_semaphore()
    for peer in everyone:
        pl.semaphore_signal(barrier, inc=1, device_id=peer, device_id_type=MESH)

    started, waited, due, clock, free = [], [], {}, [0.0], {}

    def work(t):
        clock[0] += t

    def send(src, dst, peer, link=None):
        at = len(started)
        work(0.2)
        size = src.dtype.itemsize
        for d in src.shape:
            size *= d
        rate = 45e3 if link else 500e3
        begin = max(clock[0], free.get(link, 0.0)) if link else clock[0]
        end = begin + size / rate
        if link:
            free[link] = end
        copy = pltpu.make_async_remote_copy(
            src_ref=src,
            dst_ref=dst,
            send_sem=send_sems.at[at],
            recv_sem=recv_sems.at[at],
            device_id=peer,
            device_id_type=MESH,
        )
        copy.start()
        started.append(copy)
        due[id(copy)] = end + 1.5
        return copy

    def arrive(copies):
        for copy in copies:
            clock[0] = max(clock[0], due[id(copy)])
            copy.wait()
            waited.append(id(copy))

    def spread_to(buf, mine, peers):
        return [send(buf.at[mine], buf.at[mine], peer) for peer in peers]

    own, other = pl.ds(0, frames), pl.ds(frames, frames)
    own_half = pl.ds(pl.multiple_of(c * half, 128), half)
    up, down = device(dy=1), device(dy=ny - 1)

    def piece_of(core, side):
        return pl.ds(pl.multiple_of(core * half + side * piece, 128), piece)

    for side in range(2):
        raw_b[side, own, :] = b_ref[:, piece_of(c, side)]
    pl.semaphore_wait(barrier, len(everyone))
    work(3.0)
    first = [send(raw_b.at[0, own], raw_b.at[3, own], up, "y+"), send(raw_b.at[1, own], raw_b.at[2, own], down, "y-")]
    swap_b = [send(b_ref.at[:, piece_of(1 - c, side)], raw_b.at[side, other], partner) for side in range(2)]
    swap_a = send(a_ref, raw_a, partner)

    def column_sum(fn):
        step = 64
        def body(i, acc):
            return acc + jnp.sum(fn(pl.ds(i * step, step)), axis=0, keepdims=True)
        return lax.fori_loop(0, frames // step, body, jnp.zeros((1, width), f32))

    at_cx = 2 * x + c
    for view, ref in enumerate((a_ref, b_ref)):
        center = column_sum(lambda rows: ref[rows, :].astype(f32)) / frames
        def deviation(rows, ref=ref, center=center):
            dev = ref[rows, :].astype(f32) - center
            return dev * dev
        stat_x[at_cx, 0, view : view + 1, :] = center
        stat_x[at_cx, 1, view : view + 1, :] = column_sum(deviation)
    work(2.0)

    def merge(buf, members, count):
        center = sum(buf[i, 0] for i in range(members)) * (1.0 / members)
        spread = sum(buf[i, 1] for i in range(members))
        shift = sum((buf[i, 0] - center) ** 2 for i in range(members))
        return center, spread + count * shift

    copies = spread_to(stat_x, at_cx, peers_cx)
    arrive(swap_b)
    first.append(send(raw_b.at[0, other], raw_b.at[3, other], up, "y+"))
    first.append(send(raw_b.at[1, other], raw_b.at[2, other], down, "y-"))
    arrive(copies)
    stat_z[z, 0], stat_z[z, 1] = merge(stat_x, 2 * nx, float(frames))
    copies = spread_to(stat_z, z, peers_z)
    arrive(first)
    second = [send(raw_b.at[3], raw_b.at[4], up, "y+"), send(raw_b.at[2], raw_b.at[5], down, "y-")]
    third = [send(raw_b.at[1], raw_b.at[7], up, "y+"), send(raw_b.at[0], raw_b.at[6], down, "y-")]
    arrive(copies)
    center, spread = merge(stat_z, nz, float(frames * 2 * nx))
    inv = lax.rsqrt(spread / total + epsilon)
    center_a, center_b = center[0:1], center[1:2]
    inv_a, inv_b = inv[0:1], inv[1:2]
    stat_y[0, 0:1, :] = jnp.where(c == 0, center_b[:, :half], center_b[:, half:])
    stat_y[0, 1:2, :] = jnp.where(c == 0, inv_b[:, :half], inv_b[:, half:])
    share_stat = [send(stat_y.at[0], stat_y.at[SLOT[ny - k]], peers_y[k - 1]) for k in range(1, ny)]

    def standardize(src, src_at, dst, dst_at, base, step, center, inv):
        def body(i, _):
            rows = pl.ds(pl.multiple_of(i * step, 32), step)
            there = pl.ds(pl.multiple_of(base + i * step, 32), step)
            dst[(*dst_at, there, slice(None))] = (
                (src[(*src_at, rows, slice(None))].astype(f32) - center) * inv
            ).astype(bf16)
            return 0
        return body

    def pieces_in(first):
        work(0.4)
        for p in (first, first + 1):
            slot, side = PIECES[p]
            cols = slice(side * piece, (side + 1) * piece)
            body = standardize(raw_b, (p,), nb, (p,), 0, 64, stat_y[slot, 0:1, cols], stat_y[slot, 1:2, cols])
            lax.fori_loop(0, both // 64, body, 0)

    lax.fori_loop(0, frames // 32, standardize(a_ref, (), na, (), 0, 32, center_a, inv_a), 0)
    arrive([swap_a])
    lax.fori_loop(0, frames // 32, standardize(raw_a, (), na, (), frames, 32, center_a, inv_a), 0)
    pieces_in(0)

    diag_done = []

    def diagonal():
        lax.fori_loop(0, frames // 32, standardize(b_ref, (), nb16, (), 0, 32, center_b, inv_b), 0)
        def body(i, acc):
            rows = pl.ds(pl.multiple_of(i * 32, 32), 32)
            wide_a = (a_ref[rows, :].astype(f32) - center_a) * inv_a
            wide_b = (b_ref[rows, :].astype(f32) - center_b) * inv_b
            short_a, short_b = na[rows, :].astype(f32), nb16[rows, :].astype(f32)
            terms = (short_a, short_b, short_a * short_b, wide_a * short_b, wide_b * short_a)
            return tuple(s + jnp.sum(t, axis=0, keepdims=True) for s, t in zip(acc, terms))
        sums = lax.fori_loop(0, frames // 32, body, (jnp.zeros((1, width), f32),) * 5)
        for at, value in enumerate(sums[:3] + (jnp.zeros((1, width), f32),) + sums[3:]):
            diag_c[c, at // 2, at % 2 : at % 2 + 1, :] = value
        work(1.5)
        copies = spread_to(diag_c, c, [partner])
        yield copies
        diag_x[x] = jnp.where(
            c == 0, diag_c[0, :, :, :half] + diag_c[1, :, :, :half],
            diag_c[0, :, :, half:] + diag_c[1, :, :, half:])
        copies = spread_to(diag_x, x, peers_x)
        yield copies
        diag_z[z] = sum(diag_x[i] for i in range(nx))
        copies = spread_to(diag_z, z, peers_z)
        yield copies
        diag_f[c] = sum(diag_z[i] for i in range(nz)) / total
        mean_b16[0] = diag_f[c, 0, 1:2]
        copies = spread_to(diag_f, c, [partner])
        copies += [send(mean_b16.at[0], mean_b16.at[SLOT[ny - k]], peers_y[k - 1]) for k in range(1, ny)]
        yield copies
        mean_a = jnp.concatenate([diag_f[0, 0, 0:1], diag_f[1, 0, 0:1]], axis=1)
        na[pl.ds(both, 16), :] = jnp.broadcast_to(mean_a, (16, width)).astype(bf16)
        for p, (slot, side) in enumerate(PIECES):
            mean_b = mean_b16[slot, :, side * piece : (side + 1) * piece]
            nb[p, pl.ds(both, 16), :] = jnp.broadcast_to(mean_b, (16, piece)).astype(bf16)
        diag_done.append(True)

    def correlate(first):
        work(1.5)
        def body(i, _):
            rows = pl.ds(pl.multiple_of(i * 256, 256), 256)
            for p in (first, first + 1):
                part[p, rows, :] = jnp.dot(nat[rows, :], nb[p, :both, :], preferred_element_type=f32)
            return 0
        lax.fori_loop(0, width // 256, body, 0)

    def sweep(group, rows, fn):
        first, count, _, columns = group
        work(0.004 * rows * count * columns / 1024)
        step = min(rows, 32)
        turns = count * (rows // step)
        per = min(turns, max(1, 16384 // (step * columns)))
        def body(i, _):
            stores = []
            for u in range(per):
                k = i * per + u
                p = first + k // (rows // step)
                r = k % (rows // step) * step if isinstance(k, int) else lax.rem(k, rows // step) * step
                stores += fn(p, r, step)
            for ref, at, value in stores:
                ref[at] = value
            return 0
        if turns == per:
            body(0, 0)
        else:
            lax.fori_loop(0, turns // per, body, 0)

    def strip(base, step):
        return pl.ds(base if isinstance(base, int) else pl.multiple_of(base, 16), step)

    def reduce_chain(group, base, rows, n, at, plus, minus, axis, off, bufs):
        out_p1, out_m1, out_p2, out_m2, in_p1, in_m1, in_p2, in_m2 = bufs
        far = n // 2
        first, count, column, columns = group
        some, window, every = pl.ds(first, count), pl.ds(off, rows), pl.ds(column, columns)
        left, right = pl.ds(column, columns // 2), pl.ds(column + columns // 2, columns // 2)
        short = pl.ds(column // 2, columns // 2)

        def pack(s, source, cols, out1, out2, in1, in2):
            rest = right if cols is left else left
            def fn(p, r, step):
                there = strip(source + r, step)
                here = strip(off + r, step)
                if s == 1:
                    return [(out1, (p, here, short), encode(part[p, there, cols]))]
                if s > 2:
                    value = encode(part[p, there, every] + decode(in2[s - 3, p, here, every]))
                    return [(out2, (s - 2, p, here, every), value)]
                value = encode(part[p, there, cols] + decode(in1[p, here, short]))
                return [
                    (out2, (0, p, here, cols), value),
                    (out2, (0, p, here, rest), encode(part[p, there, rest])),
                ]
            return fn

        for s in range(1, far + 1):
            distance = far + 1 - s
            go_p = pack(s, base + lax.rem(at + distance, n) * rows, left, out_p1, out_p2, in_p1, in_p2)
            go_m = pack(s, base + lax.rem(at + n - distance, n) * rows, right, out_m1, out_m2, in_m1, in_m2)
            sweep(group, rows, lambda p, r, step: go_p(p, r, step) + go_m(p, r, step))
            def view(ref1, ref2):
                return ref1.at[some, window, short] if s == 1 else ref2.at[s - 2, some, window, every]
            go = [
                send(view(out_p1, out_p2), view(in_p1, in_p2), plus, axis + "+"),
                send(view(out_m1, out_m2), view(in_m1, in_m2), minus, axis + "-"),
            ]
            yield go

        def finish(p, r, step):
            there = strip(base + at * rows + r, step)
            here = strip(off + r, step)
            value = part[p, there, every] + decode(in_p2[far - 2, p, here, every])
            return [(part, (p, there, every), value + decode(in_m2[far - 2, p, here, every]))]
        sweep(group, rows, finish)

    def gather_chain(group, base, rows, n, at, plus, minus, axis):
        far = n // 2
        first, count, column, columns = group
        some, every = pl.ds(first, count), pl.ds(column, columns)
        left, right = pl.ds(column, columns // 2), pl.ds(column + columns // 2, columns // 2)
        for s in range(1, far + 1):
            cols_p, cols_m = (left, right) if s == far else (every, every)
            from_p = base + lax.rem(at + n - (s - 1), n) * rows
            from_m = base + lax.rem(at + (s - 1), n) * rows
            ref_p = slope.at[some, strip(from_p, rows), cols_p]
            ref_m = slope.at[some, strip(from_m, rows), cols_m]
            yield [send(ref_p, ref_p, plus, axis + "+"), send(ref_m, ref_m, minus, axis + "-")]

    plus_x, minus_x = device(dx=1), device(dx=nx - 1)
    plus_z, minus_z = device(dz=1), device(dz=nz - 1)
    rows_x, rows_z, rows_o = width // nx, width // nz, width // (nx * nz)
    base_x = x * rows_x
    base_z = z * rows_z
    bufs_x = (sx_p1, sx_m1, sx_p2, sx_m2, rx_p1, rx_m1, rx_p2, rx_m2)
    bufs_z = (sz_p1, sz_m1, sz_p2, sz_m2, rz_p1, rz_m1, rz_p2, rz_m2)

    def slopes(group, base):
        first, count, column, columns = group
        rows, cols = strip(base, rows_o), pl.ds(column, columns)
        row_ids = lax.broadcasted_iota(jnp.int32, (rows_o, columns), 0) + base
        col_ids = lax.broadcasted_iota(jnp.int32, (rows_o, columns), 1) + (c * half + column)
        for p in range(first, first + count):
            value = 2.0 * off_weight * (part[p, rows, cols] / total)
            if p < 2:
                value = jnp.where(row_ids == col_ids + p * piece, 0.0, value)
            slope[p, rows, cols] = value.astype(bf16)

    def one_way(group):
        yield from reduce_chain(group, 0, rows_x, nx, x, plus_x, minus_x, "x", 0, bufs_x)
        yield from reduce_chain(group, base_x, rows_o, nz, z, plus_z, minus_z, "z", rows_z, bufs_z)
        slopes(group, base_x + z * rows_o)
        yield from gather_chain(group, base_x, rows_o, nz, z, plus_z, minus_z, "z")
        yield from gather_chain(group, 0, rows_x, nx, x, plus_x, minus_x, "x")

    def other_way(group):
        yield from reduce_chain(group, 0, rows_z, nz, z, plus_z, minus_z, "z", 0, bufs_z)
        yield from reduce_chain(group, base_z, rows_o, nx, x, plus_x, minus_x, "x", rows_x, bufs_x)
        slopes(group, base_z + x * rows_o)
        yield from gather_chain(group, base_z, rows_o, nx, x, plus_x, minus_x, "x")
        yield from gather_chain(group, 0, rows_z, nz, z, plus_z, minus_z, "z")

    live = []

    def spawn(rank, task):
        live.append([rank, len(started), task, []])

    def run():
        while live:
            best = None
            for entry in live:
                rank, _, _, wait = entry
                if callable(wait):
                    if not wait():
                        continue
                    ready = clock[0]
                else:
                    ready = max([clock[0]] + [due[id(copy)] for copy in wait])
                key = (max(ready, clock[0] + 0.2), rank)
                if best is None or key < best[0]:
                    best = (key, entry)
            entry = best[1]
            if not callable(entry[3]):
                arrive(entry[3])
            entry[3] = next(entry[2], None)
            if entry[3] is None:
                live.remove(entry)

    def group(rank, ways, first, post):
        left = [len(ways)]
        def chain(way, what):
            yield from way(what)
            left[0] -= 1
            if not left[0]:
                if not diag_done:
                    yield lambda: diag_done
                yield from post
        for at, way in enumerate(ways):
            pieces = 2 // len(ways)
            spawn(rank, chain(way, (first + at * pieces, pieces, 0, piece)))

    def to_b(p, extra=None):
        work(1.0)
        value = jnp.dot(na[...], slope[p], preferred_element_type=f32)
        if p < 2:
            part_b[p] = value
            return
        part_b[p, both:, :] = value[both:]
        value = value[:both]
        if extra is not None:
            value = value + decode(ry[extra])
        sy[p - 2] = encode(value)

    begun = []

    def to_a(first):
        fresh = not begun
        work(2.0)
        begun.append(first)
        pair = (first, first + 1)
        def body(i, sums):
            rows = pl.ds(pl.multiple_of(i * 256, 256), 256)
            acc = None if fresh else back_a[:, rows]
            for p in pair:
                term = lax.dot_general(
                    nb[p], slope[p, rows, :], (((1,), (1,)), ((), ())), preferred_element_type=f32)
                acc = term if acc is None else acc + term
            back_a[:, rows] = acc
            over, new = None, []
            for p, total_p in zip(pair, sums):
                sq = slope[p, rows, :].astype(f32)
                sq = sq * sq
                lanes = sum(sq[:, k * 128 : (k + 1) * 128] for k in range(piece // 128))
                over = lanes if over is None else over + lanes
                new.append(total_p + jnp.sum(sq, axis=0, keepdims=True))
            row_acc[rows, :] = over if fresh else row_acc[rows, :] + over
            return tuple(new)
        sums = lax.fori_loop(0, width // 256, body, (jnp.zeros((1, piece), f32),) * 2)
        for p, value in zip(pair, sums):
            square[p] = value

    def gain(base, extra):
        work(0.5)
        def body(i, _):
            rows = pl.ds(pl.multiple_of(i * 64, 64), 64)
            part_b[base, rows, :] += decode(ry[extra, rows, :])
            return 0
        lax.fori_loop(0, both // 64, body, 0)

    done, last_y = [], []

    def post(first):
        if first:
            copies = []
            if first == 6:
                yield lambda: "far" in done
            for p, peer, link in ((first, up, "y+"), (first + 1, down, "y-")):
                to_b(p, p - 4 if first == 6 else None)
                copies.append(send(sy.at[p - 2], ry.at[p - 2], peer, link))
            if first == 6:
                last_y.extend(copies)
            else:
                spawn(0, after_y(first, copies))
            yield []
        else:
            to_b(0)
            to_b(1)
            done.append("own")
        to_a(first)

    def after_y(first, copies):
        yield copies
        if first == 4:
            done.append("far")
            return
        yield lambda: "own" in done
        gain(1, 0)
        gain(0, 1)

    def blocks():
        yield share_stat
        pieces_in(2)
        correlate(2)
        group(RANKS[1], WAYS[1], 2, post(2))
        yield second
        pieces_in(4)
        correlate(4)
        group(RANKS[2], WAYS[2], 4, post(4))
        yield third
        pieces_in(6)
        correlate(6)
        group(RANKS[3], WAYS[3], 6, post(6))

    WAYS = [[one_way], [one_way], [other_way], [one_way]]
    RANKS = [4, 3, 2, 1]

    for i in range(width // 128):
        cols = pl.ds(i * 128, 128)
        nat[cols, :] = jnp.transpose(na[:both, cols])
    work(2.0)
    correlate(0)
    group(RANKS[0], WAYS[0], 0, post(0))
    for entry in live:
        entry[3] = next(entry[2])
    spawn(0, blocks())
    spawn(1, diagonal())
    run()

    swap_back = send(back_a.at[other, :], recv_a, partner)

    scale = 1.0 / (2.0 * off_weight)
    corr_half = diag_f[c, 1, 0:1]
    loss_off = jnp.sum(sum(square[p] for p in range(count)), axis=1, keepdims=True)
    loss_diag = jnp.sum((1.0 - corr_half) ** 2, axis=1, keepdims=True)
    loss_row = jnp.broadcast_to(loss_off * (off_weight * scale * scale) + loss_diag, (1, half))
    for p in range(slots):
        block = extra_y.at[ny + p] if p else extra_y.at[m]
        left, right = PIECES.index((p, 0)), PIECES.index((p, 1))
        block[0:1, :piece] = part_b[left, both : both + 1, :]
        block[0:1, piece:] = part_b[right, both : both + 1, :]
        block[1:2, :piece] = square[left] * scale
        block[1:2, piece:] = square[right] * scale
        block[2:3, :] = loss_row
        block[3:4, :] = jnp.zeros((1, half), f32)
    share_y = [
        send(extra_y.at[ny + SLOT[k]], extra_y.at[m], peers_y[k - 1]) for k in range(1, ny)
    ]
    extra_a[c, 0:1, :] = back_a[both : both + 1, :]
    extra_a[c, 1:2, :] = jnp.sum(jnp.transpose(row_acc[...]), axis=0, keepdims=True) * scale
    share_a = send(extra_a.at[c], extra_a.at[c], partner)

    diag = jnp.concatenate([diag_f[0], diag_f[1]], axis=2)
    mean_a16, mean_own_b16 = diag[0, 0:1], diag[0, 1:2]
    corr_ii = diag[1, 0:1]
    cross_a, cross_b = diag[2, 0:1], diag[2, 1:2]
    slope_ii = (-2.0 * (1.0 - corr_ii)).astype(bf16).astype(f32)

    arrive([share_a])
    last_a = extra_a[0] + extra_a[1]
    mean_a = last_a[0:1] + mean_own_b16 * slope_ii
    inner_a = last_a[1:2] + cross_a * slope_ii
    arrive([swap_back])

    def finish_a(i, _):
        rows = pl.ds(pl.multiple_of(i * 32, 32), 32)
        wide = (a_ref[rows, :].astype(f32) - center_a) * inv_a
        back = back_a[rows, :] + recv_a[rows, :] + slope_ii * nb16[rows, :].astype(f32)
        ga_ref[rows, :] = (inv_a * (back - mean_a - wide * inner_a)).astype(bf16)
        return 0

    lax.fori_loop(0, frames // 32, finish_a, 0)

    arrive(share_y)
    extra_c[c] = sum(extra_y[i] for i in range(ny))
    share_c = send(extra_c.at[c], extra_c.at[c], partner)

    def add_last(base, dst, at):
        for side, got in ((0, 4), (1, 5)):
            cols = pl.ds(at if isinstance(at, int) else pl.multiple_of(at + side * piece, 128), piece)
            if isinstance(at, int):
                cols = pl.ds(side * piece, piece)
            def body(i, _, side=side, got=got, cols=cols):
                rows = pl.ds(pl.multiple_of(base + i * 64, 64), 64)
                here = pl.ds(pl.multiple_of(i * 64, 64), 64)
                dst[here, cols] = part_b[side, rows, :] + decode(ry[got, rows, :])
                return 0
            lax.fori_loop(0, frames // 64, body, 0)

    arrive(last_y)
    add_last(frames, sum_b, 0)
    swap_sum = [send(sum_b, full_b.at[:, own_half], partner)]
    add_last(0, full_b, c * half)

    arrive([share_c])
    mean_b = jnp.concatenate([extra_c[0, 0:1], extra_c[1, 0:1]], axis=1) + mean_a16 * slope_ii
    inner_b = jnp.concatenate([extra_c[0, 1:2], extra_c[1, 1:2]], axis=1) + cross_b * slope_ii
    loss_ref[...] = jnp.broadcast_to(extra_c[0, 2:3, :128] + extra_c[1, 2:3, :128], (8, 128))
    arrive(swap_sum)

    def finish_b(i, _):
        rows = pl.ds(pl.multiple_of(i * 32, 32), 32)
        wide = (b_ref[rows, :].astype(f32) - center_b) * inv_b
        back = full_b[rows, :] + slope_ii * na[rows, :].astype(f32)
        gb_ref[rows, :] = (inv_b * (back - mean_b - wide * inner_b)).astype(bf16)
        return 0

    lax.fori_loop(0, frames // 32, finish_b, 0)
    arrive([copy for copy in started if id(copy) not in waited])


def solution(mesh):
    ny = mesh.shape["mp"]
    members = mesh.shape["dp"]
    nx = ny
    nz = members // (2 * nx)

    def per_device(view_a, view_b):
        frames, width = view_a.shape
        both, half = 2 * frames, width // 2
        rows_x, rows_z, rows_o = width // nx, width // nz, width // (nx * nz)
        vmem = pltpu.VMEM
        rings = []
        count, piece = 2 * ny, half // 2
        scratch = [
            vmem((frames, width), bf16),
            vmem((both + 16, width), bf16),
            vmem((width, both), bf16),
            vmem((frames, width), bf16),
            vmem((count, both, piece), bf16),
            vmem((count, both + 16, piece), bf16),
            vmem((count, width, piece), f32),
            vmem((count, width, piece), bf16),
            vmem((both + 16, width), f32),
            vmem((count, both + 16, piece), f32),
            vmem((frames, half), f32),
            vmem((frames, width), f32),
            vmem((2 * nx, 2, 2, width), f32),
            vmem((nz, 2, 2, width), f32),
            vmem((ny, 2, half), f32),
            vmem((2, 3, 2, width), f32),
            vmem((nx, 3, 2, half), f32),
            vmem((nz, 3, 2, half), f32),
            vmem((2, 3, 2, half), f32),
            vmem((ny, 1, half), f32),
            vmem((count, 1, piece), f32),
            vmem((2 * ny, 4, half), f32),
            vmem((2, 4, half), f32),
            vmem((2, 2, width), f32),
            vmem((width, 128), f32),
        ]
        for rows, n in ((rows_x + rows_o, nx), (rows_z + rows_o, nz)):
            ring = [vmem((count, rows, piece // 2), bf16)] * 2
            rings.append(ring + [vmem((n // 2 - 1, count, rows, piece), bf16)] * 2)
        scratch += rings[0] + rings[1] + rings[0] + rings[1] + [vmem((count - 2, both, piece), bf16)] * 2 + [
            vmem((frames, width), f32),
            pltpu.SemaphoreType.DMA((256,)),
            pltpu.SemaphoreType.DMA((256,)),
        ]
        grad_a, grad_b, loss = pl.pallas_call(
            functools.partial(kernel, nx, nz, ny, float(frames * members)),
            out_shape=(
                jax.ShapeDtypeStruct((frames, width), bf16),
                jax.ShapeDtypeStruct((frames, width), bf16),
                jax.ShapeDtypeStruct((8, 128), f32),
            ),
            in_specs=[pl.BlockSpec(memory_space=vmem)] * 2,
            out_specs=[pl.BlockSpec(memory_space=vmem)] * 3,
            scratch_shapes=scratch,
            compiler_params=pltpu.CompilerParams(
                collective_id=0, has_side_effects=True, vmem_limit_bytes=56 * 1024 * 1024
            ),
            cost_estimate=pl.CostEstimate(
                flops=3 * 2 * both * width * half * ny, bytes_accessed=4 * frames * width * 2,
                transcendentals=0),
        )(view_a, view_b)
        return grad_a, grad_b, loss[0, 0]

    placed = P("dp", "mp")
    return jax.shard_map(
        per_device,
        mesh=mesh,
        in_specs=(placed, placed),
        out_specs=(placed, placed, P()),
        check_vma=False,
    )
```

```python
import functools

import jax
import jax.numpy as jnp
from jax import lax
from jax.experimental import pallas as pl
from jax.experimental.pallas import tpu as pltpu
from jax.sharding import PartitionSpec as P

epsilon = 1e-05
off_weight = 0.0051

MESH = pl.DeviceIdType.MESH
f32 = jnp.float32
bf16 = jnp.bfloat16

PIECES = ((0, 0), (0, 1), (1, 1), (2, 0), (3, 0), (3, 1), (1, 0), (2, 1))
SLOT = (0, 1, 3, 2)


tiny = 1e-37


def encode(v):
    return ((v * v) * (v * jnp.abs(v))).astype(bf16)


def decode(y):
    y = y.astype(f32)
    y = y * lax.rsqrt(jnp.maximum(jnp.abs(y), tiny))
    return y * lax.rsqrt(jnp.maximum(jnp.abs(y), tiny))


def kernel(
    nx, nz, ny, total,
    a_ref, b_ref, ga_ref, gb_ref, loss_ref,
    nb16, na, nat, raw_a, raw_b, nb, part, slope, back_a, part_b, sum_b, full_b,
    stat_c, stat_x, stat_z, diag_c, diag_x, diag_z, diag_f,
    mean_b16, square, extra_y, extra_c, extra_a, row_acc,
    rx_p1, rx_m1, rx_p2, rx_m2, rz_p1, rz_m1, rz_p2, rz_m2,
    sx_p1, sx_m1, sx_p2, sx_m2, sz_p1, sz_m1, sz_p2, sz_m2,
    sy, ry, send_a, recv_a, recv_b,
    send_sems, recv_sems,
):
    frames, width = a_ref.shape
    both = 2 * frames
    half = width // 2
    slots, count, piece = ny, 2 * ny, half // 2
    dp = lax.axis_index("dp")
    m = lax.axis_index("mp")
    c = lax.rem(dp, 2)
    x = lax.rem(dp // 2, nx)
    z = dp // (2 * nx)

    def device(dc=0, dx=0, dz=0, dy=0):
        there = (lax.rem(z + dz, nz) * nx + lax.rem(x + dx, nx)) * 2
        there = there + (1 - c if dc else c)
        return (there, lax.rem(m + dy, ny))

    partner = device(dc=1)
    peers_x = [device(dx=k) for k in range(1, nx)]
    peers_z = [device(dz=k) for k in range(1, nz)]
    peers_y = [device(dy=k) for k in range(1, ny)]
    everyone = [partner] + peers_x + peers_z + peers_y

    barrier = pltpu.get_barrier_semaphore()
    for peer in everyone:
        pl.semaphore_signal(barrier, inc=1, device_id=peer, device_id_type=MESH)

    started, waited, due, clock, free = [], [], {}, [0.0], {}

    def work(t):
        clock[0] += t

    def send(src, dst, peer, link=None):
        at = len(started)
        work(0.2)
        size = src.dtype.itemsize
        for d in src.shape:
            size *= d
        rate = 45e3 if link else 500e3
        begin = max(clock[0], free.get(link, 0.0)) if link else clock[0]
        end = begin + size / rate
        if link:
            free[link] = end
        copy = pltpu.make_async_remote_copy(
            src_ref=src,
            dst_ref=dst,
            send_sem=send_sems.at[at],
            recv_sem=recv_sems.at[at],
            device_id=peer,
            device_id_type=MESH,
        )
        copy.start()
        started.append(copy)
        due[id(copy)] = end + 1.5
        return copy

    def arrive(copies):
        for copy in copies:
            clock[0] = max(clock[0], due[id(copy)])
            copy.wait()
            waited.append(id(copy))

    def spread_to(buf, mine, peers):
        return [send(buf.at[mine], buf.at[mine], peer) for peer in peers]

    own, other = pl.ds(0, frames), pl.ds(frames, frames)
    up, down = device(dy=1), device(dy=ny - 1)

    def piece_of(core, side):
        return pl.ds(pl.multiple_of(core * half + side * piece, 128), piece)

    def column_sum(fn):
        step = 64
        def body(i, acc):
            return acc + jnp.sum(fn(pl.ds(i * step, step)), axis=0, keepdims=True)
        return lax.fori_loop(0, frames // step, body, jnp.zeros((1, width), f32))

    for view, ref in enumerate((a_ref, b_ref)):
        center = column_sum(lambda rows: ref[rows, :].astype(f32)) / frames
        def deviation(rows, ref=ref, center=center):
            dev = ref[rows, :].astype(f32) - center
            return dev * dev
        stat_c[c, 0, view : view + 1, :] = center
        stat_c[c, 1, view : view + 1, :] = column_sum(deviation)
    work(2.0)
    pl.semaphore_wait(barrier, len(everyone))
    work(3.0)

    def merge(buf, members, count):
        center = sum(buf[i, 0] for i in range(members)) * (1.0 / members)
        spread = sum(buf[i, 1] for i in range(members))
        shift = sum((buf[i, 0] - center) ** 2 for i in range(members))
        return center, spread + count * shift

    arrive(spread_to(stat_c, c, [partner]))
    stat_x[x, 0], stat_x[x, 1] = merge(stat_c, 2, float(frames))
    arrive(spread_to(stat_x, x, peers_x))
    stat_z[z, 0], stat_z[z, 1] = merge(stat_x, nx, float(frames * 2))
    copies = spread_to(stat_z, z, peers_z)
    swap_b = [send(b_ref.at[:, piece_of(1 - c, side)], raw_b.at[side], partner) for side in range(2)]
    swap_a = send(a_ref, raw_a, partner)
    arrive(copies)
    center, spread = merge(stat_z, nz, float(frames * 2 * nx))
    inv = lax.rsqrt(spread / total + epsilon)
    center_a, center_b = center[0:1], center[1:2]
    inv_a, inv_b = inv[0:1], inv[1:2]
    def standardize(src, src_at, dst, dst_at, base, step, center, inv):
        def body(i, _):
            rows = pl.ds(pl.multiple_of(i * step, 32), step)
            there = pl.ds(pl.multiple_of(base + i * step, 32), step)
            dst[(*dst_at, there, slice(None))] = (
                (src[(*src_at, rows, slice(None))].astype(f32) - center) * inv
            ).astype(bf16)
            return 0
        return body

    def pick(row):
        return jnp.where(c == 0, row[:, :half], row[:, half:])

    center_h, inv_h = pick(center_b), pick(inv_b)
    lax.fori_loop(0, frames // 32, standardize(b_ref, (), nb16, (), 0, 32, center_b, inv_b), 0)
    for side in range(2):
        nb[side, own, :] = nb16[:, piece_of(c, side)]
    arrive(swap_b)
    first = []
    for side, at, peer, link in ((0, 3, up, "y+"), (1, 2, down, "y-")):
        cols = slice(side * piece, (side + 1) * piece)
        body = standardize(raw_b, (side,), nb, (side,), frames, 64, center_h[:, cols], inv_h[:, cols])
        lax.fori_loop(0, frames // 64, body, 0)
        first.append(send(nb.at[side, :both], nb.at[at, :both], peer, link))
    lax.fori_loop(0, frames // 32, standardize(a_ref, (), na, (), 0, 32, center_a, inv_a), 0)
    arrive([swap_a])
    lax.fori_loop(0, frames // 32, standardize(raw_a, (), na, (), frames, 32, center_a, inv_a), 0)

    diag_done = []

    def diagonal():
        def body(i, acc):
            rows = pl.ds(pl.multiple_of(i * 32, 32), 32)
            wide_a = (a_ref[rows, :].astype(f32) - center_a) * inv_a
            wide_b = (b_ref[rows, :].astype(f32) - center_b) * inv_b
            short_a, short_b = na[rows, :].astype(f32), nb16[rows, :].astype(f32)
            terms = (short_a, short_b, short_a * short_b, wide_a * short_b, wide_b * short_a)
            return tuple(s + jnp.sum(t, axis=0, keepdims=True) for s, t in zip(acc, terms))
        sums = lax.fori_loop(0, frames // 32, body, (jnp.zeros((1, width), f32),) * 5)
        for at, value in enumerate(sums[:3] + (jnp.zeros((1, width), f32),) + sums[3:]):
            diag_c[c, at // 2, at % 2 : at % 2 + 1, :] = value
        work(1.5)
        copies = spread_to(diag_c, c, [partner])
        yield copies
        diag_x[x] = jnp.where(
            c == 0, diag_c[0, :, :, :half] + diag_c[1, :, :, :half],
            diag_c[0, :, :, half:] + diag_c[1, :, :, half:])
        copies = spread_to(diag_x, x, peers_x)
        yield copies
        diag_z[z] = sum(diag_x[i] for i in range(nx))
        copies = spread_to(diag_z, z, peers_z)
        yield copies
        diag_f[c] = sum(diag_z[i] for i in range(nz)) / total
        mean_b16[0] = diag_f[c, 0, 1:2]
        copies = spread_to(diag_f, c, [partner])
        copies += [send(mean_b16.at[0], mean_b16.at[SLOT[ny - k]], peers_y[k - 1]) for k in range(1, ny)]
        yield copies
        mean_a = jnp.concatenate([diag_f[0, 0, 0:1], diag_f[1, 0, 0:1]], axis=1)
        na[pl.ds(both, 16), :] = jnp.broadcast_to(mean_a, (16, width)).astype(bf16)
        for p, (slot, side) in enumerate(PIECES):
            mean_b = mean_b16[slot, :, side * piece : (side + 1) * piece]
            nb[p, pl.ds(both, 16), :] = jnp.broadcast_to(mean_b, (16, piece)).astype(bf16)
        diag_done.append(True)

    def correlate(first):
        work(1.5)
        def body(i, _):
            rows = pl.ds(pl.multiple_of(i * 256, 256), 256)
            for p in (first, first + 1):
                part[p, rows, :] = jnp.dot(nat[rows, :], nb[p, :both, :], preferred_element_type=f32)
            return 0
        lax.fori_loop(0, width // 256, body, 0)

    def sweep(group, rows, fn):
        first, count, _, columns = group
        work(0.004 * rows * count * columns / 1024)
        step = min(rows, 32)
        turns = count * (rows // step)
        per = min(turns, max(1, 16384 // (step * columns)))
        def body(i, _):
            stores = []
            for u in range(per):
                k = i * per + u
                p = first + k // (rows // step)
                r = k % (rows // step) * step if isinstance(k, int) else lax.rem(k, rows // step) * step
                stores += fn(p, r, step)
            for ref, at, value in stores:
                ref[at] = value
            return 0
        if turns == per:
            body(0, 0)
        else:
            lax.fori_loop(0, turns // per, body, 0)

    def strip(base, step):
        return pl.ds(base if isinstance(base, int) else pl.multiple_of(base, 16), step)

    def reduce_chain(group, base, rows, n, at, plus, minus, axis, off, bufs):
        out_p1, out_m1, out_p2, out_m2, in_p1, in_m1, in_p2, in_m2 = bufs
        far = n // 2
        first, count, column, columns = group
        some, window, every = pl.ds(first, count), pl.ds(off, rows), pl.ds(column, columns)
        left, right = pl.ds(column, columns // 2), pl.ds(column + columns // 2, columns // 2)
        short = pl.ds(column // 2, columns // 2)

        def pack(s, source, cols, out1, out2, in1, in2):
            rest = right if cols is left else left
            def fn(p, r, step):
                there = strip(source + r, step)
                here = strip(off + r, step)
                if s == 1:
                    return [(out1, (p, here, short), encode(part[p, there, cols]))]
                if s > 2:
                    value = encode(part[p, there, every] + decode(in2[s - 3, p, here, every]))
                    return [(out2, (s - 2, p, here, every), value)]
                value = encode(part[p, there, cols] + decode(in1[p, here, short]))
                return [
                    (out2, (0, p, here, cols), value),
                    (out2, (0, p, here, rest), encode(part[p, there, rest])),
                ]
            return fn

        for s in range(1, far + 1):
            distance = far + 1 - s
            go_p = pack(s, base + lax.rem(at + distance, n) * rows, left, out_p1, out_p2, in_p1, in_p2)
            go_m = pack(s, base + lax.rem(at + n - distance, n) * rows, right, out_m1, out_m2, in_m1, in_m2)
            sweep(group, rows, lambda p, r, step: go_p(p, r, step) + go_m(p, r, step))
            def view(ref1, ref2):
                return ref1.at[some, window, short] if s == 1 else ref2.at[s - 2, some, window, every]
            go = [
                send(view(out_p1, out_p2), view(in_p1, in_p2), plus, axis + "+"),
                send(view(out_m1, out_m2), view(in_m1, in_m2), minus, axis + "-"),
            ]
            yield go

        def finish(p, r, step):
            there = strip(base + at * rows + r, step)
            here = strip(off + r, step)
            value = part[p, there, every] + decode(in_p2[far - 2, p, here, every])
            return [(part, (p, there, every), value + decode(in_m2[far - 2, p, here, every]))]
        sweep(group, rows, finish)

    def gather_chain(group, base, rows, n, at, plus, minus, axis):
        far = n // 2
        first, count, column, columns = group
        some, every = pl.ds(first, count), pl.ds(column, columns)
        left, right = pl.ds(column, columns // 2), pl.ds(column + columns // 2, columns // 2)
        for s in range(1, far + 1):
            cols_p, cols_m = (left, right) if s == far else (every, every)
            from_p = base + lax.rem(at + n - (s - 1), n) * rows
            from_m = base + lax.rem(at + (s - 1), n) * rows
            ref_p = slope.at[some, strip(from_p, rows), cols_p]
            ref_m = slope.at[some, strip(from_m, rows), cols_m]
            yield [send(ref_p, ref_p, plus, axis + "+"), send(ref_m, ref_m, minus, axis + "-")]

    plus_x, minus_x = device(dx=1), device(dx=nx - 1)
    plus_z, minus_z = device(dz=1), device(dz=nz - 1)
    rows_x, rows_z, rows_o = width // nx, width // nz, width // (nx * nz)
    base_x = x * rows_x
    base_z = z * rows_z
    bufs_x = (sx_p1, sx_m1, sx_p2, sx_m2, rx_p1, rx_m1, rx_p2, rx_m2)
    bufs_z = (sz_p1, sz_m1, sz_p2, sz_m2, rz_p1, rz_m1, rz_p2, rz_m2)

    def slopes(group, base):
        first, count, column, columns = group
        rows, cols = strip(base, rows_o), pl.ds(column, columns)
        row_ids = lax.broadcasted_iota(jnp.int32, (rows_o, columns), 0) + base
        col_ids = lax.broadcasted_iota(jnp.int32, (rows_o, columns), 1) + (c * half + column)
        for p in range(first, first + count):
            value = 2.0 * off_weight * (part[p, rows, cols] / total)
            if p < 2:
                value = jnp.where(row_ids == col_ids + p * piece, 0.0, value)
            slope[p, rows, cols] = value.astype(bf16)

    def one_way(group):
        yield from reduce_chain(group, 0, rows_x, nx, x, plus_x, minus_x, "x", 0, bufs_x)
        yield from reduce_chain(group, base_x, rows_o, nz, z, plus_z, minus_z, "z", rows_z, bufs_z)
        slopes(group, base_x + z * rows_o)
        yield from gather_chain(group, base_x, rows_o, nz, z, plus_z, minus_z, "z")
        yield from gather_chain(group, 0, rows_x, nx, x, plus_x, minus_x, "x")

    def other_way(group):
        yield from reduce_chain(group, 0, rows_z, nz, z, plus_z, minus_z, "z", 0, bufs_z)
        yield from reduce_chain(group, base_z, rows_o, nx, x, plus_x, minus_x, "x", rows_x, bufs_x)
        slopes(group, base_z + x * rows_o)
        yield from gather_chain(group, base_z, rows_o, nx, x, plus_x, minus_x, "x")
        yield from gather_chain(group, 0, rows_z, nz, z, plus_z, minus_z, "z")

    live = []

    def spawn(rank, task):
        live.append([rank, len(started), task, []])

    def run():
        while live:
            best = None
            for entry in live:
                rank, _, _, wait = entry
                if callable(wait):
                    if not wait():
                        continue
                    ready = clock[0]
                else:
                    ready = max([clock[0]] + [due[id(copy)] for copy in wait])
                key = (max(ready, clock[0] + 0.2), rank)
                if best is None or key < best[0]:
                    best = (key, entry)
            entry = best[1]
            if not callable(entry[3]):
                arrive(entry[3])
            entry[3] = next(entry[2], None)
            if entry[3] is None:
                live.remove(entry)

    def group(rank, ways, first, post):
        left = [len(ways)]
        def chain(way, what):
            yield from way(what)
            left[0] -= 1
            if not left[0]:
                if not diag_done:
                    yield lambda: diag_done
                yield from post
        for at, way in enumerate(ways):
            pieces = 2 // len(ways)
            spawn(rank, chain(way, (first + at * pieces, pieces, 0, piece)))

    def to_b(p, extra=None):
        work(1.0)
        value = jnp.dot(na[...], slope[p], preferred_element_type=f32)
        if p < 2:
            part_b[p] = value
            return
        part_b[p, both:, :] = value[both:]
        value = value[:both]
        if extra is not None:
            value = value + decode(ry[extra])
        sy[p - 2] = encode(value)

    begun = []

    def to_a(first):
        fresh = not begun
        work(2.0)
        begun.append(first)
        pair = (first, first + 1)
        def body(i, sums):
            rows = pl.ds(pl.multiple_of(i * 256, 256), 256)
            acc = None if fresh else back_a[:, rows]
            for p in pair:
                term = lax.dot_general(
                    nb[p], slope[p, rows, :], (((1,), (1,)), ((), ())), preferred_element_type=f32)
                acc = term if acc is None else acc + term
            back_a[:, rows] = acc
            over, new = None, []
            for p, total_p in zip(pair, sums):
                sq = slope[p, rows, :].astype(f32)
                sq = sq * sq
                lanes = sum(sq[:, k * 128 : (k + 1) * 128] for k in range(piece // 128))
                over = lanes if over is None else over + lanes
                new.append(total_p + jnp.sum(sq, axis=0, keepdims=True))
            row_acc[rows, :] = over if fresh else row_acc[rows, :] + over
            return tuple(new)
        sums = lax.fori_loop(0, width // 256, body, (jnp.zeros((1, piece), f32),) * 2)
        for p, value in zip(pair, sums):
            square[p] = value

    def gain(base, extra):
        work(0.5)
        def body(i, _):
            rows = pl.ds(pl.multiple_of(i * 64, 64), 64)
            part_b[base, rows, :] += decode(ry[extra, rows, :])
            return 0
        lax.fori_loop(0, both // 64, body, 0)

    done, last_y = [], []

    def post(first):
        if first:
            copies = []
            if first == 6:
                yield lambda: "far" in done
            for p, peer, link in ((first, up, "y+"), (first + 1, down, "y-")):
                to_b(p, p - 4 if first == 6 else None)
                copies.append(send(sy.at[p - 2], ry.at[p - 2], peer, link))
            if first == 6:
                last_y.extend(copies)
            else:
                spawn(0, after_y(first, copies))
            yield []
        else:
            to_b(0)
            to_b(1)
            done.append("own")
        to_a(first)

    def after_y(first, copies):
        yield copies
        if first == 4:
            done.append("far")
            return
        yield lambda: "own" in done
        gain(1, 0)
        gain(0, 1)

    def blocks():
        yield first
        second = [send(nb.at[3, :both], nb.at[4, :both], up, "y+"), send(nb.at[2, :both], nb.at[5, :both], down, "y-")]
        third = [send(nb.at[1, :both], nb.at[7, :both], up, "y+"), send(nb.at[0, :both], nb.at[6, :both], down, "y-")]
        correlate(2)
        group(RANKS[1], WAYS[1], 2, post(2))
        yield second
        correlate(4)
        group(RANKS[2], WAYS[2], 4, post(4))
        yield third
        correlate(6)
        group(RANKS[3], WAYS[3], 6, post(6))

    WAYS = [[one_way], [one_way], [other_way], [one_way]]
    RANKS = [4, 3, 2, 1]

    for i in range(width // 128):
        cols = pl.ds(i * 128, 128)
        nat[cols, :] = jnp.transpose(na[:both, cols])
    work(2.0)
    correlate(0)
    group(RANKS[0], WAYS[0], 0, post(0))
    for entry in live:
        entry[3] = next(entry[2])
    spawn(0, blocks())
    spawn(1, diagonal())
    run()

    def code_a(i, _):
        rows = pl.ds(pl.multiple_of(i * 32, 32), 32)
        there = pl.ds(pl.multiple_of(i * 32 + frames, 32), 32)
        send_a[rows, :] = encode(back_a[there, :])
        return 0

    lax.fori_loop(0, frames // 32, code_a, 0)
    swap_back = send(send_a, recv_a, partner)

    scale = 1.0 / (2.0 * off_weight)
    corr_half = diag_f[c, 1, 0:1]
    loss_off = jnp.sum(sum(square[p] for p in range(count)), axis=1, keepdims=True)
    loss_diag = jnp.sum((1.0 - corr_half) ** 2, axis=1, keepdims=True)
    loss_row = jnp.broadcast_to(loss_off * (off_weight * scale * scale) + loss_diag, (1, half))
    for p in range(slots):
        block = extra_y.at[ny + p] if p else extra_y.at[m]
        left, right = PIECES.index((p, 0)), PIECES.index((p, 1))
        block[0:1, :piece] = part_b[left, both : both + 1, :]
        block[0:1, piece:] = part_b[right, both : both + 1, :]
        block[1:2, :piece] = square[left] * scale
        block[1:2, piece:] = square[right] * scale
        block[2:3, :] = loss_row
        block[3:4, :] = jnp.zeros((1, half), f32)
    share_y = [
        send(extra_y.at[ny + SLOT[k]], extra_y.at[m], peers_y[k - 1]) for k in range(1, ny)
    ]
    extra_a[c, 0:1, :] = back_a[both : both + 1, :]
    extra_a[c, 1:2, :] = jnp.sum(jnp.transpose(row_acc[...]), axis=0, keepdims=True) * scale
    share_a = send(extra_a.at[c], extra_a.at[c], partner)

    diag = jnp.concatenate([diag_f[0], diag_f[1]], axis=2)
    mean_a16, mean_own_b16 = diag[0, 0:1], diag[0, 1:2]
    corr_ii = diag[1, 0:1]
    cross_a, cross_b = diag[2, 0:1], diag[2, 1:2]
    slope_ii = (-2.0 * (1.0 - corr_ii)).astype(bf16).astype(f32)

    arrive([share_a])
    last_a = extra_a[0] + extra_a[1]
    mean_a = last_a[0:1] + mean_own_b16 * slope_ii
    inner_a = last_a[1:2] + cross_a * slope_ii
    arrive([swap_back])

    def finish_a(i, _):
        rows = pl.ds(pl.multiple_of(i * 32, 32), 32)
        wide = (a_ref[rows, :].astype(f32) - center_a) * inv_a
        back = back_a[rows, :] + decode(recv_a[rows, :]) + slope_ii * nb16[rows, :].astype(f32)
        ga_ref[rows, :] = (inv_a * (back - mean_a - wide * inner_a)).astype(bf16)
        return 0

    lax.fori_loop(0, frames // 32, finish_a, 0)

    arrive(share_y)
    extra_c[c] = sum(extra_y[i] for i in range(ny))
    share_c = send(extra_c.at[c], extra_c.at[c], partner)

    def add_last(base, store):
        for side, got in ((0, 4), (1, 5)):
            def body(i, _, side=side, got=got):
                rows = pl.ds(pl.multiple_of(base + i * 64, 64), 64)
                here = pl.ds(pl.multiple_of(i * 64, 64), 64)
                store(side, here, part_b[side, rows, :] + decode(ry[got, rows, :]))
                return 0
            lax.fori_loop(0, frames // 64, body, 0)

    def store_other(side, rows, value):
        sum_b[rows, side * piece : (side + 1) * piece] = encode(value)

    def store_own(side, rows, value):
        full_b[rows, piece_of(c, side)] = value

    arrive(last_y)
    add_last(frames, store_other)
    swap_sum = [send(sum_b, recv_b, partner)]
    add_last(0, store_own)

    arrive([share_c])
    mean_b = jnp.concatenate([extra_c[0, 0:1], extra_c[1, 0:1]], axis=1) + mean_a16 * slope_ii
    inner_b = jnp.concatenate([extra_c[0, 1:2], extra_c[1, 1:2]], axis=1) + cross_b * slope_ii
    loss_ref[...] = jnp.broadcast_to(extra_c[0, 2:3, :128] + extra_c[1, 2:3, :128], (8, 128))
    arrive(swap_sum)
    there_half = pl.ds(pl.multiple_of((1 - c) * half, 128), half)

    def take_b(i, _):
        rows = pl.ds(pl.multiple_of(i * 32, 32), 32)
        full_b[rows, there_half] = decode(recv_b[rows, :])
        return 0

    lax.fori_loop(0, frames // 32, take_b, 0)

    def finish_b(i, _):
        rows = pl.ds(pl.multiple_of(i * 32, 32), 32)
        wide = (b_ref[rows, :].astype(f32) - center_b) * inv_b
        back = full_b[rows, :] + slope_ii * na[rows, :].astype(f32)
        gb_ref[rows, :] = (inv_b * (back - mean_b - wide * inner_b)).astype(bf16)
        return 0

    lax.fori_loop(0, frames // 32, finish_b, 0)
    arrive([copy for copy in started if id(copy) not in waited])


def solution(mesh):
    ny = mesh.shape["mp"]
    members = mesh.shape["dp"]
    nx = ny
    nz = members // (2 * nx)

    def per_device(view_a, view_b):
        frames, width = view_a.shape
        both, half = 2 * frames, width // 2
        rows_x, rows_z, rows_o = width // nx, width // nz, width // (nx * nz)
        vmem = pltpu.VMEM
        rings = []
        count, piece = 2 * ny, half // 2
        scratch = [
            vmem((frames, width), bf16),
            vmem((both + 16, width), bf16),
            vmem((width, both), bf16),
            vmem((frames, width), bf16),
            vmem((2, frames, piece), bf16),
            vmem((count, both + 16, piece), bf16),
            vmem((count, width, piece), f32),
            vmem((count, width, piece), bf16),
            vmem((both + 16, width), f32),
            vmem((count, both + 16, piece), f32),
            vmem((frames, half), bf16),
            vmem((frames, width), f32),
            vmem((2, 2, 2, width), f32),
            vmem((nx, 2, 2, width), f32),
            vmem((nz, 2, 2, width), f32),
            vmem((2, 3, 2, width), f32),
            vmem((nx, 3, 2, half), f32),
            vmem((nz, 3, 2, half), f32),
            vmem((2, 3, 2, half), f32),
            vmem((ny, 1, half), f32),
            vmem((count, 1, piece), f32),
            vmem((2 * ny, 4, half), f32),
            vmem((2, 4, half), f32),
            vmem((2, 2, width), f32),
            vmem((width, 128), f32),
        ]
        for rows, n in ((rows_x + rows_o, nx), (rows_z + rows_o, nz)):
            ring = [vmem((count, rows, piece // 2), bf16)] * 2
            rings.append(ring + [vmem((n // 2 - 1, count, rows, piece), bf16)] * 2)
        scratch += rings[0] + rings[1] + rings[0] + rings[1] + [vmem((count - 2, both, piece), bf16)] * 2 + [
            vmem((frames, width), bf16),
            vmem((frames, width), bf16),
            vmem((frames, half), bf16),
            pltpu.SemaphoreType.DMA((256,)),
            pltpu.SemaphoreType.DMA((256,)),
        ]
        grad_a, grad_b, loss = pl.pallas_call(
            functools.partial(kernel, nx, nz, ny, float(frames * members)),
            out_shape=(
                jax.ShapeDtypeStruct((frames, width), bf16),
                jax.ShapeDtypeStruct((frames, width), bf16),
                jax.ShapeDtypeStruct((8, 128), f32),
            ),
            in_specs=[pl.BlockSpec(memory_space=vmem)] * 2,
            out_specs=[pl.BlockSpec(memory_space=vmem)] * 3,
            scratch_shapes=scratch,
            compiler_params=pltpu.CompilerParams(
                collective_id=0, has_side_effects=True, vmem_limit_bytes=56 * 1024 * 1024
            ),
            cost_estimate=pl.CostEstimate(
                flops=3 * 2 * both * width * half * ny, bytes_accessed=4 * frames * width * 2,
                transcendentals=0),
        )(view_a, view_b)
        return grad_a, grad_b, loss[0, 0]

    placed = P("dp", "mp")
    return jax.shard_map(
        per_device,
        mesh=mesh,
        in_specs=(placed, placed),
        out_specs=(placed, placed, P()),
        check_vma=False,
    )
```

```python
import functools

import jax
import jax.numpy as jnp
from jax import lax
from jax.experimental import pallas as pl
from jax.experimental.pallas import tpu as pltpu
from jax.sharding import PartitionSpec as P

epsilon = 1e-05
off_weight = 0.0051

MESH = pl.DeviceIdType.MESH
f32 = jnp.float32
bf16 = jnp.bfloat16

PIECES = ((0, 0), (0, 1), (1, 1), (2, 0), (3, 0), (3, 1), (1, 0), (2, 1))
SLOT = (0, 1, 3, 2)


tiny = 1e-37


def encode(v):
    return ((v * v) * (v * jnp.abs(v))).astype(bf16)


def decode(y):
    y = y.astype(f32)
    y = y * lax.rsqrt(jnp.maximum(jnp.abs(y), tiny))
    return y * lax.rsqrt(jnp.maximum(jnp.abs(y), tiny))


def kernel(
    nx, nz, ny, total,
    a_ref, b_ref, ga_ref, gb_ref, loss_ref,
    nb16, na, nat, raw_a, raw_b, nb, part, slope, back_a, part_b, sum_b, full_b,
    stat_c, stat_x, stat_z, diag_c, diag_x, diag_z, diag_f,
    mean_b16, square, extra_y, extra_c, extra_a, row_acc,
    rx_p1, rx_m1, rx_p2, rx_m2, rz_p1, rz_m1, rz_p2, rz_m2,
    sx_p1, sx_m1, sx_p2, sx_m2, sz_p1, sz_m1, sz_p2, sz_m2,
    sy, ry, send_a, recv_a, recv_b,
    send_sems, recv_sems,
):
    frames, width = a_ref.shape
    both = 2 * frames
    half = width // 2
    slots, count, piece = ny, 2 * ny, half // 2
    dp = lax.axis_index("dp")
    m = lax.axis_index("mp")
    c = lax.rem(dp, 2)
    x = lax.rem(dp // 2, nx)
    z = dp // (2 * nx)

    def device(dc=0, dx=0, dz=0, dy=0):
        there = (lax.rem(z + dz, nz) * nx + lax.rem(x + dx, nx)) * 2
        there = there + (1 - c if dc else c)
        return (there, lax.rem(m + dy, ny))

    partner = device(dc=1)
    peers_x = [device(dx=k) for k in range(1, nx)]
    peers_z = [device(dz=k) for k in range(1, nz)]
    peers_y = [device(dy=k) for k in range(1, ny)]
    everyone = [partner] + peers_x + peers_z + peers_y

    barrier = pltpu.get_barrier_semaphore()
    for peer in everyone:
        pl.semaphore_signal(barrier, inc=1, device_id=peer, device_id_type=MESH)

    started, due, clock, free = [], {}, [0.0], {}

    def work(t):
        clock[0] += t

    def send(src, dst, peer, link=None):
        at = len(started)
        work(0.2)
        size = src.dtype.itemsize
        for d in src.shape:
            size *= d
        rate = 45e3 if link else 500e3
        begin = max(clock[0], free.get(link, 0.0)) if link else clock[0]
        end = begin + size / rate
        if link:
            free[link] = end
        copy = pltpu.make_async_remote_copy(
            src_ref=src,
            dst_ref=dst,
            send_sem=send_sems.at[at],
            recv_sem=recv_sems.at[at],
            device_id=peer,
            device_id_type=MESH,
        )
        copy.start()
        started.append(copy)
        due[id(copy)] = end + 1.5
        return copy

    def arrive(copies):
        for copy in copies:
            clock[0] = max(clock[0], due[id(copy)])
            copy.wait_recv()

    def spread_to(buf, mine, peers):
        return [send(buf.at[mine], buf.at[mine], peer) for peer in peers]

    own, other = pl.ds(0, frames), pl.ds(frames, frames)
    up, down = device(dy=1), device(dy=ny - 1)

    def piece_of(core, side):
        return pl.ds(pl.multiple_of(core * half + side * piece, 128), piece)

    def column_sum(fn):
        step = 64
        def body(i, acc):
            return acc + jnp.sum(fn(pl.ds(i * step, step)), axis=0, keepdims=True)
        return lax.fori_loop(0, frames // step, body, jnp.zeros((1, width), f32))

    for view, ref in enumerate((a_ref, b_ref)):
        center = column_sum(lambda rows: ref[rows, :].astype(f32)) / frames
        def deviation(rows, ref=ref, center=center):
            dev = ref[rows, :].astype(f32) - center
            return dev * dev
        stat_c[c, 0, view : view + 1, :] = center
        stat_c[c, 1, view : view + 1, :] = column_sum(deviation)
    work(2.0)
    pl.semaphore_wait(barrier, len(everyone))
    work(3.0)

    def merge(buf, members, count):
        center = sum(buf[i, 0] for i in range(members)) * (1.0 / members)
        spread = sum(buf[i, 1] for i in range(members))
        shift = sum((buf[i, 0] - center) ** 2 for i in range(members))
        return center, spread + count * shift

    arrive(spread_to(stat_c, c, [partner]))
    stat_x[x, 0], stat_x[x, 1] = merge(stat_c, 2, float(frames))
    arrive(spread_to(stat_x, x, peers_x))
    stat_z[z, 0], stat_z[z, 1] = merge(stat_x, nx, float(frames * 2))
    copies = spread_to(stat_z, z, peers_z)
    swap_b = [send(b_ref.at[:, piece_of(1 - c, side)], raw_b.at[side], partner) for side in range(2)]
    swap_a = send(a_ref, raw_a, partner)
    arrive(copies)
    center, spread = merge(stat_z, nz, float(frames * 2 * nx))
    inv = lax.rsqrt(spread / total + epsilon)
    center_a, center_b = center[0:1], center[1:2]
    inv_a, inv_b = inv[0:1], inv[1:2]
    def standardize(src, src_at, dst, dst_at, base, step, center, inv):
        def body(i, _):
            rows = pl.ds(pl.multiple_of(i * step, 32), step)
            there = pl.ds(pl.multiple_of(base + i * step, 32), step)
            dst[(*dst_at, there, slice(None))] = (
                (src[(*src_at, rows, slice(None))].astype(f32) - center) * inv
            ).astype(bf16)
            return 0
        return body

    def pick(row):
        return jnp.where(c == 0, row[:, :half], row[:, half:])

    center_h, inv_h = pick(center_b), pick(inv_b)
    lax.fori_loop(0, frames // 32, standardize(b_ref, (), nb16, (), 0, 32, center_b, inv_b), 0)
    for side in range(2):
        nb[side, own, :] = nb16[:, piece_of(c, side)]
    arrive(swap_b)
    first = []
    for side, at, peer, link in ((0, 3, up, "y+"), (1, 2, down, "y-")):
        cols = slice(side * piece, (side + 1) * piece)
        body = standardize(raw_b, (side,), nb, (side,), frames, 64, center_h[:, cols], inv_h[:, cols])
        lax.fori_loop(0, frames // 64, body, 0)
        first.append(send(nb.at[side, :both], nb.at[at, :both], peer, link))
    lax.fori_loop(0, frames // 32, standardize(a_ref, (), na, (), 0, 32, center_a, inv_a), 0)
    arrive([swap_a])
    lax.fori_loop(0, frames // 32, standardize(raw_a, (), na, (), frames, 32, center_a, inv_a), 0)

    diag_done = []

    def diagonal():
        def body(i, acc):
            rows = pl.ds(pl.multiple_of(i * 32, 32), 32)
            wide_a = (a_ref[rows, :].astype(f32) - center_a) * inv_a
            wide_b = (b_ref[rows, :].astype(f32) - center_b) * inv_b
            short_a, short_b = na[rows, :].astype(f32), nb16[rows, :].astype(f32)
            terms = (short_a, short_b, short_a * short_b, wide_a * short_b, wide_b * short_a)
            return tuple(s + jnp.sum(t, axis=0, keepdims=True) for s, t in zip(acc, terms))
        sums = lax.fori_loop(0, frames // 32, body, (jnp.zeros((1, width), f32),) * 5)
        for at, value in enumerate(sums[:3] + (jnp.zeros((1, width), f32),) + sums[3:]):
            diag_c[c, at // 2, at % 2 : at % 2 + 1, :] = value
        work(1.5)
        copies = spread_to(diag_c, c, [partner])
        yield copies
        diag_x[x] = jnp.where(
            c == 0, diag_c[0, :, :, :half] + diag_c[1, :, :, :half],
            diag_c[0, :, :, half:] + diag_c[1, :, :, half:])
        copies = spread_to(diag_x, x, peers_x)
        yield copies
        diag_z[z] = sum(diag_x[i] for i in range(nx))
        copies = spread_to(diag_z, z, peers_z)
        yield copies
        diag_f[c] = sum(diag_z[i] for i in range(nz)) / total
        mean_b16[0] = diag_f[c, 0, 1:2]
        copies = spread_to(diag_f, c, [partner])
        copies += [send(mean_b16.at[0], mean_b16.at[SLOT[ny - k]], peers_y[k - 1]) for k in range(1, ny)]
        yield copies
        mean_a = jnp.concatenate([diag_f[0, 0, 0:1], diag_f[1, 0, 0:1]], axis=1)
        na[pl.ds(both, 16), :] = jnp.broadcast_to(mean_a, (16, width)).astype(bf16)
        for p, (slot, side) in enumerate(PIECES):
            mean_b = mean_b16[slot, :, side * piece : (side + 1) * piece]
            nb[p, pl.ds(both, 16), :] = jnp.broadcast_to(mean_b, (16, piece)).astype(bf16)
        diag_done.append(True)

    def correlate(first):
        work(1.5)
        def body(i, _):
            rows = pl.ds(pl.multiple_of(i * 256, 256), 256)
            for p in (first, first + 1):
                part[p, rows, :] = jnp.dot(nat[rows, :], nb[p, :both, :], preferred_element_type=f32)
            return 0
        lax.fori_loop(0, width // 256, body, 0)

    def sweep(group, rows, fn):
        first, count, _, columns = group
        work(0.004 * rows * count * columns / 1024)
        step = min(rows, 32)
        turns = count * (rows // step)
        per = min(turns, max(1, 16384 // (step * columns)))
        def body(i, _):
            stores = []
            for u in range(per):
                k = i * per + u
                p = first + k // (rows // step)
                r = k % (rows // step) * step if isinstance(k, int) else lax.rem(k, rows // step) * step
                stores += fn(p, r, step)
            for ref, at, value in stores:
                ref[at] = value
            return 0
        if turns == per:
            body(0, 0)
        else:
            lax.fori_loop(0, turns // per, body, 0)

    def strip(base, step):
        return pl.ds(base if isinstance(base, int) else pl.multiple_of(base, 16), step)

    def reduce_chain(group, base, rows, n, at, plus, minus, axis, off, bufs):
        out_p1, out_m1, out_p2, out_m2, in_p1, in_m1, in_p2, in_m2 = bufs
        far = n // 2
        first, count, column, columns = group
        some, window, every = pl.ds(first, count), pl.ds(off, rows), pl.ds(column, columns)
        left, right = pl.ds(column, columns // 2), pl.ds(column + columns // 2, columns // 2)
        short = pl.ds(column // 2, columns // 2)

        def pack(s, source, cols, out1, out2, in1, in2):
            rest = right if cols is left else left
            def fn(p, r, step):
                there = strip(source + r, step)
                here = strip(off + r, step)
                if s == 1:
                    return [(out1, (p, here, short), encode(part[p, there, cols]))]
                if s > 2:
                    value = encode(part[p, there, every] + decode(in2[s - 3, p, here, every]))
                    return [(out2, (s - 2, p, here, every), value)]
                value = encode(part[p, there, cols] + decode(in1[p, here, short]))
                return [
                    (out2, (0, p, here, cols), value),
                    (out2, (0, p, here, rest), encode(part[p, there, rest])),
                ]
            return fn

        for s in range(1, far + 1):
            distance = far + 1 - s
            go_p = pack(s, base + lax.rem(at + distance, n) * rows, left, out_p1, out_p2, in_p1, in_p2)
            go_m = pack(s, base + lax.rem(at + n - distance, n) * rows, right, out_m1, out_m2, in_m1, in_m2)
            sweep(group, rows, lambda p, r, step: go_p(p, r, step) + go_m(p, r, step))
            def view(ref1, ref2):
                return ref1.at[some, window, short] if s == 1 else ref2.at[s - 2, some, window, every]
            go = [
                send(view(out_p1, out_p2), view(in_p1, in_p2), plus, axis + "+"),
                send(view(out_m1, out_m2), view(in_m1, in_m2), minus, axis + "-"),
            ]
            yield go

        def finish(p, r, step):
            there = strip(base + at * rows + r, step)
            here = strip(off + r, step)
            value = part[p, there, every] + decode(in_p2[far - 2, p, here, every])
            return [(part, (p, there, every), value + decode(in_m2[far - 2, p, here, every]))]
        sweep(group, rows, finish)

    def gather_chain(group, base, rows, n, at, plus, minus, axis):
        far = n // 2
        first, count, column, columns = group
        some, every = pl.ds(first, count), pl.ds(column, columns)
        left, right = pl.ds(column, columns // 2), pl.ds(column + columns // 2, columns // 2)
        for s in range(1, far + 1):
            cols_p, cols_m = (left, right) if s == far else (every, every)
            from_p = base + lax.rem(at + n - (s - 1), n) * rows
            from_m = base + lax.rem(at + (s - 1), n) * rows
            ref_p = slope.at[some, strip(from_p, rows), cols_p]
            ref_m = slope.at[some, strip(from_m, rows), cols_m]
            yield [send(ref_p, ref_p, plus, axis + "+"), send(ref_m, ref_m, minus, axis + "-")]

    plus_x, minus_x = device(dx=1), device(dx=nx - 1)
    plus_z, minus_z = device(dz=1), device(dz=nz - 1)
    rows_x, rows_z, rows_o = width // nx, width // nz, width // (nx * nz)
    base_x = x * rows_x
    base_z = z * rows_z
    bufs_x = (sx_p1, sx_m1, sx_p2, sx_m2, rx_p1, rx_m1, rx_p2, rx_m2)
    bufs_z = (sz_p1, sz_m1, sz_p2, sz_m2, rz_p1, rz_m1, rz_p2, rz_m2)

    def slopes(group, base):
        first, count, column, columns = group
        rows, cols = strip(base, rows_o), pl.ds(column, columns)
        row_ids = lax.broadcasted_iota(jnp.int32, (rows_o, columns), 0) + base
        col_ids = lax.broadcasted_iota(jnp.int32, (rows_o, columns), 1) + (c * half + column)
        for p in range(first, first + count):
            value = 2.0 * off_weight * (part[p, rows, cols] / total)
            if p < 2:
                value = jnp.where(row_ids == col_ids + p * piece, 0.0, value)
            slope[p, rows, cols] = value.astype(bf16)

    def one_way(group):
        yield from reduce_chain(group, 0, rows_x, nx, x, plus_x, minus_x, "x", 0, bufs_x)
        yield from reduce_chain(group, base_x, rows_o, nz, z, plus_z, minus_z, "z", rows_z, bufs_z)
        slopes(group, base_x + z * rows_o)
        yield from gather_chain(group, base_x, rows_o, nz, z, plus_z, minus_z, "z")
        yield from gather_chain(group, 0, rows_x, nx, x, plus_x, minus_x, "x")

    def other_way(group):
        yield from reduce_chain(group, 0, rows_z, nz, z, plus_z, minus_z, "z", 0, bufs_z)
        yield from reduce_chain(group, base_z, rows_o, nx, x, plus_x, minus_x, "x", rows_x, bufs_x)
        slopes(group, base_z + x * rows_o)
        yield from gather_chain(group, base_z, rows_o, nx, x, plus_x, minus_x, "x")
        yield from gather_chain(group, 0, rows_z, nz, z, plus_z, minus_z, "z")

    live = []

    def spawn(rank, task):
        live.append([rank, len(started), task, []])

    def run():
        while live:
            best = None
            for entry in live:
                rank, _, _, wait = entry
                if callable(wait):
                    if not wait():
                        continue
                    ready = clock[0]
                else:
                    ready = max([clock[0]] + [due[id(copy)] for copy in wait])
                key = (max(ready, clock[0] + 0.2), rank)
                if best is None or key < best[0]:
                    best = (key, entry)
            entry = best[1]
            if not callable(entry[3]):
                arrive(entry[3])
            entry[3] = next(entry[2], None)
            if entry[3] is None:
                live.remove(entry)

    def group(rank, ways, first, post):
        left = [len(ways)]
        def chain(way, what):
            yield from way(what)
            left[0] -= 1
            if not left[0]:
                if not diag_done:
                    yield lambda: diag_done
                yield from post
        for at, way in enumerate(ways):
            pieces = 2 // len(ways)
            spawn(rank, chain(way, (first + at * pieces, pieces, 0, piece)))

    def to_b(p, extra=None):
        work(1.0)
        value = jnp.dot(na[...], slope[p], preferred_element_type=f32)
        if p < 2:
            part_b[p] = value
            return
        part_b[p, both:, :] = value[both:]
        value = value[:both]
        if extra is not None:
            value = value + decode(ry[extra])
        sy[p - 2] = encode(value)

    begun = []

    def to_a(first):
        fresh = not begun
        work(2.0)
        begun.append(first)
        pair = (first, first + 1)
        def body(i, sums):
            rows = pl.ds(pl.multiple_of(i * 256, 256), 256)
            acc = None if fresh else back_a[:, rows]
            for p in pair:
                term = lax.dot_general(
                    nb[p], slope[p, rows, :], (((1,), (1,)), ((), ())), preferred_element_type=f32)
                acc = term if acc is None else acc + term
            back_a[:, rows] = acc
            over, new = None, []
            for p, total_p in zip(pair, sums):
                sq = slope[p, rows, :].astype(f32)
                sq = sq * sq
                lanes = sum(sq[:, k * 128 : (k + 1) * 128] for k in range(piece // 128))
                over = lanes if over is None else over + lanes
                new.append(total_p + jnp.sum(sq, axis=0, keepdims=True))
            row_acc[rows, :] = over if fresh else row_acc[rows, :] + over
            return tuple(new)
        sums = lax.fori_loop(0, width // 256, body, (jnp.zeros((1, piece), f32),) * 2)
        for p, value in zip(pair, sums):
            square[p] = value

    def gain(base, extra):
        work(0.5)
        def body(i, _):
            rows = pl.ds(pl.multiple_of(i * 64, 64), 64)
            part_b[base, rows, :] += decode(ry[extra, rows, :])
            return 0
        lax.fori_loop(0, both // 64, body, 0)

    done, last_y = [], []

    def post(first):
        if first:
            copies = []
            if first == 6:
                yield lambda: "far" in done
            for p, peer, link in ((first, up, "y+"), (first + 1, down, "y-")):
                to_b(p, p - 4 if first == 6 else None)
                copies.append(send(sy.at[p - 2], ry.at[p - 2], peer, link))
            if first == 6:
                last_y.extend(copies)
            else:
                spawn(0, after_y(first, copies))
            yield []
        else:
            to_b(0)
            to_b(1)
            done.append("own")
        to_a(first)

    def after_y(first, copies):
        yield copies
        if first == 4:
            done.append("far")
            return
        yield lambda: "own" in done
        gain(1, 0)
        gain(0, 1)

    def blocks():
        yield first
        second = [send(nb.at[3, :both], nb.at[4, :both], up, "y+"), send(nb.at[2, :both], nb.at[5, :both], down, "y-")]
        third = [send(nb.at[1, :both], nb.at[7, :both], up, "y+"), send(nb.at[0, :both], nb.at[6, :both], down, "y-")]
        correlate(2)
        group(RANKS[1], WAYS[1], 2, post(2))
        yield second
        correlate(4)
        group(RANKS[2], WAYS[2], 4, post(4))
        yield third
        correlate(6)
        group(RANKS[3], WAYS[3], 6, post(6))

    WAYS = [[one_way], [one_way], [other_way], [one_way]]
    RANKS = [4, 3, 2, 1]

    for i in range(width // 128):
        cols = pl.ds(i * 128, 128)
        nat[cols, :] = jnp.transpose(na[:both, cols])
    work(2.0)
    correlate(0)
    group(RANKS[0], WAYS[0], 0, post(0))
    for entry in live:
        entry[3] = next(entry[2])
    spawn(0, blocks())
    spawn(2, diagonal())
    run()

    def code_a(i, _):
        rows = pl.ds(pl.multiple_of(i * 32, 32), 32)
        there = pl.ds(pl.multiple_of(i * 32 + frames, 32), 32)
        send_a[rows, :] = encode(back_a[there, :])
        return 0

    lax.fori_loop(0, frames // 32, code_a, 0)
    swap_back = send(send_a, recv_a, partner)

    scale = 1.0 / (2.0 * off_weight)
    corr_half = diag_f[c, 1, 0:1]
    loss_off = jnp.sum(sum(square[p] for p in range(count)), axis=1, keepdims=True)
    loss_diag = jnp.sum((1.0 - corr_half) ** 2, axis=1, keepdims=True)
    loss_row = jnp.broadcast_to(loss_off * (off_weight * scale * scale) + loss_diag, (1, half))
    for p in range(slots):
        block = extra_y.at[ny + p] if p else extra_y.at[m]
        left, right = PIECES.index((p, 0)), PIECES.index((p, 1))
        block[0:1, :piece] = part_b[left, both : both + 1, :]
        block[0:1, piece:] = part_b[right, both : both + 1, :]
        block[1:2, :piece] = square[left] * scale
        block[1:2, piece:] = square[right] * scale
        block[2:3, :] = loss_row
        block[3:4, :] = jnp.zeros((1, half), f32)
    share_y = [
        send(extra_y.at[ny + SLOT[k]], extra_y.at[m], peers_y[k - 1]) for k in range(1, ny)
    ]
    extra_a[c, 0:1, :] = back_a[both : both + 1, :]
    extra_a[c, 1:2, :] = jnp.sum(jnp.transpose(row_acc[...]), axis=0, keepdims=True) * scale
    share_a = send(extra_a.at[c], extra_a.at[c], partner)

    diag = jnp.concatenate([diag_f[0], diag_f[1]], axis=2)
    mean_a16, mean_own_b16 = diag[0, 0:1], diag[0, 1:2]
    corr_ii = diag[1, 0:1]
    cross_a, cross_b = diag[2, 0:1], diag[2, 1:2]
    slope_ii = (-2.0 * (1.0 - corr_ii)).astype(bf16).astype(f32)

    arrive([share_a])
    last_a = extra_a[0] + extra_a[1]
    mean_a = last_a[0:1] + mean_own_b16 * slope_ii
    inner_a = last_a[1:2] + cross_a * slope_ii
    arrive([swap_back])

    def finish_a(i, _):
        rows = pl.ds(pl.multiple_of(i * 32, 32), 32)
        wide = (a_ref[rows, :].astype(f32) - center_a) * inv_a
        back = back_a[rows, :] + decode(recv_a[rows, :]) + slope_ii * nb16[rows, :].astype(f32)
        ga_ref[rows, :] = (inv_a * (back - mean_a - wide * inner_a)).astype(bf16)
        return 0

    lax.fori_loop(0, frames // 32, finish_a, 0)

    arrive(share_y)
    extra_c[c] = sum(extra_y[i] for i in range(ny))
    share_c = send(extra_c.at[c], extra_c.at[c], partner)

    def add_last(base, store):
        for side, got in ((0, 4), (1, 5)):
            def body(i, _, side=side, got=got):
                rows = pl.ds(pl.multiple_of(base + i * 64, 64), 64)
                here = pl.ds(pl.multiple_of(i * 64, 64), 64)
                store(side, here, part_b[side, rows, :] + decode(ry[got, rows, :]))
                return 0
            lax.fori_loop(0, frames // 64, body, 0)

    def store_other(side, rows, value):
        sum_b[rows, side * piece : (side + 1) * piece] = encode(value)

    def store_own(side, rows, value):
        full_b[rows, piece_of(c, side)] = value

    arrive(last_y)
    add_last(frames, store_other)
    swap_sum = [send(sum_b, recv_b, partner)]
    add_last(0, store_own)

    arrive([share_c])
    mean_b = jnp.concatenate([extra_c[0, 0:1], extra_c[1, 0:1]], axis=1) + mean_a16 * slope_ii
    inner_b = jnp.concatenate([extra_c[0, 1:2], extra_c[1, 1:2]], axis=1) + cross_b * slope_ii
    loss_ref[...] = jnp.broadcast_to(extra_c[0, 2:3, :128] + extra_c[1, 2:3, :128], (8, 128))
    arrive(swap_sum)
    there_half = pl.ds(pl.multiple_of((1 - c) * half, 128), half)

    def take_b(i, _):
        rows = pl.ds(pl.multiple_of(i * 32, 32), 32)
        full_b[rows, there_half] = decode(recv_b[rows, :])
        return 0

    lax.fori_loop(0, frames // 32, take_b, 0)

    def finish_b(i, _):
        rows = pl.ds(pl.multiple_of(i * 32, 32), 32)
        wide = (b_ref[rows, :].astype(f32) - center_b) * inv_b
        back = full_b[rows, :] + slope_ii * na[rows, :].astype(f32)
        gb_ref[rows, :] = (inv_b * (back - mean_b - wide * inner_b)).astype(bf16)
        return 0

    lax.fori_loop(0, frames // 32, finish_b, 0)
    for copy in started:
        copy.wait_send()


def solution(mesh):
    ny = mesh.shape["mp"]
    members = mesh.shape["dp"]
    nx = ny
    nz = members // (2 * nx)

    def per_device(view_a, view_b):
        frames, width = view_a.shape
        both, half = 2 * frames, width // 2
        rows_x, rows_z, rows_o = width // nx, width // nz, width // (nx * nz)
        vmem = pltpu.VMEM
        rings = []
        count, piece = 2 * ny, half // 2
        scratch = [
            vmem((frames, width), bf16),
            vmem((both + 16, width), bf16),
            vmem((width, both), bf16),
            vmem((frames, width), bf16),
            vmem((2, frames, piece), bf16),
            vmem((count, both + 16, piece), bf16),
            vmem((count, width, piece), f32),
            vmem((count, width, piece), bf16),
            vmem((both + 16, width), f32),
            vmem((count, both + 16, piece), f32),
            vmem((frames, half), bf16),
            vmem((frames, width), f32),
            vmem((2, 2, 2, width), f32),
            vmem((nx, 2, 2, width), f32),
            vmem((nz, 2, 2, width), f32),
            vmem((2, 3, 2, width), f32),
            vmem((nx, 3, 2, half), f32),
            vmem((nz, 3, 2, half), f32),
            vmem((2, 3, 2, half), f32),
            vmem((ny, 1, half), f32),
            vmem((count, 1, piece), f32),
            vmem((2 * ny, 4, half), f32),
            vmem((2, 4, half), f32),
            vmem((2, 2, width), f32),
            vmem((width, 128), f32),
        ]
        for rows, n in ((rows_x + rows_o, nx), (rows_z + rows_o, nz)):
            ring = [vmem((count, rows, piece // 2), bf16)] * 2
            rings.append(ring + [vmem((n // 2 - 1, count, rows, piece), bf16)] * 2)
        scratch += rings[0] + rings[1] + rings[0] + rings[1] + [vmem((count - 2, both, piece), bf16)] * 2 + [
            vmem((frames, width), bf16),
            vmem((frames, width), bf16),
            vmem((frames, half), bf16),
            pltpu.SemaphoreType.DMA((256,)),
            pltpu.SemaphoreType.DMA((256,)),
        ]
        grad_a, grad_b, loss = pl.pallas_call(
            functools.partial(kernel, nx, nz, ny, float(frames * members)),
            out_shape=(
                jax.ShapeDtypeStruct((frames, width), bf16),
                jax.ShapeDtypeStruct((frames, width), bf16),
                jax.ShapeDtypeStruct((8, 128), f32),
            ),
            in_specs=[pl.BlockSpec(memory_space=vmem)] * 2,
            out_specs=[pl.BlockSpec(memory_space=vmem)] * 3,
            scratch_shapes=scratch,
            compiler_params=pltpu.CompilerParams(
                collective_id=0, has_side_effects=True, vmem_limit_bytes=56 * 1024 * 1024
            ),
            cost_estimate=pl.CostEstimate(
                flops=3 * 2 * both * width * half * ny, bytes_accessed=4 * frames * width * 2,
                transcendentals=0),
        )(view_a, view_b)
        return grad_a, grad_b, loss[0, 0]

    placed = P("dp", "mp")
    return jax.shard_map(
        per_device,
        mesh=mesh,
        in_specs=(placed, placed),
        out_specs=(placed, placed, P()),
        check_vma=False,
    )
```

```python
import functools

import jax
import jax.numpy as jnp
from jax import lax
from jax.experimental import pallas as pl
from jax.experimental.pallas import tpu as pltpu
from jax.sharding import PartitionSpec as P

epsilon = 1e-05
off_weight = 0.0051

MESH = pl.DeviceIdType.MESH
f32 = jnp.float32
bf16 = jnp.bfloat16

PIECES = ((0, 0), (0, 1), (1, 1), (2, 0), (3, 0), (3, 1), (1, 0), (2, 1))
SLOT = (0, 1, 3, 2)


tiny = 1e-37


def encode(v):
    return ((v * v) * (v * jnp.abs(v))).astype(bf16)


def decode(y):
    y = y.astype(f32)
    y = y * lax.rsqrt(jnp.maximum(jnp.abs(y), tiny))
    return y * lax.rsqrt(jnp.maximum(jnp.abs(y), tiny))


def kernel(
    nx, nz, ny, total,
    a_ref, b_ref, ga_ref, gb_ref, loss_ref,
    nb16, na, nat, nb, part, slope, back_a, part_b, sum_b, full_b,
    stat_c, stat_x, stat_z, diag_c, diag_x, diag_z, diag_f,
    mean_b16, square, extra_y, extra_c, extra_a, row_acc,
    rx_p1, rx_m1, rx_p2, rx_m2, rz_p1, rz_m1, rz_p2, rz_m2,
    sx_p1, sx_m1, sx_p2, sx_m2, sz_p1, sz_m1, sz_p2, sz_m2,
    sy, ry, recv_a,
    send_sems, recv_sems,
):
    frames, width = a_ref.shape
    both = 2 * frames
    half = width // 2
    slots, count, piece = ny, 2 * ny, half // 2
    dp = lax.axis_index("dp")
    m = lax.axis_index("mp")
    c = lax.rem(dp, 2)
    x = lax.rem(dp // 2, nx)
    z = dp // (2 * nx)

    def device(dc=0, dx=0, dz=0, dy=0):
        there = (lax.rem(z + dz, nz) * nx + lax.rem(x + dx, nx)) * 2
        there = there + (1 - c if dc else c)
        return (there, lax.rem(m + dy, ny))

    partner = device(dc=1)
    peers_x = [device(dx=k) for k in range(1, nx)]
    peers_z = [device(dz=k) for k in range(1, nz)]
    peers_y = [device(dy=k) for k in range(1, ny)]
    everyone = [partner] + peers_x + peers_z + peers_y

    barrier = pltpu.get_barrier_semaphore()
    for peer in everyone:
        pl.semaphore_signal(barrier, inc=1, device_id=peer, device_id_type=MESH)

    started, due, clock, free = [], {}, [0.0], {}

    def work(t):
        clock[0] += t

    def send(src, dst, peer, link=None):
        at = len(started)
        work(0.2)
        size = src.dtype.itemsize
        for d in src.shape:
            size *= d
        rate = 45e3 if link else 500e3
        begin = max(clock[0], free.get(link, 0.0)) if link else clock[0]
        end = begin + size / rate
        if link:
            free[link] = end
        copy = pltpu.make_async_remote_copy(
            src_ref=src,
            dst_ref=dst,
            send_sem=send_sems.at[at],
            recv_sem=recv_sems.at[at],
            device_id=peer,
            device_id_type=MESH,
        )
        copy.start()
        started.append(copy)
        due[id(copy)] = end + 1.5
        return copy

    def arrive(copies):
        for copy in copies:
            clock[0] = max(clock[0], due[id(copy)])
            copy.wait_recv()

    def spread_to(buf, mine, peers):
        return [send(buf.at[mine], buf.at[mine], peer) for peer in peers]

    def column_sum(fn):
        step = 64
        def body(i, acc):
            return acc + jnp.sum(fn(pl.ds(i * step, step)), axis=0, keepdims=True)
        return lax.fori_loop(0, frames // step, body, jnp.zeros((1, width), f32))

    for view, ref in enumerate((a_ref, b_ref)):
        center = column_sum(lambda rows: ref[rows, :].astype(f32)) / frames
        def deviation(rows, ref=ref, center=center):
            dev = ref[rows, :].astype(f32) - center
            return dev * dev
        stat_c[c, 0, view : view + 1, :] = center
        stat_c[c, 1, view : view + 1, :] = column_sum(deviation)

    pl.semaphore_wait(barrier, len(everyone))
    work(5.0)

    def merge(buf, members, count):
        center = sum(buf[i, 0] for i in range(members)) * (1.0 / members)
        spread = sum(buf[i, 1] for i in range(members))
        shift = sum((buf[i, 0] - center) ** 2 for i in range(members))
        return center, spread + count * shift

    arrive(spread_to(stat_c, c, [partner]))
    stat_x[x, 0], stat_x[x, 1] = merge(stat_c, 2, float(frames))
    arrive(spread_to(stat_x, x, peers_x))
    stat_z[z, 0], stat_z[z, 1] = merge(stat_x, nx, float(frames * 2))
    arrive(spread_to(stat_z, z, peers_z))
    center, spread = merge(stat_z, nz, float(frames * 2 * nx))
    inv = lax.rsqrt(spread / total + epsilon)
    center_a, center_b = center[0:1], center[1:2]
    inv_a, inv_b = inv[0:1], inv[1:2]

    own, other = pl.ds(0, frames), pl.ds(frames, frames)
    own_half = pl.ds(pl.multiple_of(c * half, 128), half)
    other_half = pl.ds(pl.multiple_of((1 - c) * half, 128), half)

    def standardize(src, dst, center, inv):
        def body(i, _):
            rows = pl.ds(pl.multiple_of(i * 32, 32), 32)
            dst[rows, :] = ((src[rows, :].astype(f32) - center) * inv).astype(bf16)
            return 0
        lax.fori_loop(0, frames // 32, body, 0)

    standardize(b_ref, nb16, center_b, inv_b)
    swap_b = [
        send(
            nb16.at[:, pl.ds(pl.multiple_of((1 - c) * half + side * piece, 128), piece)],
            nb.at[side, other], partner)
        for side in range(2)
    ]
    for side in range(2):
        nb[side, own, :] = nb16[:, pl.ds(pl.multiple_of(c * half + side * piece, 128), piece)]
    up, down = device(dy=1), device(dy=ny - 1)
    first = [send(nb.at[0, own], nb.at[3, own], up, "y+"), send(nb.at[1, own], nb.at[2, own], down, "y-")]
    standardize(a_ref, na, center_a, inv_a)
    swap_a = send(na.at[own], na.at[other], partner)
    arrive(swap_b)
    first.append(send(nb.at[0, other], nb.at[3, other], up, "y+"))
    first.append(send(nb.at[1, other], nb.at[2, other], down, "y-"))

    diag_done = []

    def diagonal():
        def body(i, acc):
            rows = pl.ds(pl.multiple_of(i * 32, 32), 32)
            wide_a = (a_ref[rows, :].astype(f32) - center_a) * inv_a
            wide_b = (b_ref[rows, :].astype(f32) - center_b) * inv_b
            short_a, short_b = na[rows, :].astype(f32), nb16[rows, :].astype(f32)
            terms = (short_a, short_b, short_a * short_b, wide_a * short_b, wide_b * short_a)
            return tuple(s + jnp.sum(t, axis=0, keepdims=True) for s, t in zip(acc, terms))
        sums = lax.fori_loop(0, frames // 32, body, (jnp.zeros((1, width), f32),) * 5)
        for at, value in enumerate(sums[:3] + (jnp.zeros((1, width), f32),) + sums[3:]):
            diag_c[c, at // 2, at % 2 : at % 2 + 1, :] = value
        work(1.5)
        copies = spread_to(diag_c, c, [partner])
        yield copies
        diag_x[x] = jnp.where(
            c == 0, diag_c[0, :, :, :half] + diag_c[1, :, :, :half],
            diag_c[0, :, :, half:] + diag_c[1, :, :, half:])
        copies = spread_to(diag_x, x, peers_x)
        yield copies
        diag_z[z] = sum(diag_x[i] for i in range(nx))
        copies = spread_to(diag_z, z, peers_z)
        yield copies
        diag_f[c] = sum(diag_z[i] for i in range(nz)) / total
        mean_b16[0] = diag_f[c, 0, 1:2]
        copies = spread_to(diag_f, c, [partner])
        copies += [send(mean_b16.at[0], mean_b16.at[SLOT[ny - k]], peers_y[k - 1]) for k in range(1, ny)]
        yield copies
        mean_a = jnp.concatenate([diag_f[0, 0, 0:1], diag_f[1, 0, 0:1]], axis=1)
        na[pl.ds(both, 16), :] = jnp.broadcast_to(mean_a, (16, width)).astype(bf16)
        for p, (slot, side) in enumerate(PIECES):
            mean_b = mean_b16[slot, :, side * piece : (side + 1) * piece]
            nb[p, pl.ds(both, 16), :] = jnp.broadcast_to(mean_b, (16, piece)).astype(bf16)
        diag_done.append(True)

    def correlate(first):
        work(1.5)
        def body(i, _):
            rows = pl.ds(pl.multiple_of(i * 256, 256), 256)
            for p in (first, first + 1):
                part[p, rows, :] = jnp.dot(nat[rows, :], nb[p, :both, :], preferred_element_type=f32)
            return 0
        lax.fori_loop(0, width // 256, body, 0)

    def sweep(group, rows, fn):
        first, count, _, columns = group
        work(0.004 * rows * count * columns / 1024)
        step = min(rows, 32)
        turns = count * (rows // step)
        per = min(turns, max(1, 16384 // (step * columns)))
        def body(i, _):
            stores = []
            for u in range(per):
                k = i * per + u
                p = first + k // (rows // step)
                r = k % (rows // step) * step if isinstance(k, int) else lax.rem(k, rows // step) * step
                stores += fn(p, r, step)
            for ref, at, value in stores:
                ref[at] = value
            return 0
        if turns == per:
            body(0, 0)
        else:
            lax.fori_loop(0, turns // per, body, 0)

    def strip(base, step):
        return pl.ds(base if isinstance(base, int) else pl.multiple_of(base, 16), step)

    def reduce_chain(group, base, rows, n, at, plus, minus, axis, off, bufs):
        out_p1, out_m1, out_p2, out_m2, in_p1, in_m1, in_p2, in_m2 = bufs
        far = n // 2
        first, count, column, columns = group
        some, window, every = pl.ds(first, count), pl.ds(off, rows), pl.ds(column, columns)
        left, right = pl.ds(column, columns // 2), pl.ds(column + columns // 2, columns // 2)
        short = pl.ds(column // 2, columns // 2)

        def pack(s, source, cols, out1, out2, in1, in2):
            rest = right if cols is left else left
            def fn(p, r, step):
                there = strip(source + r, step)
                here = strip(off + r, step)
                if s == 1:
                    return [(out1, (p, here, short), encode(part[p, there, cols]))]
                if s > 2:
                    value = encode(part[p, there, every] + decode(in2[s - 3, p, here, every]))
                    return [(out2, (s - 2, p, here, every), value)]
                value = encode(part[p, there, cols] + decode(in1[p, here, short]))
                return [
                    (out2, (0, p, here, cols), value),
                    (out2, (0, p, here, rest), encode(part[p, there, rest])),
                ]
            return fn

        for s in range(1, far + 1):
            distance = far + 1 - s
            go_p = pack(s, base + lax.rem(at + distance, n) * rows, left, out_p1, out_p2, in_p1, in_p2)
            go_m = pack(s, base + lax.rem(at + n - distance, n) * rows, right, out_m1, out_m2, in_m1, in_m2)
            sweep(group, rows, lambda p, r, step: go_p(p, r, step) + go_m(p, r, step))
            def view(ref1, ref2):
                return ref1.at[some, window, short] if s == 1 else ref2.at[s - 2, some, window, every]
            go = [
                send(view(out_p1, out_p2), view(in_p1, in_p2), plus, axis + "+"),
                send(view(out_m1, out_m2), view(in_m1, in_m2), minus, axis + "-"),
            ]
            yield go

        def finish(p, r, step):
            there = strip(base + at * rows + r, step)
            here = strip(off + r, step)
            value = part[p, there, every] + decode(in_p2[far - 2, p, here, every])
            return [(part, (p, there, every), value + decode(in_m2[far - 2, p, here, every]))]
        sweep(group, rows, finish)

    def gather_chain(group, base, rows, n, at, plus, minus, axis):
        far = n // 2
        first, count, column, columns = group
        some, every = pl.ds(first, count), pl.ds(column, columns)
        left, right = pl.ds(column, columns // 2), pl.ds(column + columns // 2, columns // 2)
        for s in range(1, far + 1):
            cols_p, cols_m = (left, right) if s == far else (every, every)
            from_p = base + lax.rem(at + n - (s - 1), n) * rows
            from_m = base + lax.rem(at + (s - 1), n) * rows
            ref_p = slope.at[some, strip(from_p, rows), cols_p]
            ref_m = slope.at[some, strip(from_m, rows), cols_m]
            yield [send(ref_p, ref_p, plus, axis + "+"), send(ref_m, ref_m, minus, axis + "-")]

    plus_x, minus_x = device(dx=1), device(dx=nx - 1)
    plus_z, minus_z = device(dz=1), device(dz=nz - 1)
    rows_x, rows_z, rows_o = width // nx, width // nz, width // (nx * nz)
    base_x = x * rows_x
    base_z = z * rows_z
    bufs_x = (sx_p1, sx_m1, sx_p2, sx_m2, rx_p1, rx_m1, rx_p2, rx_m2)
    bufs_z = (sz_p1, sz_m1, sz_p2, sz_m2, rz_p1, rz_m1, rz_p2, rz_m2)

    def slopes(group, base):
        first, count, column, columns = group
        rows, cols = strip(base, rows_o), pl.ds(column, columns)
        row_ids = lax.broadcasted_iota(jnp.int32, (rows_o, columns), 0) + base
        col_ids = lax.broadcasted_iota(jnp.int32, (rows_o, columns), 1) + (c * half + column)
        for p in range(first, first + count):
            value = 2.0 * off_weight * (part[p, rows, cols] / total)
            if p < 2:
                value = jnp.where(row_ids == col_ids + p * piece, 0.0, value)
            slope[p, rows, cols] = value.astype(bf16)

    def one_way(group):
        yield from reduce_chain(group, 0, rows_x, nx, x, plus_x, minus_x, "x", 0, bufs_x)
        yield from reduce_chain(group, base_x, rows_o, nz, z, plus_z, minus_z, "z", rows_z, bufs_z)
        slopes(group, base_x + z * rows_o)
        yield from gather_chain(group, base_x, rows_o, nz, z, plus_z, minus_z, "z")
        yield from gather_chain(group, 0, rows_x, nx, x, plus_x, minus_x, "x")

    def other_way(group):
        yield from reduce_chain(group, 0, rows_z, nz, z, plus_z, minus_z, "z", 0, bufs_z)
        yield from reduce_chain(group, base_z, rows_o, nx, x, plus_x, minus_x, "x", rows_x, bufs_x)
        slopes(group, base_z + x * rows_o)
        yield from gather_chain(group, base_z, rows_o, nx, x, plus_x, minus_x, "x")
        yield from gather_chain(group, 0, rows_z, nz, z, plus_z, minus_z, "z")

    live = []

    def spawn(rank, task):
        live.append([rank, len(started), task, []])

    def run():
        while live:
            best = None
            for entry in live:
                rank, _, _, wait = entry
                if callable(wait):
                    if not wait():
                        continue
                    ready = clock[0]
                else:
                    ready = max([clock[0]] + [due[id(copy)] for copy in wait])
                key = (max(ready, clock[0] + 0.2), rank)
                if best is None or key < best[0]:
                    best = (key, entry)
            entry = best[1]
            if not callable(entry[3]):
                arrive(entry[3])
            entry[3] = next(entry[2], None)
            if entry[3] is None:
                live.remove(entry)

    def group(rank, ways, first, post):
        left = [len(ways)]
        def chain(way, what):
            yield from way(what)
            left[0] -= 1
            if not left[0]:
                yield lambda: diag_done
                yield from post
        for at, way in enumerate(ways):
            pieces = 2 // len(ways)
            spawn(rank, chain(way, (first + at * pieces, pieces, 0, piece)))

    def to_b(p):
        work(0.75)
        part_b[p] = jnp.dot(na[...], slope[p], preferred_element_type=f32)

    begun = []

    def to_a(first):
        fresh = not begun
        work(2.0)
        begun.append(first)
        def body(i, _):
            rows = pl.ds(pl.multiple_of(i * 256, 256), 256)
            acc = None if fresh else back_a[:, rows]
            for p in (first, first + 1):
                term = lax.dot_general(
                    nb[p], slope[p, rows, :], (((1,), (1,)), ((), ())), preferred_element_type=f32)
                acc = term if acc is None else acc + term
            back_a[:, rows] = acc
            return 0
        lax.fori_loop(0, width // 256, body, 0)

    def squares(first):
        work(0.6)
        for p in (first, first + 1):
            def body(i, acc, p=p):
                rows = pl.ds(pl.multiple_of(i * 64, 64), 64)
                s = slope[p, rows, :].astype(f32)
                s = s * s
                row_acc[rows, :] += sum(s[:, k * 128 : (k + 1) * 128] for k in range(piece // 128))
                return acc + jnp.sum(s, axis=0, keepdims=True)
            square[p] = lax.fori_loop(0, width // 64, body, jnp.zeros((1, piece), f32))

    def code(out, base, extra):
        work(0.5)
        def body(i, _):
            rows = pl.ds(pl.multiple_of(i * 64, 64), 64)
            value = part_b[base, rows, :]
            if extra is not None:
                value = value + decode(ry[extra, rows, :])
            sy[out, rows, :] = encode(value)
            return 0
        lax.fori_loop(0, both // 64, body, 0)

    def gain(base, extra):
        work(0.5)
        def body(i, _):
            rows = pl.ds(pl.multiple_of(i * 64, 64), 64)
            part_b[base, rows, :] += decode(ry[extra, rows, :])
            return 0
        lax.fori_loop(0, both // 64, body, 0)

    done, last_y = [], []

    def post(first):
        if first:
            copies = []
            if first == 6:
                yield lambda: "far" in done
            for p, peer, link in ((first, up, "y+"), (first + 1, down, "y-")):
                to_b(p)
                code(p - 2, p, p - 4 if first == 6 else None)
                copies.append(send(sy.at[p - 2], ry.at[p - 2], peer, link))
            if first == 6:
                last_y.extend(copies)
            else:
                spawn(0, after_y(first, copies))
            yield []
        else:
            to_b(0)
            to_b(1)
            done.append("own")
        to_a(first)
        squares(first)

    def after_y(first, copies):
        yield copies
        if first == 4:
            done.append("far")
            return
        yield lambda: "own" in done
        gain(1, 0)
        gain(0, 1)

    def blocks():
        yield first
        second = [send(nb.at[3, :both], nb.at[4, :both], up, "y+"), send(nb.at[2, :both], nb.at[5, :both], down, "y-")]
        third = [send(nb.at[1, :both], nb.at[7, :both], up, "y+"), send(nb.at[0, :both], nb.at[6, :both], down, "y-")]
        correlate(2)
        group(RANKS[1], WAYS[1], 2, post(2))
        yield second
        correlate(4)
        group(RANKS[2], WAYS[2], 4, post(4))
        yield third
        correlate(6)
        group(RANKS[3], WAYS[3], 6, post(6))

    WAYS = [[one_way], [one_way], [other_way], [one_way]]
    RANKS = [4, 3, 2, 1]

    row_acc[...] = jnp.zeros_like(row_acc)
    arrive([swap_a])
    for i in range(width // 128):
        cols = pl.ds(i * 128, 128)
        nat[cols, :] = jnp.transpose(na[:both, cols].astype(f32)).astype(bf16)
    work(2.0)
    correlate(0)
    group(RANKS[0], WAYS[0], 0, post(0))
    for entry in live:
        entry[3] = next(entry[2])
    spawn(0, blocks())
    spawn(2, diagonal())
    run()

    swap_back = send(back_a.at[other, :], recv_a, partner)

    scale = 1.0 / (2.0 * off_weight)
    corr_half = diag_f[c, 1, 0:1]
    loss_off = jnp.sum(sum(square[p] for p in range(count)), axis=1, keepdims=True)
    loss_diag = jnp.sum((1.0 - corr_half) ** 2, axis=1, keepdims=True)
    loss_row = jnp.broadcast_to(loss_off * (off_weight * scale * scale) + loss_diag, (1, half))
    for p in range(slots):
        block = extra_y.at[ny + p] if p else extra_y.at[m]
        left, right = PIECES.index((p, 0)), PIECES.index((p, 1))
        block[0:1, :piece] = part_b[left, both : both + 1, :]
        block[0:1, piece:] = part_b[right, both : both + 1, :]
        block[1:2, :piece] = square[left] * scale
        block[1:2, piece:] = square[right] * scale
        block[2:3, :] = loss_row
        block[3:4, :] = jnp.zeros((1, half), f32)
    share_y = [
        send(extra_y.at[ny + SLOT[k]], extra_y.at[m], peers_y[k - 1]) for k in range(1, ny)
    ]
    extra_a[c, 0:1, :] = back_a[both : both + 1, :]
    extra_a[c, 1:2, :] = jnp.sum(jnp.transpose(row_acc[...]), axis=0, keepdims=True) * scale
    share_a = send(extra_a.at[c], extra_a.at[c], partner)

    diag = jnp.concatenate([diag_f[0], diag_f[1]], axis=2)
    mean_a16, mean_own_b16 = diag[0, 0:1], diag[0, 1:2]
    corr_ii = diag[1, 0:1]
    cross_a, cross_b = diag[2, 0:1], diag[2, 1:2]
    slope_ii = (-2.0 * (1.0 - corr_ii)).astype(bf16).astype(f32)

    arrive([share_a])
    last_a = extra_a[0] + extra_a[1]
    mean_a = last_a[0:1] + mean_own_b16 * slope_ii
    inner_a = last_a[1:2] + cross_a * slope_ii
    arrive([swap_back])

    def finish_a(i, _):
        rows = pl.ds(pl.multiple_of(i * 32, 32), 32)
        wide = (a_ref[rows, :].astype(f32) - center_a) * inv_a
        back = back_a[rows, :] + recv_a[rows, :] + slope_ii * nb16[rows, :].astype(f32)
        ga_ref[rows, :] = (inv_a * (back - mean_a - wide * inner_a)).astype(bf16)
        return 0

    lax.fori_loop(0, frames // 32, finish_a, 0)

    arrive(share_y)
    extra_c[c] = sum(extra_y[i] for i in range(ny))
    share_c = send(extra_c.at[c], extra_c.at[c], partner)

    def add_last(base, dst, at):
        for side, got in ((0, 4), (1, 5)):
            cols = pl.ds(at if isinstance(at, int) else pl.multiple_of(at + side * piece, 128), piece)
            if isinstance(at, int):
                cols = pl.ds(side * piece, piece)
            def body(i, _, side=side, got=got, cols=cols):
                rows = pl.ds(pl.multiple_of(base + i * 64, 64), 64)
                here = pl.ds(pl.multiple_of(i * 64, 64), 64)
                dst[here, cols] = part_b[side, rows, :] + decode(ry[got, rows, :])
                return 0
            lax.fori_loop(0, frames // 64, body, 0)

    arrive(last_y)
    add_last(frames, sum_b, 0)
    swap_sum = [send(sum_b, full_b.at[:, own_half], partner)]
    add_last(0, full_b, c * half)

    arrive([share_c])
    mean_b = jnp.concatenate([extra_c[0, 0:1], extra_c[1, 0:1]], axis=1) + mean_a16 * slope_ii
    inner_b = jnp.concatenate([extra_c[0, 1:2], extra_c[1, 1:2]], axis=1) + cross_b * slope_ii
    loss_ref[...] = jnp.broadcast_to(extra_c[0, 2:3, :128] + extra_c[1, 2:3, :128], (8, 128))
    arrive(swap_sum)

    def finish_b(i, _):
        rows = pl.ds(pl.multiple_of(i * 32, 32), 32)
        wide = (b_ref[rows, :].astype(f32) - center_b) * inv_b
        back = full_b[rows, :] + slope_ii * na[rows, :].astype(f32)
        gb_ref[rows, :] = (inv_b * (back - mean_b - wide * inner_b)).astype(bf16)
        return 0

    lax.fori_loop(0, frames // 32, finish_b, 0)
    for copy in started:
        copy.wait_send()


def solution(mesh):
    ny = mesh.shape["mp"]
    members = mesh.shape["dp"]
    nx = ny
    nz = members // (2 * nx)

    def per_device(view_a, view_b):
        frames, width = view_a.shape
        both, half = 2 * frames, width // 2
        rows_x, rows_z, rows_o = width // nx, width // nz, width // (nx * nz)
        vmem = pltpu.VMEM
        rings = []
        count, piece = 2 * ny, half // 2
        scratch = [
            vmem((frames, width), bf16),
            vmem((both + 16, width), bf16),
            vmem((width, both), bf16),
            vmem((count, both + 16, piece), bf16),
            vmem((count, width, piece), f32),
            vmem((count, width, piece), bf16),
            vmem((both + 16, width), f32),
            vmem((count, both + 16, piece), f32),
            vmem((frames, half), f32),
            vmem((frames, width), f32),
            vmem((2, 2, 2, width), f32),
            vmem((nx, 2, 2, width), f32),
            vmem((nz, 2, 2, width), f32),
            vmem((2, 3, 2, width), f32),
            vmem((nx, 3, 2, half), f32),
            vmem((nz, 3, 2, half), f32),
            vmem((2, 3, 2, half), f32),
            vmem((ny, 1, half), f32),
            vmem((count, 1, piece), f32),
            vmem((2 * ny, 4, half), f32),
            vmem((2, 4, half), f32),
            vmem((2, 2, width), f32),
            vmem((width, 128), f32),
        ]
        for rows, n in ((rows_x + rows_o, nx), (rows_z + rows_o, nz)):
            ring = [vmem((count, rows, piece // 2), bf16)] * 2
            rings.append(ring + [vmem((n // 2 - 1, count, rows, piece), bf16)] * 2)
        scratch += rings[0] + rings[1] + rings[0] + rings[1] + [vmem((count - 2, both, piece), bf16)] * 2 + [
            vmem((frames, width), f32),
            pltpu.SemaphoreType.DMA((256,)),
            pltpu.SemaphoreType.DMA((256,)),
        ]
        grad_a, grad_b, loss = pl.pallas_call(
            functools.partial(kernel, nx, nz, ny, float(frames * members)),
            out_shape=(
                jax.ShapeDtypeStruct((frames, width), bf16),
                jax.ShapeDtypeStruct((frames, width), bf16),
                jax.ShapeDtypeStruct((8, 128), f32),
            ),
            in_specs=[pl.BlockSpec(memory_space=vmem)] * 2,
            out_specs=[pl.BlockSpec(memory_space=vmem)] * 3,
            scratch_shapes=scratch,
            compiler_params=pltpu.CompilerParams(
                collective_id=0, has_side_effects=True, vmem_limit_bytes=56 * 1024 * 1024
            ),
            cost_estimate=pl.CostEstimate(
                flops=3 * 2 * both * width * half * ny, bytes_accessed=4 * frames * width * 2,
                transcendentals=0),
        )(view_a, view_b)
        return grad_a, grad_b, loss[0, 0]

    placed = P("dp", "mp")
    return jax.shard_map(
        per_device,
        mesh=mesh,
        in_specs=(placed, placed),
        out_specs=(placed, placed, P()),
        check_vma=False,
    )
```

```python
import functools

import jax
import jax.numpy as jnp
from jax import lax
from jax.experimental import pallas as pl
from jax.experimental.pallas import tpu as pltpu
from jax.sharding import PartitionSpec as P

epsilon = 1e-05
off_weight = 0.0051

MESH = pl.DeviceIdType.MESH
f32 = jnp.float32
bf16 = jnp.bfloat16

PIECES = ((0, 0), (0, 1), (1, 1), (2, 0), (3, 0), (3, 1), (1, 0), (2, 1))
SLOT = (0, 1, 3, 2)


tiny = 1e-37


def encode(v):
    return ((v * v) * (v * jnp.abs(v))).astype(bf16)


def decode(y):
    y = y.astype(f32)
    y = y * lax.rsqrt(jnp.maximum(jnp.abs(y), tiny))
    return y * lax.rsqrt(jnp.maximum(jnp.abs(y), tiny))


def kernel(
    nx, nz, ny, total,
    a_ref, b_ref, ga_ref, gb_ref, loss_ref,
    nb16, na, nat, nb, part, slope, back_a, part_b, sum_b, full_b,
    stat_c, stat_x, stat_z, diag_c, diag_x, diag_z, diag_f,
    mean_b16, square, extra_y, extra_c, extra_a, row_acc,
    rx_p1, rx_m1, rx_p2, rx_m2, rz_p1, rz_m1, rz_p2, rz_m2,
    sx_p1, sx_m1, sx_p2, sx_m2, sz_p1, sz_m1, sz_p2, sz_m2,
    sy, ry, recv_a,
    send_sems, recv_sems,
):
    frames, width = a_ref.shape
    both = 2 * frames
    half = width // 2
    slots, count, piece = ny, 2 * ny, half // 2
    dp = lax.axis_index("dp")
    m = lax.axis_index("mp")
    c = lax.rem(dp, 2)
    x = lax.rem(dp // 2, nx)
    z = dp // (2 * nx)

    def device(dc=0, dx=0, dz=0, dy=0):
        there = (lax.rem(z + dz, nz) * nx + lax.rem(x + dx, nx)) * 2
        there = there + (1 - c if dc else c)
        return (there, lax.rem(m + dy, ny))

    partner = device(dc=1)
    peers_x = [device(dx=k) for k in range(1, nx)]
    peers_z = [device(dz=k) for k in range(1, nz)]
    peers_y = [device(dy=k) for k in range(1, ny)]
    everyone = [partner] + peers_x + peers_z + peers_y

    barrier = pltpu.get_barrier_semaphore()
    for peer in everyone:
        pl.semaphore_signal(barrier, inc=1, device_id=peer, device_id_type=MESH)

    started, due, clock, free = [], {}, [0.0], {}

    def work(t):
        clock[0] += t

    def send(src, dst, peer, link=None):
        at = len(started)
        work(0.2)
        size = src.dtype.itemsize
        for d in src.shape:
            size *= d
        rate = 45e3 if link else 500e3
        begin = max(clock[0], free.get(link, 0.0)) if link else clock[0]
        end = begin + size / rate
        if link:
            free[link] = end
        copy = pltpu.make_async_remote_copy(
            src_ref=src,
            dst_ref=dst,
            send_sem=send_sems.at[at],
            recv_sem=recv_sems.at[at],
            device_id=peer,
            device_id_type=MESH,
        )
        copy.start()
        started.append(copy)
        due[id(copy)] = end + 1.5
        return copy

    def arrive(copies):
        for copy in copies:
            clock[0] = max(clock[0], due[id(copy)])
            copy.wait_recv()

    def spread_to(buf, mine, peers):
        return [send(buf.at[mine], buf.at[mine], peer) for peer in peers]

    def column_sum(fn):
        step = 64
        def body(i, acc):
            return acc + jnp.sum(fn(pl.ds(i * step, step)), axis=0, keepdims=True)
        return lax.fori_loop(0, frames // step, body, jnp.zeros((1, width), f32))

    for view, ref in enumerate((a_ref, b_ref)):
        center = column_sum(lambda rows: ref[rows, :].astype(f32)) / frames
        def deviation(rows, ref=ref, center=center):
            dev = ref[rows, :].astype(f32) - center
            return dev * dev
        stat_c[c, 0, view : view + 1, :] = center
        stat_c[c, 1, view : view + 1, :] = column_sum(deviation)

    pl.semaphore_wait(barrier, len(everyone))
    work(5.0)

    def merge(buf, members, count):
        center = sum(buf[i, 0] for i in range(members)) * (1.0 / members)
        spread = sum(buf[i, 1] for i in range(members))
        shift = sum((buf[i, 0] - center) ** 2 for i in range(members))
        return center, spread + count * shift

    arrive(spread_to(stat_c, c, [partner]))
    stat_x[x, 0], stat_x[x, 1] = merge(stat_c, 2, float(frames))
    arrive(spread_to(stat_x, x, peers_x))
    stat_z[z, 0], stat_z[z, 1] = merge(stat_x, nx, float(frames * 2))
    arrive(spread_to(stat_z, z, peers_z))
    center, spread = merge(stat_z, nz, float(frames * 2 * nx))
    inv = lax.rsqrt(spread / total + epsilon)
    center_a, center_b = center[0:1], center[1:2]
    inv_a, inv_b = inv[0:1], inv[1:2]

    own, other = pl.ds(0, frames), pl.ds(frames, frames)
    own_half = pl.ds(pl.multiple_of(c * half, 128), half)
    other_half = pl.ds(pl.multiple_of((1 - c) * half, 128), half)

    def standardize(src, dst, center, inv):
        def body(i, _):
            rows = pl.ds(pl.multiple_of(i * 32, 32), 32)
            dst[rows, :] = ((src[rows, :].astype(f32) - center) * inv).astype(bf16)
            return 0
        lax.fori_loop(0, frames // 32, body, 0)

    standardize(b_ref, nb16, center_b, inv_b)
    swap_b = [
        send(
            nb16.at[:, pl.ds(pl.multiple_of((1 - c) * half + side * piece, 128), piece)],
            nb.at[side, other], partner)
        for side in range(2)
    ]
    for side in range(2):
        nb[side, own, :] = nb16[:, pl.ds(pl.multiple_of(c * half + side * piece, 128), piece)]
    up, down = device(dy=1), device(dy=ny - 1)
    first = [send(nb.at[0, own], nb.at[3, own], up, "y+"), send(nb.at[1, own], nb.at[2, own], down, "y-")]
    standardize(a_ref, na, center_a, inv_a)
    swap_a = send(na.at[own], na.at[other], partner)
    arrive(swap_b)
    first.append(send(nb.at[0, other], nb.at[3, other], up, "y+"))
    first.append(send(nb.at[1, other], nb.at[2, other], down, "y-"))

    diag_done = []

    def diagonal():
        def body(i, acc):
            rows = pl.ds(pl.multiple_of(i * 32, 32), 32)
            wide_a = (a_ref[rows, :].astype(f32) - center_a) * inv_a
            wide_b = (b_ref[rows, :].astype(f32) - center_b) * inv_b
            short_a, short_b = na[rows, :].astype(f32), nb16[rows, :].astype(f32)
            terms = (short_a, short_b, short_a * short_b, wide_a * short_b, wide_b * short_a)
            return tuple(s + jnp.sum(t, axis=0, keepdims=True) for s, t in zip(acc, terms))
        sums = lax.fori_loop(0, frames // 32, body, (jnp.zeros((1, width), f32),) * 5)
        for at, value in enumerate(sums[:3] + (jnp.zeros((1, width), f32),) + sums[3:]):
            diag_c[c, at // 2, at % 2 : at % 2 + 1, :] = value
        work(1.5)
        copies = spread_to(diag_c, c, [partner])
        yield copies
        diag_x[x] = jnp.where(
            c == 0, diag_c[0, :, :, :half] + diag_c[1, :, :, :half],
            diag_c[0, :, :, half:] + diag_c[1, :, :, half:])
        copies = spread_to(diag_x, x, peers_x)
        yield copies
        diag_z[z] = sum(diag_x[i] for i in range(nx))
        copies = spread_to(diag_z, z, peers_z)
        yield copies
        diag_f[c] = sum(diag_z[i] for i in range(nz)) / total
        mean_b16[0] = diag_f[c, 0, 1:2]
        copies = spread_to(diag_f, c, [partner])
        copies += [send(mean_b16.at[0], mean_b16.at[SLOT[ny - k]], peers_y[k - 1]) for k in range(1, ny)]
        yield copies
        mean_a = jnp.concatenate([diag_f[0, 0, 0:1], diag_f[1, 0, 0:1]], axis=1)
        na[pl.ds(both, 16), :] = jnp.broadcast_to(mean_a, (16, width)).astype(bf16)
        for p, (slot, side) in enumerate(PIECES):
            mean_b = mean_b16[slot, :, side * piece : (side + 1) * piece]
            nb[p, pl.ds(both, 16), :] = jnp.broadcast_to(mean_b, (16, piece)).astype(bf16)
        diag_done.append(True)

    def correlate(first):
        work(1.5)
        def body(i, _):
            rows = pl.ds(pl.multiple_of(i * 256, 256), 256)
            for p in (first, first + 1):
                part[p, rows, :] = jnp.dot(nat[rows, :], nb[p, :both, :], preferred_element_type=f32)
            return 0
        lax.fori_loop(0, width // 256, body, 0)

    def sweep(group, rows, fn):
        first, count, _, columns = group
        work(0.004 * rows * count * columns / 1024)
        step = min(rows, 32)
        turns = count * (rows // step)
        per = min(turns, max(1, 16384 // (step * columns)))
        def body(i, _):
            stores = []
            for u in range(per):
                k = i * per + u
                p = first + k // (rows // step)
                r = k % (rows // step) * step if isinstance(k, int) else lax.rem(k, rows // step) * step
                stores += fn(p, r, step)
            for ref, at, value in stores:
                ref[at] = value
            return 0
        if turns == per:
            body(0, 0)
        else:
            lax.fori_loop(0, turns // per, body, 0)

    def strip(base, step):
        return pl.ds(base if isinstance(base, int) else pl.multiple_of(base, 16), step)

    def reduce_chain(group, base, rows, n, at, plus, minus, axis, off, bufs):
        out_p1, out_m1, out_p2, out_m2, in_p1, in_m1, in_p2, in_m2 = bufs
        far = n // 2
        first, count, column, columns = group
        some, window, every = pl.ds(first, count), pl.ds(off, rows), pl.ds(column, columns)
        left, right = pl.ds(column, columns // 2), pl.ds(column + columns // 2, columns // 2)
        short = pl.ds(column // 2, columns // 2)

        def pack(s, source, cols, out1, out2, in1, in2):
            rest = right if cols is left else left
            def fn(p, r, step):
                there = strip(source + r, step)
                here = strip(off + r, step)
                if s == 1:
                    return [(out1, (p, here, short), encode(part[p, there, cols]))]
                if s > 2:
                    value = encode(part[p, there, every] + decode(in2[s - 3, p, here, every]))
                    return [(out2, (s - 2, p, here, every), value)]
                value = encode(part[p, there, cols] + decode(in1[p, here, short]))
                return [
                    (out2, (0, p, here, cols), value),
                    (out2, (0, p, here, rest), encode(part[p, there, rest])),
                ]
            return fn

        for s in range(1, far + 1):
            distance = far + 1 - s
            go_p = pack(s, base + lax.rem(at + distance, n) * rows, left, out_p1, out_p2, in_p1, in_p2)
            go_m = pack(s, base + lax.rem(at + n - distance, n) * rows, right, out_m1, out_m2, in_m1, in_m2)
            sweep(group, rows, lambda p, r, step: go_p(p, r, step) + go_m(p, r, step))
            def view(ref1, ref2):
                return ref1.at[some, window, short] if s == 1 else ref2.at[s - 2, some, window, every]
            go = [
                send(view(out_p1, out_p2), view(in_p1, in_p2), plus, axis + "+"),
                send(view(out_m1, out_m2), view(in_m1, in_m2), minus, axis + "-"),
            ]
            yield go

        def finish(p, r, step):
            there = strip(base + at * rows + r, step)
            here = strip(off + r, step)
            value = part[p, there, every] + decode(in_p2[far - 2, p, here, every])
            return [(part, (p, there, every), value + decode(in_m2[far - 2, p, here, every]))]
        sweep(group, rows, finish)

    def gather_chain(group, base, rows, n, at, plus, minus, axis):
        far = n // 2
        first, count, column, columns = group
        some, every = pl.ds(first, count), pl.ds(column, columns)
        left, right = pl.ds(column, columns // 2), pl.ds(column + columns // 2, columns // 2)
        for s in range(1, far + 1):
            cols_p, cols_m = (left, right) if s == far else (every, every)
            from_p = base + lax.rem(at + n - (s - 1), n) * rows
            from_m = base + lax.rem(at + (s - 1), n) * rows
            ref_p = slope.at[some, strip(from_p, rows), cols_p]
            ref_m = slope.at[some, strip(from_m, rows), cols_m]
            yield [send(ref_p, ref_p, plus, axis + "+"), send(ref_m, ref_m, minus, axis + "-")]

    plus_x, minus_x = device(dx=1), device(dx=nx - 1)
    plus_z, minus_z = device(dz=1), device(dz=nz - 1)
    rows_x, rows_z, rows_o = width // nx, width // nz, width // (nx * nz)
    base_x = x * rows_x
    base_z = z * rows_z
    bufs_x = (sx_p1, sx_m1, sx_p2, sx_m2, rx_p1, rx_m1, rx_p2, rx_m2)
    bufs_z = (sz_p1, sz_m1, sz_p2, sz_m2, rz_p1, rz_m1, rz_p2, rz_m2)

    def slopes(group, base):
        first, count, column, columns = group
        rows, cols = strip(base, rows_o), pl.ds(column, columns)
        row_ids = lax.broadcasted_iota(jnp.int32, (rows_o, columns), 0) + base
        col_ids = lax.broadcasted_iota(jnp.int32, (rows_o, columns), 1) + (c * half + column)
        for p in range(first, first + count):
            value = 2.0 * off_weight * (part[p, rows, cols] / total)
            if p < 2:
                value = jnp.where(row_ids == col_ids + p * piece, 0.0, value)
            slope[p, rows, cols] = value.astype(bf16)

    def one_way(group):
        yield from reduce_chain(group, 0, rows_x, nx, x, plus_x, minus_x, "x", 0, bufs_x)
        yield from reduce_chain(group, base_x, rows_o, nz, z, plus_z, minus_z, "z", rows_z, bufs_z)
        slopes(group, base_x + z * rows_o)
        yield from gather_chain(group, base_x, rows_o, nz, z, plus_z, minus_z, "z")
        yield from gather_chain(group, 0, rows_x, nx, x, plus_x, minus_x, "x")

    def other_way(group):
        yield from reduce_chain(group, 0, rows_z, nz, z, plus_z, minus_z, "z", 0, bufs_z)
        yield from reduce_chain(group, base_z, rows_o, nx, x, plus_x, minus_x, "x", rows_x, bufs_x)
        slopes(group, base_z + x * rows_o)
        yield from gather_chain(group, base_z, rows_o, nx, x, plus_x, minus_x, "x")
        yield from gather_chain(group, 0, rows_z, nz, z, plus_z, minus_z, "z")

    live = []

    def spawn(rank, task):
        live.append([rank, len(started), task, []])

    def run():
        while live:
            best = None
            for entry in live:
                rank, _, _, wait = entry
                if callable(wait):
                    if not wait():
                        continue
                    ready = clock[0]
                else:
                    ready = max([clock[0]] + [due[id(copy)] for copy in wait])
                key = (max(ready, clock[0] + 0.2), rank)
                if best is None or key < best[0]:
                    best = (key, entry)
            entry = best[1]
            if not callable(entry[3]):
                arrive(entry[3])
            entry[3] = next(entry[2], None)
            if entry[3] is None:
                live.remove(entry)

    def group(rank, ways, first, post):
        left = [len(ways)]
        def chain(way, what):
            yield from way(what)
            left[0] -= 1
            if not left[0]:
                yield lambda: diag_done
                yield from post
        for at, way in enumerate(ways):
            pieces = 2 // len(ways)
            spawn(rank, chain(way, (first + at * pieces, pieces, 0, piece)))

    def to_b(first):
        work(1.5)
        for p in (first, first + 1):
            part_b[p] = jnp.dot(na[...], slope[p], preferred_element_type=f32)

    begun = []

    def to_a(first):
        fresh = not begun
        work(2.0)
        begun.append(first)
        def body(i, _):
            rows = pl.ds(pl.multiple_of(i * 256, 256), 256)
            acc = None if fresh else back_a[:, rows]
            for p in (first, first + 1):
                term = lax.dot_general(
                    nb[p], slope[p, rows, :], (((1,), (1,)), ((), ())), preferred_element_type=f32)
                acc = term if acc is None else acc + term
            back_a[:, rows] = acc
            return 0
        lax.fori_loop(0, width // 256, body, 0)

    def squares(first):
        work(0.6)
        for p in (first, first + 1):
            def body(i, acc, p=p):
                rows = pl.ds(pl.multiple_of(i * 64, 64), 64)
                s = slope[p, rows, :].astype(f32)
                s = s * s
                row_acc[rows, :] += sum(s[:, k * 128 : (k + 1) * 128] for k in range(piece // 128))
                return acc + jnp.sum(s, axis=0, keepdims=True)
            square[p] = lax.fori_loop(0, width // 64, body, jnp.zeros((1, piece), f32))

    def code(out, base, extra):
        work(0.5)
        def body(i, _):
            rows = pl.ds(pl.multiple_of(i * 64, 64), 64)
            value = part_b[base, rows, :]
            if extra is not None:
                value = value + decode(ry[extra, rows, :])
            sy[out, rows, :] = encode(value)
            return 0
        lax.fori_loop(0, both // 64, body, 0)

    def gain(base, extra):
        work(0.5)
        def body(i, _):
            rows = pl.ds(pl.multiple_of(i * 64, 64), 64)
            part_b[base, rows, :] += decode(ry[extra, rows, :])
            return 0
        lax.fori_loop(0, both // 64, body, 0)

    done, last_y = [], []

    def post(first):
        to_b(first)
        if first:
            copies = []
            if first == 6:
                yield lambda: "far" in done
            for p, peer, link in ((first, up, "y+"), (first + 1, down, "y-")):
                code(p - 2, p, p - 4 if first == 6 else None)
                copies.append(send(sy.at[p - 2], ry.at[p - 2], peer, link))
            if first == 6:
                last_y.extend(copies)
            else:
                spawn(0, after_y(first, copies))
            yield []
        else:
            done.append("own")
        to_a(first)
        squares(first)

    def after_y(first, copies):
        yield copies
        if first == 4:
            done.append("far")
            return
        yield lambda: "own" in done
        gain(1, 0)
        gain(0, 1)

    def blocks():
        yield first
        second = [send(nb.at[3, :both], nb.at[4, :both], up, "y+"), send(nb.at[2, :both], nb.at[5, :both], down, "y-")]
        third = [send(nb.at[1, :both], nb.at[7, :both], up, "y+"), send(nb.at[0, :both], nb.at[6, :both], down, "y-")]
        correlate(2)
        group(RANKS[1], WAYS[1], 2, post(2))
        yield second
        correlate(4)
        group(RANKS[2], WAYS[2], 4, post(4))
        yield third
        correlate(6)
        group(RANKS[3], WAYS[3], 6, post(6))

    WAYS = [[one_way], [one_way], [other_way], [one_way]]
    RANKS = [4, 3, 2, 1]

    row_acc[...] = jnp.zeros_like(row_acc)
    arrive([swap_a])
    for i in range(width // 128):
        cols = pl.ds(i * 128, 128)
        nat[cols, :] = jnp.transpose(na[:both, cols].astype(f32)).astype(bf16)
    work(2.0)
    correlate(0)
    spawn(0, blocks())
    group(RANKS[0], WAYS[0], 0, post(0))
    spawn(2, diagonal())
    run()

    swap_back = send(back_a.at[other, :], recv_a, partner)

    scale = 1.0 / (2.0 * off_weight)
    corr_half = diag_f[c, 1, 0:1]
    loss_off = jnp.sum(sum(square[p] for p in range(count)), axis=1, keepdims=True)
    loss_diag = jnp.sum((1.0 - corr_half) ** 2, axis=1, keepdims=True)
    loss_row = jnp.broadcast_to(loss_off * (off_weight * scale * scale) + loss_diag, (1, half))
    for p in range(slots):
        block = extra_y.at[ny + p] if p else extra_y.at[m]
        left, right = PIECES.index((p, 0)), PIECES.index((p, 1))
        block[0:1, :piece] = part_b[left, both : both + 1, :]
        block[0:1, piece:] = part_b[right, both : both + 1, :]
        block[1:2, :piece] = square[left] * scale
        block[1:2, piece:] = square[right] * scale
        block[2:3, :] = loss_row
        block[3:4, :] = jnp.zeros((1, half), f32)
    share_y = [
        send(extra_y.at[ny + SLOT[k]], extra_y.at[m], peers_y[k - 1]) for k in range(1, ny)
    ]
    extra_a[c, 0:1, :] = back_a[both : both + 1, :]
    extra_a[c, 1:2, :] = jnp.sum(jnp.transpose(row_acc[...]), axis=0, keepdims=True) * scale
    share_a = send(extra_a.at[c], extra_a.at[c], partner)

    diag = jnp.concatenate([diag_f[0], diag_f[1]], axis=2)
    mean_a16, mean_own_b16 = diag[0, 0:1], diag[0, 1:2]
    corr_ii = diag[1, 0:1]
    cross_a, cross_b = diag[2, 0:1], diag[2, 1:2]
    slope_ii = (-2.0 * (1.0 - corr_ii)).astype(bf16).astype(f32)

    arrive([share_a])
    last_a = extra_a[0] + extra_a[1]
    mean_a = last_a[0:1] + mean_own_b16 * slope_ii
    inner_a = last_a[1:2] + cross_a * slope_ii
    arrive([swap_back])

    def finish_a(i, _):
        rows = pl.ds(pl.multiple_of(i * 32, 32), 32)
        wide = (a_ref[rows, :].astype(f32) - center_a) * inv_a
        back = back_a[rows, :] + recv_a[rows, :] + slope_ii * nb16[rows, :].astype(f32)
        ga_ref[rows, :] = (inv_a * (back - mean_a - wide * inner_a)).astype(bf16)
        return 0

    lax.fori_loop(0, frames // 32, finish_a, 0)

    arrive(share_y)
    extra_c[c] = sum(extra_y[i] for i in range(ny))
    share_c = send(extra_c.at[c], extra_c.at[c], partner)

    def add_last(base, dst, at):
        for side, got in ((0, 4), (1, 5)):
            cols = pl.ds(at if isinstance(at, int) else pl.multiple_of(at + side * piece, 128), piece)
            if isinstance(at, int):
                cols = pl.ds(side * piece, piece)
            def body(i, _, side=side, got=got, cols=cols):
                rows = pl.ds(pl.multiple_of(base + i * 64, 64), 64)
                here = pl.ds(pl.multiple_of(i * 64, 64), 64)
                dst[here, cols] = part_b[side, rows, :] + decode(ry[got, rows, :])
                return 0
            lax.fori_loop(0, frames // 64, body, 0)

    late = last_y + [swap_back, share_a, share_c] + share_y
    late = [id(copy) for copy in late]
    for copy in started:
        if id(copy) not in late:
            copy.wait_send()
    before = len(started)
    arrive(last_y)
    add_last(frames, sum_b, 0)
    swap_sum = [send(sum_b, full_b.at[:, own_half], partner)]
    add_last(0, full_b, c * half)

    arrive([share_c])
    mean_b = jnp.concatenate([extra_c[0, 0:1], extra_c[1, 0:1]], axis=1) + mean_a16 * slope_ii
    inner_b = jnp.concatenate([extra_c[0, 1:2], extra_c[1, 1:2]], axis=1) + cross_b * slope_ii
    loss_ref[...] = jnp.broadcast_to(extra_c[0, 2:3, :128] + extra_c[1, 2:3, :128], (8, 128))
    arrive(swap_sum)

    def finish_b(i, _):
        rows = pl.ds(pl.multiple_of(i * 32, 32), 32)
        wide = (b_ref[rows, :].astype(f32) - center_b) * inv_b
        back = full_b[rows, :] + slope_ii * na[rows, :].astype(f32)
        gb_ref[rows, :] = (inv_b * (back - mean_b - wide * inner_b)).astype(bf16)
        return 0

    lax.fori_loop(0, frames // 32, finish_b, 0)
    for at, copy in enumerate(started):
        if at >= before or id(copy) in late:
            copy.wait_send()


def solution(mesh):
    ny = mesh.shape["mp"]
    members = mesh.shape["dp"]
    nx = ny
    nz = members // (2 * nx)

    def per_device(view_a, view_b):
        frames, width = view_a.shape
        both, half = 2 * frames, width // 2
        rows_x, rows_z, rows_o = width // nx, width // nz, width // (nx * nz)
        vmem = pltpu.VMEM
        rings = []
        count, piece = 2 * ny, half // 2
        scratch = [
            vmem((frames, width), bf16),
            vmem((both + 16, width), bf16),
            vmem((width, both), bf16),
            vmem((count, both + 16, piece), bf16),
            vmem((count, width, piece), f32),
            vmem((count, width, piece), bf16),
            vmem((both + 16, width), f32),
            vmem((count, both + 16, piece), f32),
            vmem((frames, half), f32),
            vmem((frames, width), f32),
            vmem((2, 2, 2, width), f32),
            vmem((nx, 2, 2, width), f32),
            vmem((nz, 2, 2, width), f32),
            vmem((2, 3, 2, width), f32),
            vmem((nx, 3, 2, half), f32),
            vmem((nz, 3, 2, half), f32),
            vmem((2, 3, 2, half), f32),
            vmem((ny, 1, half), f32),
            vmem((count, 1, piece), f32),
            vmem((2 * ny, 4, half), f32),
            vmem((2, 4, half), f32),
            vmem((2, 2, width), f32),
            vmem((width, 128), f32),
        ]
        for rows, n in ((rows_x + rows_o, nx), (rows_z + rows_o, nz)):
            ring = [vmem((count, rows, piece // 2), bf16)] * 2
            rings.append(ring + [vmem((n // 2 - 1, count, rows, piece), bf16)] * 2)
        scratch += rings[0] + rings[1] + rings[0] + rings[1] + [vmem((count - 2, both, piece), bf16)] * 2 + [
            vmem((frames, width), f32),
            pltpu.SemaphoreType.DMA((256,)),
            pltpu.SemaphoreType.DMA((256,)),
        ]
        grad_a, grad_b, loss = pl.pallas_call(
            functools.partial(kernel, nx, nz, ny, float(frames * members)),
            out_shape=(
                jax.ShapeDtypeStruct((frames, width), bf16),
                jax.ShapeDtypeStruct((frames, width), bf16),
                jax.ShapeDtypeStruct((8, 128), f32),
            ),
            in_specs=[pl.BlockSpec(memory_space=vmem)] * 2,
            out_specs=[pl.BlockSpec(memory_space=vmem)] * 3,
            scratch_shapes=scratch,
            compiler_params=pltpu.CompilerParams(
                collective_id=0, has_side_effects=True, vmem_limit_bytes=56 * 1024 * 1024
            ),
            cost_estimate=pl.CostEstimate(
                flops=3 * 2 * both * width * half * ny, bytes_accessed=4 * frames * width * 2,
                transcendentals=0),
        )(view_a, view_b)
        return grad_a, grad_b, loss[0, 0]

    placed = P("dp", "mp")
    return jax.shard_map(
        per_device,
        mesh=mesh,
        in_specs=(placed, placed),
        out_specs=(placed, placed, P()),
        check_vma=False,
    )
```

```python
import functools

import jax
import jax.numpy as jnp
from jax import lax
from jax.experimental import pallas as pl
from jax.experimental.pallas import tpu as pltpu
from jax.sharding import PartitionSpec as P

epsilon = 1e-05
off_weight = 0.0051

MESH = pl.DeviceIdType.MESH
f32 = jnp.float32
bf16 = jnp.bfloat16

PIECES = ((0, 0), (0, 1), (1, 1), (2, 0), (3, 0), (3, 1), (1, 0), (2, 1))
SLOT = (0, 1, 3, 2)


tiny = 1e-37


def encode(v):
    return ((v * v) * (v * jnp.abs(v))).astype(bf16)


def decode(y):
    y = y.astype(f32)
    y = y * lax.rsqrt(jnp.maximum(jnp.abs(y), tiny))
    return y * lax.rsqrt(jnp.maximum(jnp.abs(y), tiny))


def kernel(
    nx, nz, ny, total,
    a_ref, b_ref, ga_ref, gb_ref, loss_ref,
    nb16, na, nat, nb, part, slope, back_a, part_b, sum_b, full_b,
    stat_c, stat_x, stat_z, diag_c, diag_x, diag_z, diag_f,
    mean_b16, square, extra_y, extra_c, extra_a, row_acc,
    rx_p1, rx_m1, rx_p2, rx_m2, rz_p1, rz_m1, rz_p2, rz_m2,
    sx_p1, sx_m1, sx_p2, sx_m2, sz_p1, sz_m1, sz_p2, sz_m2,
    sy, ry, recv_a,
    send_sems, recv_sems,
):
    frames, width = a_ref.shape
    both = 2 * frames
    half = width // 2
    slots, count, piece = ny, 2 * ny, half // 2
    dp = lax.axis_index("dp")
    m = lax.axis_index("mp")
    c = lax.rem(dp, 2)
    x = lax.rem(dp // 2, nx)
    z = dp // (2 * nx)

    def device(dc=0, dx=0, dz=0, dy=0):
        there = (lax.rem(z + dz, nz) * nx + lax.rem(x + dx, nx)) * 2
        there = there + (1 - c if dc else c)
        return (there, lax.rem(m + dy, ny))

    partner = device(dc=1)
    peers_x = [device(dx=k) for k in range(1, nx)]
    peers_z = [device(dz=k) for k in range(1, nz)]
    peers_y = [device(dy=k) for k in range(1, ny)]
    everyone = [partner] + peers_x + peers_z + peers_y

    barrier = pltpu.get_barrier_semaphore()
    for peer in everyone:
        pl.semaphore_signal(barrier, inc=1, device_id=peer, device_id_type=MESH)

    started, due, clock, free = [], {}, [0.0], {}

    def work(t):
        clock[0] += t

    def send(src, dst, peer, link=None):
        at = len(started)
        work(0.2)
        size = src.dtype.itemsize
        for d in src.shape:
            size *= d
        rate = 45e3 if link else 500e3
        begin = max(clock[0], free.get(link, 0.0)) if link else clock[0]
        end = begin + size / rate
        if link:
            free[link] = end
        copy = pltpu.make_async_remote_copy(
            src_ref=src,
            dst_ref=dst,
            send_sem=send_sems.at[at],
            recv_sem=recv_sems.at[at],
            device_id=peer,
            device_id_type=MESH,
        )
        copy.start()
        started.append(copy)
        due[id(copy)] = end + 1.5
        return copy

    def arrive(copies):
        for copy in copies:
            clock[0] = max(clock[0], due[id(copy)])
            copy.wait_recv()

    def spread_to(buf, mine, peers):
        return [send(buf.at[mine], buf.at[mine], peer) for peer in peers]

    def column_sum(fn):
        step = 64
        def body(i, acc):
            return acc + jnp.sum(fn(pl.ds(i * step, step)), axis=0, keepdims=True)
        return lax.fori_loop(0, frames // step, body, jnp.zeros((1, width), f32))

    for view, ref in enumerate((a_ref, b_ref)):
        center = column_sum(lambda rows: ref[rows, :].astype(f32)) / frames
        def deviation(rows, ref=ref, center=center):
            dev = ref[rows, :].astype(f32) - center
            return dev * dev
        stat_c[c, 0, view : view + 1, :] = center
        stat_c[c, 1, view : view + 1, :] = column_sum(deviation)

    pl.semaphore_wait(barrier, len(everyone))
    work(5.0)

    def merge(buf, members, count):
        center = sum(buf[i, 0] for i in range(members)) * (1.0 / members)
        spread = sum(buf[i, 1] for i in range(members))
        shift = sum((buf[i, 0] - center) ** 2 for i in range(members))
        return center, spread + count * shift

    arrive(spread_to(stat_c, c, [partner]))
    stat_x[x, 0], stat_x[x, 1] = merge(stat_c, 2, float(frames))
    arrive(spread_to(stat_x, x, peers_x))
    stat_z[z, 0], stat_z[z, 1] = merge(stat_x, nx, float(frames * 2))
    arrive(spread_to(stat_z, z, peers_z))
    center, spread = merge(stat_z, nz, float(frames * 2 * nx))
    inv = lax.rsqrt(spread / total + epsilon)
    center_a, center_b = center[0:1], center[1:2]
    inv_a, inv_b = inv[0:1], inv[1:2]

    own, other = pl.ds(0, frames), pl.ds(frames, frames)
    own_half = pl.ds(pl.multiple_of(c * half, 128), half)
    other_half = pl.ds(pl.multiple_of((1 - c) * half, 128), half)

    def standardize(src, dst, center, inv):
        def body(i, _):
            rows = pl.ds(pl.multiple_of(i * 32, 32), 32)
            dst[rows, :] = ((src[rows, :].astype(f32) - center) * inv).astype(bf16)
            return 0
        lax.fori_loop(0, frames // 32, body, 0)

    standardize(b_ref, nb16, center_b, inv_b)
    swap_b = [
        send(
            nb16.at[:, pl.ds(pl.multiple_of((1 - c) * half + side * piece, 128), piece)],
            nb.at[side, other], partner)
        for side in range(2)
    ]
    for side in range(2):
        nb[side, own, :] = nb16[:, pl.ds(pl.multiple_of(c * half + side * piece, 128), piece)]
    up, down = device(dy=1), device(dy=ny - 1)
    first = [send(nb.at[0, own], nb.at[3, own], up, "y+"), send(nb.at[1, own], nb.at[2, own], down, "y-")]
    standardize(a_ref, na, center_a, inv_a)
    swap_a = send(na.at[own], na.at[other], partner)
    arrive(swap_b)
    first.append(send(nb.at[0, other], nb.at[3, other], up, "y+"))
    first.append(send(nb.at[1, other], nb.at[2, other], down, "y-"))

    diag_done = []

    def diagonal():
        def body(i, acc):
            rows = pl.ds(pl.multiple_of(i * 32, 32), 32)
            wide_a = (a_ref[rows, :].astype(f32) - center_a) * inv_a
            wide_b = (b_ref[rows, :].astype(f32) - center_b) * inv_b
            short_a, short_b = na[rows, :].astype(f32), nb16[rows, :].astype(f32)
            terms = (short_a, short_b, short_a * short_b, wide_a * short_b, wide_b * short_a)
            return tuple(s + jnp.sum(t, axis=0, keepdims=True) for s, t in zip(acc, terms))
        sums = lax.fori_loop(0, frames // 32, body, (jnp.zeros((1, width), f32),) * 5)
        for at, value in enumerate(sums[:3] + (jnp.zeros((1, width), f32),) + sums[3:]):
            diag_c[c, at // 2, at % 2 : at % 2 + 1, :] = value
        work(1.5)
        copies = spread_to(diag_c, c, [partner])
        yield copies
        diag_x[x] = jnp.where(
            c == 0, diag_c[0, :, :, :half] + diag_c[1, :, :, :half],
            diag_c[0, :, :, half:] + diag_c[1, :, :, half:])
        copies = spread_to(diag_x, x, peers_x)
        yield copies
        diag_z[z] = sum(diag_x[i] for i in range(nx))
        copies = spread_to(diag_z, z, peers_z)
        yield copies
        diag_f[c] = sum(diag_z[i] for i in range(nz)) / total
        mean_b16[0] = diag_f[c, 0, 1:2]
        copies = spread_to(diag_f, c, [partner])
        copies += [send(mean_b16.at[0], mean_b16.at[SLOT[ny - k]], peers_y[k - 1]) for k in range(1, ny)]
        yield copies
        mean_a = jnp.concatenate([diag_f[0, 0, 0:1], diag_f[1, 0, 0:1]], axis=1)
        na[pl.ds(both, 16), :] = jnp.broadcast_to(mean_a, (16, width)).astype(bf16)
        for p, (slot, side) in enumerate(PIECES):
            mean_b = mean_b16[slot, :, side * piece : (side + 1) * piece]
            nb[p, pl.ds(both, 16), :] = jnp.broadcast_to(mean_b, (16, piece)).astype(bf16)
        diag_done.append(True)

    def correlate(first):
        work(1.5)
        def body(i, _):
            rows = pl.ds(pl.multiple_of(i * 256, 256), 256)
            for p in (first, first + 1):
                part[p, rows, :] = jnp.dot(nat[rows, :], nb[p, :both, :], preferred_element_type=f32)
            return 0
        lax.fori_loop(0, width // 256, body, 0)

    def sweep(group, rows, fn):
        first, count, _, columns = group
        work(0.004 * rows * count * columns / 1024)
        step = min(rows, 32)
        turns = count * (rows // step)
        per = min(turns, max(1, 16384 // (step * columns)))
        def body(i, _):
            stores = []
            for u in range(per):
                k = i * per + u
                p = first + k // (rows // step)
                r = k % (rows // step) * step if isinstance(k, int) else lax.rem(k, rows // step) * step
                stores += fn(p, r, step)
            for ref, at, value in stores:
                ref[at] = value
            return 0
        if turns == per:
            body(0, 0)
        else:
            lax.fori_loop(0, turns // per, body, 0)

    def strip(base, step):
        return pl.ds(base if isinstance(base, int) else pl.multiple_of(base, 16), step)

    def reduce_chain(group, base, rows, n, at, plus, minus, axis, off, bufs):
        out_p1, out_m1, out_p2, out_m2, in_p1, in_m1, in_p2, in_m2 = bufs
        far = n // 2
        first, count, column, columns = group
        some, window, every = pl.ds(first, count), pl.ds(off, rows), pl.ds(column, columns)
        left, right = pl.ds(column, columns // 2), pl.ds(column + columns // 2, columns // 2)
        short = pl.ds(column // 2, columns // 2)

        def pack(s, source, cols, out1, out2, in1, in2):
            rest = right if cols is left else left
            def fn(p, r, step):
                there = strip(source + r, step)
                here = strip(off + r, step)
                if s == 1:
                    return [(out1, (p, here, short), encode(part[p, there, cols]))]
                if s > 2:
                    value = encode(part[p, there, every] + decode(in2[s - 3, p, here, every]))
                    return [(out2, (s - 2, p, here, every), value)]
                value = encode(part[p, there, cols] + decode(in1[p, here, short]))
                return [
                    (out2, (0, p, here, cols), value),
                    (out2, (0, p, here, rest), encode(part[p, there, rest])),
                ]
            return fn

        for s in range(1, far + 1):
            distance = far + 1 - s
            go_p = pack(s, base + lax.rem(at + distance, n) * rows, left, out_p1, out_p2, in_p1, in_p2)
            go_m = pack(s, base + lax.rem(at + n - distance, n) * rows, right, out_m1, out_m2, in_m1, in_m2)
            sweep(group, rows, lambda p, r, step: go_p(p, r, step) + go_m(p, r, step))
            def view(ref1, ref2):
                return ref1.at[some, window, short] if s == 1 else ref2.at[s - 2, some, window, every]
            go = [
                send(view(out_p1, out_p2), view(in_p1, in_p2), plus, axis + "+"),
                send(view(out_m1, out_m2), view(in_m1, in_m2), minus, axis + "-"),
            ]
            yield go

        def finish(p, r, step):
            there = strip(base + at * rows + r, step)
            here = strip(off + r, step)
            value = part[p, there, every] + decode(in_p2[far - 2, p, here, every])
            return [(part, (p, there, every), value + decode(in_m2[far - 2, p, here, every]))]
        sweep(group, rows, finish)

    def gather_chain(group, base, rows, n, at, plus, minus, axis):
        far = n // 2
        first, count, column, columns = group
        some, every = pl.ds(first, count), pl.ds(column, columns)
        left, right = pl.ds(column, columns // 2), pl.ds(column + columns // 2, columns // 2)
        for s in range(1, far + 1):
            cols_p, cols_m = (left, right) if s == far else (every, every)
            from_p = base + lax.rem(at + n - (s - 1), n) * rows
            from_m = base + lax.rem(at + (s - 1), n) * rows
            ref_p = slope.at[some, strip(from_p, rows), cols_p]
            ref_m = slope.at[some, strip(from_m, rows), cols_m]
            yield [send(ref_p, ref_p, plus, axis + "+"), send(ref_m, ref_m, minus, axis + "-")]

    plus_x, minus_x = device(dx=1), device(dx=nx - 1)
    plus_z, minus_z = device(dz=1), device(dz=nz - 1)
    rows_x, rows_z, rows_o = width // nx, width // nz, width // (nx * nz)
    base_x = x * rows_x
    base_z = z * rows_z
    bufs_x = (sx_p1, sx_m1, sx_p2, sx_m2, rx_p1, rx_m1, rx_p2, rx_m2)
    bufs_z = (sz_p1, sz_m1, sz_p2, sz_m2, rz_p1, rz_m1, rz_p2, rz_m2)

    def slopes(group, base):
        first, count, column, columns = group
        rows, cols = strip(base, rows_o), pl.ds(column, columns)
        row_ids = lax.broadcasted_iota(jnp.int32, (rows_o, columns), 0) + base
        col_ids = lax.broadcasted_iota(jnp.int32, (rows_o, columns), 1) + (c * half + column)
        for p in range(first, first + count):
            value = 2.0 * off_weight * (part[p, rows, cols] / total)
            if p < 2:
                value = jnp.where(row_ids == col_ids + p * piece, 0.0, value)
            slope[p, rows, cols] = value.astype(bf16)

    def one_way(group):
        yield from reduce_chain(group, 0, rows_x, nx, x, plus_x, minus_x, "x", 0, bufs_x)
        yield from reduce_chain(group, base_x, rows_o, nz, z, plus_z, minus_z, "z", rows_z, bufs_z)
        slopes(group, base_x + z * rows_o)
        yield from gather_chain(group, base_x, rows_o, nz, z, plus_z, minus_z, "z")
        yield from gather_chain(group, 0, rows_x, nx, x, plus_x, minus_x, "x")

    def other_way(group):
        yield from reduce_chain(group, 0, rows_z, nz, z, plus_z, minus_z, "z", 0, bufs_z)
        yield from reduce_chain(group, base_z, rows_o, nx, x, plus_x, minus_x, "x", rows_x, bufs_x)
        slopes(group, base_z + x * rows_o)
        yield from gather_chain(group, base_z, rows_o, nx, x, plus_x, minus_x, "x")
        yield from gather_chain(group, 0, rows_z, nz, z, plus_z, minus_z, "z")

    live = []

    def spawn(rank, task):
        live.append([rank, len(started), task, []])

    def run():
        while live:
            best = None
            for entry in live:
                rank, _, _, wait = entry
                if callable(wait):
                    if not wait():
                        continue
                    ready = clock[0]
                else:
                    ready = max([clock[0]] + [due[id(copy)] for copy in wait])
                key = (max(ready, clock[0] + 0.2), rank)
                if best is None or key < best[0]:
                    best = (key, entry)
            entry = best[1]
            if not callable(entry[3]):
                arrive(entry[3])
            entry[3] = next(entry[2], None)
            if entry[3] is None:
                live.remove(entry)

    def group(rank, ways, first, post):
        left = [len(ways)]
        def chain(way, what):
            yield from way(what)
            left[0] -= 1
            if not left[0]:
                yield lambda: diag_done
                yield from post
        for at, way in enumerate(ways):
            pieces = 2 // len(ways)
            spawn(rank, chain(way, (first + at * pieces, pieces, 0, piece)))

    def to_b(first):
        work(1.5)
        for p in (first, first + 1):
            part_b[p] = jnp.dot(na[...], slope[p], preferred_element_type=f32)

    begun = []

    def to_a(first):
        fresh = not begun
        work(2.0)
        begun.append(first)
        def body(i, _):
            rows = pl.ds(pl.multiple_of(i * 256, 256), 256)
            acc = None if fresh else back_a[:, rows]
            for p in (first, first + 1):
                term = lax.dot_general(
                    nb[p], slope[p, rows, :], (((1,), (1,)), ((), ())), preferred_element_type=f32)
                acc = term if acc is None else acc + term
            back_a[:, rows] = acc
            return 0
        lax.fori_loop(0, width // 256, body, 0)

    def squares(first):
        work(0.6)
        for p in (first, first + 1):
            def body(i, acc, p=p):
                rows = pl.ds(pl.multiple_of(i * 64, 64), 64)
                s = slope[p, rows, :].astype(f32)
                s = s * s
                row_acc[rows, :] += sum(s[:, k * 128 : (k + 1) * 128] for k in range(piece // 128))
                return acc + jnp.sum(s, axis=0, keepdims=True)
            square[p] = lax.fori_loop(0, width // 64, body, jnp.zeros((1, piece), f32))

    def code(out, base, extra):
        work(0.5)
        def body(i, _):
            rows = pl.ds(pl.multiple_of(i * 64, 64), 64)
            value = part_b[base, rows, :]
            if extra is not None:
                value = value + decode(ry[extra, rows, :])
            sy[out, rows, :] = encode(value)
            return 0
        lax.fori_loop(0, both // 64, body, 0)

    def gain(base, extra):
        work(0.5)
        def body(i, _):
            rows = pl.ds(pl.multiple_of(i * 64, 64), 64)
            part_b[base, rows, :] += decode(ry[extra, rows, :])
            return 0
        lax.fori_loop(0, both // 64, body, 0)

    done, last_y = [], []

    def post(first):
        to_b(first)
        if first:
            copies = []
            if first == 6:
                yield lambda: "far" in done
            for p, peer, link in ((first, up, "y+"), (first + 1, down, "y-")):
                code(p - 2, p, p - 4 if first == 6 else None)
                if first == 6:
                    last_y.extend(
                        send(sy.at[p - 2, rows], ry.at[p - 2, rows], peer, link) for rows in (other, own))
                else:
                    copies.append(send(sy.at[p - 2], ry.at[p - 2], peer, link))
            if first < 6:
                spawn(0, after_y(first, copies))
            yield []
        else:
            done.append("own")
        to_a(first)
        squares(first)

    def after_y(first, copies):
        yield copies
        if first == 4:
            done.append("far")
            return
        yield lambda: "own" in done
        gain(1, 0)
        gain(0, 1)

    def blocks():
        yield first
        second = [send(nb.at[3, :both], nb.at[4, :both], up, "y+"), send(nb.at[2, :both], nb.at[5, :both], down, "y-")]
        third = [send(nb.at[1, :both], nb.at[7, :both], up, "y+"), send(nb.at[0, :both], nb.at[6, :both], down, "y-")]
        correlate(2)
        group(RANKS[1], WAYS[1], 2, post(2))
        yield second
        correlate(4)
        group(RANKS[2], WAYS[2], 4, post(4))
        yield third
        correlate(6)
        group(RANKS[3], WAYS[3], 6, post(6))

    WAYS = [[one_way], [one_way], [other_way], [one_way]]
    RANKS = [4, 3, 2, 1]

    row_acc[...] = jnp.zeros_like(row_acc)
    arrive([swap_a])
    for i in range(width // 128):
        cols = pl.ds(i * 128, 128)
        nat[cols, :] = jnp.transpose(na[:both, cols].astype(f32)).astype(bf16)
    work(2.0)
    correlate(0)
    spawn(0, blocks())
    group(RANKS[0], WAYS[0], 0, post(0))
    spawn(2, diagonal())
    run()

    swap_back = send(back_a.at[other, :], recv_a, partner)

    scale = 1.0 / (2.0 * off_weight)
    corr_half = diag_f[c, 1, 0:1]
    loss_off = jnp.sum(sum(square[p] for p in range(count)), axis=1, keepdims=True)
    loss_diag = jnp.sum((1.0 - corr_half) ** 2, axis=1, keepdims=True)
    loss_row = jnp.broadcast_to(loss_off * (off_weight * scale * scale) + loss_diag, (1, half))
    for p in range(slots):
        block = extra_y.at[ny + p] if p else extra_y.at[m]
        left, right = PIECES.index((p, 0)), PIECES.index((p, 1))
        block[0:1, :piece] = part_b[left, both : both + 1, :]
        block[0:1, piece:] = part_b[right, both : both + 1, :]
        block[1:2, :piece] = square[left] * scale
        block[1:2, piece:] = square[right] * scale
        block[2:3, :] = loss_row
        block[3:4, :] = jnp.zeros((1, half), f32)
    share_y = [
        send(extra_y.at[ny + SLOT[k]], extra_y.at[m], peers_y[k - 1]) for k in range(1, ny)
    ]
    extra_a[c, 0:1, :] = back_a[both : both + 1, :]
    extra_a[c, 1:2, :] = jnp.sum(jnp.transpose(row_acc[...]), axis=0, keepdims=True) * scale
    share_a = send(extra_a.at[c], extra_a.at[c], partner)

    diag = jnp.concatenate([diag_f[0], diag_f[1]], axis=2)
    mean_a16, mean_own_b16 = diag[0, 0:1], diag[0, 1:2]
    corr_ii = diag[1, 0:1]
    cross_a, cross_b = diag[2, 0:1], diag[2, 1:2]
    slope_ii = (-2.0 * (1.0 - corr_ii)).astype(bf16).astype(f32)

    arrive([share_a])
    last_a = extra_a[0] + extra_a[1]
    mean_a = last_a[0:1] + mean_own_b16 * slope_ii
    inner_a = last_a[1:2] + cross_a * slope_ii
    arrive([swap_back])

    def finish_a(i, _):
        rows = pl.ds(pl.multiple_of(i * 32, 32), 32)
        wide = (a_ref[rows, :].astype(f32) - center_a) * inv_a
        back = back_a[rows, :] + recv_a[rows, :] + slope_ii * nb16[rows, :].astype(f32)
        ga_ref[rows, :] = (inv_a * (back - mean_a - wide * inner_a)).astype(bf16)
        return 0

    lax.fori_loop(0, frames // 32, finish_a, 0)

    arrive(share_y)
    extra_c[c] = sum(extra_y[i] for i in range(ny))
    share_c = send(extra_c.at[c], extra_c.at[c], partner)

    def add_last(base, dst, at):
        for side, got in ((0, 4), (1, 5)):
            cols = pl.ds(at if isinstance(at, int) else pl.multiple_of(at + side * piece, 128), piece)
            if isinstance(at, int):
                cols = pl.ds(side * piece, piece)
            def body(i, _, side=side, got=got, cols=cols):
                rows = pl.ds(pl.multiple_of(base + i * 64, 64), 64)
                here = pl.ds(pl.multiple_of(i * 64, 64), 64)
                dst[here, cols] = part_b[side, rows, :] + decode(ry[got, rows, :])
                return 0
            lax.fori_loop(0, frames // 64, body, 0)

    late = last_y + [swap_back, share_a, share_c] + share_y
    late = [id(copy) for copy in late]
    for copy in started:
        if id(copy) not in late:
            copy.wait_send()
    before = len(started)
    arrive(last_y[0::2])
    add_last(frames, sum_b, 0)
    swap_sum = [send(sum_b, full_b.at[:, own_half], partner)]
    arrive(last_y[1::2])
    add_last(0, full_b, c * half)

    arrive([share_c])
    mean_b = jnp.concatenate([extra_c[0, 0:1], extra_c[1, 0:1]], axis=1) + mean_a16 * slope_ii
    inner_b = jnp.concatenate([extra_c[0, 1:2], extra_c[1, 1:2]], axis=1) + cross_b * slope_ii
    loss_ref[...] = jnp.broadcast_to(extra_c[0, 2:3, :128] + extra_c[1, 2:3, :128], (8, 128))
    arrive(swap_sum)

    def finish_b(i, _):
        rows = pl.ds(pl.multiple_of(i * 32, 32), 32)
        wide = (b_ref[rows, :].astype(f32) - center_b) * inv_b
        back = full_b[rows, :] + slope_ii * na[rows, :].astype(f32)
        gb_ref[rows, :] = (inv_b * (back - mean_b - wide * inner_b)).astype(bf16)
        return 0

    lax.fori_loop(0, frames // 32, finish_b, 0)
    for at, copy in enumerate(started):
        if at >= before or id(copy) in late:
            copy.wait_send()


def solution(mesh):
    ny = mesh.shape["mp"]
    members = mesh.shape["dp"]
    nx = ny
    nz = members // (2 * nx)

    def per_device(view_a, view_b):
        frames, width = view_a.shape
        both, half = 2 * frames, width // 2
        rows_x, rows_z, rows_o = width // nx, width // nz, width // (nx * nz)
        vmem = pltpu.VMEM
        rings = []
        count, piece = 2 * ny, half // 2
        scratch = [
            vmem((frames, width), bf16),
            vmem((both + 16, width), bf16),
            vmem((width, both), bf16),
            vmem((count, both + 16, piece), bf16),
            vmem((count, width, piece), f32),
            vmem((count, width, piece), bf16),
            vmem((both + 16, width), f32),
            vmem((count, both + 16, piece), f32),
            vmem((frames, half), f32),
            vmem((frames, width), f32),
            vmem((2, 2, 2, width), f32),
            vmem((nx, 2, 2, width), f32),
            vmem((nz, 2, 2, width), f32),
            vmem((2, 3, 2, width), f32),
            vmem((nx, 3, 2, half), f32),
            vmem((nz, 3, 2, half), f32),
            vmem((2, 3, 2, half), f32),
            vmem((ny, 1, half), f32),
            vmem((count, 1, piece), f32),
            vmem((2 * ny, 4, half), f32),
            vmem((2, 4, half), f32),
            vmem((2, 2, width), f32),
            vmem((width, 128), f32),
        ]
        for rows, n in ((rows_x + rows_o, nx), (rows_z + rows_o, nz)):
            ring = [vmem((count, rows, piece // 2), bf16)] * 2
            rings.append(ring + [vmem((n // 2 - 1, count, rows, piece), bf16)] * 2)
        scratch += rings[0] + rings[1] + rings[0] + rings[1] + [vmem((count - 2, both, piece), bf16)] * 2 + [
            vmem((frames, width), f32),
            pltpu.SemaphoreType.DMA((256,)),
            pltpu.SemaphoreType.DMA((256,)),
        ]
        grad_a, grad_b, loss = pl.pallas_call(
            functools.partial(kernel, nx, nz, ny, float(frames * members)),
            out_shape=(
                jax.ShapeDtypeStruct((frames, width), bf16),
                jax.ShapeDtypeStruct((frames, width), bf16),
                jax.ShapeDtypeStruct((8, 128), f32),
            ),
            in_specs=[pl.BlockSpec(memory_space=vmem)] * 2,
            out_specs=[pl.BlockSpec(memory_space=vmem)] * 3,
            scratch_shapes=scratch,
            compiler_params=pltpu.CompilerParams(
                collective_id=0, has_side_effects=True, vmem_limit_bytes=56 * 1024 * 1024
            ),
            cost_estimate=pl.CostEstimate(
                flops=3 * 2 * both * width * half * ny, bytes_accessed=4 * frames * width * 2,
                transcendentals=0),
        )(view_a, view_b)
        return grad_a, grad_b, loss[0, 0]

    placed = P("dp", "mp")
    return jax.shard_map(
        per_device,
        mesh=mesh,
        in_specs=(placed, placed),
        out_specs=(placed, placed, P()),
        check_vma=False,
    )
```

```python
import functools

import jax
import jax.numpy as jnp
from jax import lax
from jax.experimental import pallas as pl
from jax.experimental.pallas import tpu as pltpu
from jax.sharding import PartitionSpec as P

epsilon = 1e-05
off_weight = 0.0051

MESH = pl.DeviceIdType.MESH
f32 = jnp.float32
bf16 = jnp.bfloat16

PIECES = ((0, 0), (0, 1), (1, 1), (2, 0), (3, 0), (3, 1), (1, 0), (2, 1))
SLOT = (0, 1, 3, 2)


tiny = 1e-37


def encode(v):
    return ((v * v) * (v * jnp.abs(v))).astype(bf16)


def decode(y):
    y = y.astype(f32)
    y = y * lax.rsqrt(jnp.maximum(jnp.abs(y), tiny))
    return y * lax.rsqrt(jnp.maximum(jnp.abs(y), tiny))


def kernel(
    nx, nz, ny, total,
    a_ref, b_ref, ga_ref, gb_ref, loss_ref,
    nb16, na, nat, nb, part, slope, back_a, part_b, sum_b, full_b,
    stat_c, stat_x, stat_z, diag_c, diag_x, diag_z, diag_f,
    mean_b16, square, extra_y, extra_c, extra_a, row_acc,
    rx_p1, rx_m1, rx_p2, rx_m2, rz_p1, rz_m1, rz_p2, rz_m2,
    sx_p1, sx_m1, sx_p2, sx_m2, sz_p1, sz_m1, sz_p2, sz_m2,
    sy, ry, recv_a,
    send_sems, recv_sems,
):
    frames, width = a_ref.shape
    both = 2 * frames
    half = width // 2
    slots, count, piece = ny, 2 * ny, half // 2
    dp = lax.axis_index("dp")
    m = lax.axis_index("mp")
    c = lax.rem(dp, 2)
    x = lax.rem(dp // 2, nx)
    z = dp // (2 * nx)

    def device(dc=0, dx=0, dz=0, dy=0):
        there = (lax.rem(z + dz, nz) * nx + lax.rem(x + dx, nx)) * 2
        there = there + (1 - c if dc else c)
        return (there, lax.rem(m + dy, ny))

    partner = device(dc=1)
    peers_x = [device(dx=k) for k in range(1, nx)]
    peers_z = [device(dz=k) for k in range(1, nz)]
    peers_y = [device(dy=k) for k in range(1, ny)]
    everyone = [partner] + peers_x + peers_z + peers_y

    barrier = pltpu.get_barrier_semaphore()
    for peer in everyone:
        pl.semaphore_signal(barrier, inc=1, device_id=peer, device_id_type=MESH)

    started, due, clock, free = [], {}, [0.0], {}

    def work(t):
        clock[0] += t

    def send(src, dst, peer, link=None):
        at = len(started)
        work(0.2)
        size = src.dtype.itemsize
        for d in src.shape:
            size *= d
        rate = 45e3 if link else 500e3
        begin = max(clock[0], free.get(link, 0.0)) if link else clock[0]
        end = begin + size / rate
        if link:
            free[link] = end
        copy = pltpu.make_async_remote_copy(
            src_ref=src,
            dst_ref=dst,
            send_sem=send_sems.at[at],
            recv_sem=recv_sems.at[at],
            device_id=peer,
            device_id_type=MESH,
        )
        copy.start()
        started.append(copy)
        due[id(copy)] = end + 1.5
        return copy

    def arrive(copies):
        for copy in copies:
            clock[0] = max(clock[0], due[id(copy)])
            copy.wait_recv()

    def spread_to(buf, mine, peers):
        return [send(buf.at[mine], buf.at[mine], peer) for peer in peers]

    def column_sum(fn):
        step = 64
        def body(i, acc):
            return acc + jnp.sum(fn(pl.ds(i * step, step)), axis=0, keepdims=True)
        return lax.fori_loop(0, frames // step, body, jnp.zeros((1, width), f32))

    for view, ref in enumerate((a_ref, b_ref)):
        center = column_sum(lambda rows: ref[rows, :].astype(f32)) / frames
        def deviation(rows, ref=ref, center=center):
            dev = ref[rows, :].astype(f32) - center
            return dev * dev
        stat_c[c, 0, view : view + 1, :] = center
        stat_c[c, 1, view : view + 1, :] = column_sum(deviation)

    pl.semaphore_wait(barrier, len(everyone))
    work(5.0)

    def merge(buf, members, count):
        center = sum(buf[i, 0] for i in range(members)) * (1.0 / members)
        spread = sum(buf[i, 1] for i in range(members))
        shift = sum((buf[i, 0] - center) ** 2 for i in range(members))
        return center, spread + count * shift

    arrive(spread_to(stat_c, c, [partner]))
    stat_x[x, 0], stat_x[x, 1] = merge(stat_c, 2, float(frames))
    arrive(spread_to(stat_x, x, peers_x))
    stat_z[z, 0], stat_z[z, 1] = merge(stat_x, nx, float(frames * 2))
    arrive(spread_to(stat_z, z, peers_z))
    center, spread = merge(stat_z, nz, float(frames * 2 * nx))
    inv = lax.rsqrt(spread / total + epsilon)
    center_a, center_b = center[0:1], center[1:2]
    inv_a, inv_b = inv[0:1], inv[1:2]

    own, other = pl.ds(0, frames), pl.ds(frames, frames)
    own_half = pl.ds(pl.multiple_of(c * half, 128), half)
    other_half = pl.ds(pl.multiple_of((1 - c) * half, 128), half)

    def standardize(src, dst, center, inv):
        def body(i, _):
            rows = pl.ds(pl.multiple_of(i * 32, 32), 32)
            dst[rows, :] = ((src[rows, :].astype(f32) - center) * inv).astype(bf16)
            return 0
        lax.fori_loop(0, frames // 32, body, 0)

    standardize(b_ref, nb16, center_b, inv_b)
    swap_b = [
        send(
            nb16.at[:, pl.ds(pl.multiple_of((1 - c) * half + side * piece, 128), piece)],
            nb.at[side, other], partner)
        for side in range(2)
    ]
    for side in range(2):
        nb[side, own, :] = nb16[:, pl.ds(pl.multiple_of(c * half + side * piece, 128), piece)]
    up, down = device(dy=1), device(dy=ny - 1)
    first = [send(nb.at[0, own], nb.at[3, own], up, "y+"), send(nb.at[1, own], nb.at[2, own], down, "y-")]
    standardize(a_ref, na, center_a, inv_a)
    swap_a = send(na.at[own], na.at[other], partner)
    arrive(swap_b)
    first.append(send(nb.at[0, other], nb.at[3, other], up, "y+"))
    first.append(send(nb.at[1, other], nb.at[2, other], down, "y-"))

    diag_done = []

    def diagonal():
        def body(i, acc):
            rows = pl.ds(pl.multiple_of(i * 32, 32), 32)
            wide_a = (a_ref[rows, :].astype(f32) - center_a) * inv_a
            wide_b = (b_ref[rows, :].astype(f32) - center_b) * inv_b
            short_a, short_b = na[rows, :].astype(f32), nb16[rows, :].astype(f32)
            terms = (short_a, short_b, short_a * short_b, wide_a * short_b, wide_b * short_a)
            return tuple(s + jnp.sum(t, axis=0, keepdims=True) for s, t in zip(acc, terms))
        sums = lax.fori_loop(0, frames // 32, body, (jnp.zeros((1, width), f32),) * 5)
        for at, value in enumerate(sums[:3] + (jnp.zeros((1, width), f32),) + sums[3:]):
            diag_c[c, at // 2, at % 2 : at % 2 + 1, :] = value
        work(1.5)
        copies = spread_to(diag_c, c, [partner])
        yield copies
        diag_x[x] = jnp.where(
            c == 0, diag_c[0, :, :, :half] + diag_c[1, :, :, :half],
            diag_c[0, :, :, half:] + diag_c[1, :, :, half:])
        copies = spread_to(diag_x, x, peers_x)
        yield copies
        diag_z[z] = sum(diag_x[i] for i in range(nx))
        copies = spread_to(diag_z, z, peers_z)
        yield copies
        diag_f[c] = sum(diag_z[i] for i in range(nz)) / total
        mean_b16[0] = diag_f[c, 0, 1:2]
        copies = spread_to(diag_f, c, [partner])
        copies += [send(mean_b16.at[0], mean_b16.at[SLOT[ny - k]], peers_y[k - 1]) for k in range(1, ny)]
        yield copies
        mean_a = jnp.concatenate([diag_f[0, 0, 0:1], diag_f[1, 0, 0:1]], axis=1)
        na[pl.ds(both, 16), :] = jnp.broadcast_to(mean_a, (16, width)).astype(bf16)
        for p, (slot, side) in enumerate(PIECES):
            mean_b = mean_b16[slot, :, side * piece : (side + 1) * piece]
            nb[p, pl.ds(both, 16), :] = jnp.broadcast_to(mean_b, (16, piece)).astype(bf16)
        diag_done.append(True)

    def correlate(first):
        work(1.5)
        def body(i, _):
            rows = pl.ds(pl.multiple_of(i * 256, 256), 256)
            for p in (first, first + 1):
                part[p, rows, :] = jnp.dot(nat[rows, :], nb[p, :both, :], preferred_element_type=f32)
            return 0
        lax.fori_loop(0, width // 256, body, 0)

    def sweep(group, rows, fn):
        first, count, _, columns = group
        work(0.004 * rows * count * columns / 1024)
        step = min(rows, 32)
        turns = count * (rows // step)
        per = min(turns, max(1, 16384 // (step * columns)))
        def body(i, _):
            stores = []
            for u in range(per):
                k = i * per + u
                p = first + k // (rows // step)
                r = k % (rows // step) * step if isinstance(k, int) else lax.rem(k, rows // step) * step
                stores += fn(p, r, step)
            for ref, at, value in stores:
                ref[at] = value
            return 0
        if turns == per:
            body(0, 0)
        else:
            lax.fori_loop(0, turns // per, body, 0)

    def strip(base, step):
        return pl.ds(base if isinstance(base, int) else pl.multiple_of(base, 16), step)

    def reduce_chain(group, base, rows, n, at, plus, minus, axis, off, bufs):
        out_p1, out_m1, out_p2, out_m2, in_p1, in_m1, in_p2, in_m2 = bufs
        far = n // 2
        first, count, column, columns = group
        some, window, every = pl.ds(first, count), pl.ds(off, rows), pl.ds(column, columns)
        left, right = pl.ds(column, columns // 2), pl.ds(column + columns // 2, columns // 2)
        short = pl.ds(column // 2, columns // 2)

        def pack(s, source, cols, out1, out2, in1, in2):
            rest = right if cols is left else left
            def fn(p, r, step):
                there = strip(source + r, step)
                here = strip(off + r, step)
                if s == 1:
                    return [(out1, (p, here, short), encode(part[p, there, cols]))]
                if s > 2:
                    value = encode(part[p, there, every] + decode(in2[s - 3, p, here, every]))
                    return [(out2, (s - 2, p, here, every), value)]
                value = encode(part[p, there, cols] + decode(in1[p, here, short]))
                return [
                    (out2, (0, p, here, cols), value),
                    (out2, (0, p, here, rest), encode(part[p, there, rest])),
                ]
            return fn

        for s in range(1, far + 1):
            distance = far + 1 - s
            go_p = pack(s, base + lax.rem(at + distance, n) * rows, left, out_p1, out_p2, in_p1, in_p2)
            go_m = pack(s, base + lax.rem(at + n - distance, n) * rows, right, out_m1, out_m2, in_m1, in_m2)
            sweep(group, rows, lambda p, r, step: go_p(p, r, step) + go_m(p, r, step))
            def view(ref1, ref2):
                return ref1.at[some, window, short] if s == 1 else ref2.at[s - 2, some, window, every]
            go = [
                send(view(out_p1, out_p2), view(in_p1, in_p2), plus, axis + "+"),
                send(view(out_m1, out_m2), view(in_m1, in_m2), minus, axis + "-"),
            ]
            yield go

        def finish(p, r, step):
            there = strip(base + at * rows + r, step)
            here = strip(off + r, step)
            value = part[p, there, every] + decode(in_p2[far - 2, p, here, every])
            return [(part, (p, there, every), value + decode(in_m2[far - 2, p, here, every]))]
        sweep(group, rows, finish)

    def gather_chain(group, base, rows, n, at, plus, minus, axis):
        far = n // 2
        first, count, column, columns = group
        some, every = pl.ds(first, count), pl.ds(column, columns)
        left, right = pl.ds(column, columns // 2), pl.ds(column + columns // 2, columns // 2)
        for s in range(1, far + 1):
            cols_p, cols_m = (left, right) if s == far else (every, every)
            from_p = base + lax.rem(at + n - (s - 1), n) * rows
            from_m = base + lax.rem(at + (s - 1), n) * rows
            ref_p = slope.at[some, strip(from_p, rows), cols_p]
            ref_m = slope.at[some, strip(from_m, rows), cols_m]
            yield [send(ref_p, ref_p, plus, axis + "+"), send(ref_m, ref_m, minus, axis + "-")]

    plus_x, minus_x = device(dx=1), device(dx=nx - 1)
    plus_z, minus_z = device(dz=1), device(dz=nz - 1)
    rows_x, rows_z, rows_o = width // nx, width // nz, width // (nx * nz)
    base_x = x * rows_x
    base_z = z * rows_z
    bufs_x = (sx_p1, sx_m1, sx_p2, sx_m2, rx_p1, rx_m1, rx_p2, rx_m2)
    bufs_z = (sz_p1, sz_m1, sz_p2, sz_m2, rz_p1, rz_m1, rz_p2, rz_m2)

    def slopes(group, base):
        first, count, column, columns = group
        rows, cols = strip(base, rows_o), pl.ds(column, columns)
        row_ids = lax.broadcasted_iota(jnp.int32, (rows_o, columns), 0) + base
        col_ids = lax.broadcasted_iota(jnp.int32, (rows_o, columns), 1) + (c * half + column)
        for p in range(first, first + count):
            value = 2.0 * off_weight * (part[p, rows, cols] / total)
            if p < 2:
                value = jnp.where(row_ids == col_ids + p * piece, 0.0, value)
            slope[p, rows, cols] = value.astype(bf16)

    def one_way(group):
        yield from reduce_chain(group, 0, rows_x, nx, x, plus_x, minus_x, "x", 0, bufs_x)
        yield from reduce_chain(group, base_x, rows_o, nz, z, plus_z, minus_z, "z", rows_z, bufs_z)
        slopes(group, base_x + z * rows_o)
        yield from gather_chain(group, base_x, rows_o, nz, z, plus_z, minus_z, "z")
        yield from gather_chain(group, 0, rows_x, nx, x, plus_x, minus_x, "x")

    def other_way(group):
        yield from reduce_chain(group, 0, rows_z, nz, z, plus_z, minus_z, "z", 0, bufs_z)
        yield from reduce_chain(group, base_z, rows_o, nx, x, plus_x, minus_x, "x", rows_x, bufs_x)
        slopes(group, base_z + x * rows_o)
        yield from gather_chain(group, base_z, rows_o, nx, x, plus_x, minus_x, "x")
        yield from gather_chain(group, 0, rows_z, nz, z, plus_z, minus_z, "z")

    live = []

    def spawn(rank, task):
        live.append([rank, len(started), task, []])

    def run():
        while live:
            best = None
            for entry in live:
                rank, _, _, wait = entry
                if callable(wait):
                    if not wait():
                        continue
                    ready = clock[0]
                else:
                    ready = max([clock[0]] + [due[id(copy)] for copy in wait])
                key = (max(ready, clock[0] + 0.2), rank)
                if best is None or key < best[0]:
                    best = (key, entry)
            entry = best[1]
            if not callable(entry[3]):
                arrive(entry[3])
            entry[3] = next(entry[2], None)
            if entry[3] is None:
                live.remove(entry)

    def group(rank, ways, first, post):
        left = [len(ways)]
        def chain(way, what):
            yield from way(what)
            left[0] -= 1
            if not left[0]:
                yield lambda: diag_done
                yield from post
        for at, way in enumerate(ways):
            pieces = 2 // len(ways)
            spawn(rank, chain(way, (first + at * pieces, pieces, 0, piece)))

    def to_b(first):
        work(1.5)
        for p in (first, first + 1):
            part_b[p] = jnp.dot(na[...], slope[p], preferred_element_type=f32)

    begun = []

    def to_a(first):
        fresh = not begun
        work(2.0)
        begun.append(first)
        def body(i, _):
            rows = pl.ds(pl.multiple_of(i * 256, 256), 256)
            acc = None if fresh else back_a[:, rows]
            for p in (first, first + 1):
                term = lax.dot_general(
                    nb[p], slope[p, rows, :], (((1,), (1,)), ((), ())), preferred_element_type=f32)
                acc = term if acc is None else acc + term
            back_a[:, rows] = acc
            return 0
        lax.fori_loop(0, width // 256, body, 0)

    def squares(first):
        work(0.6)
        for p in (first, first + 1):
            def body(i, acc, p=p):
                rows = pl.ds(pl.multiple_of(i * 64, 64), 64)
                s = slope[p, rows, :].astype(f32)
                s = s * s
                row_acc[rows, :] += sum(s[:, k * 128 : (k + 1) * 128] for k in range(piece // 128))
                return acc + jnp.sum(s, axis=0, keepdims=True)
            square[p] = lax.fori_loop(0, width // 64, body, jnp.zeros((1, piece), f32))

    def code(out, base, extra):
        work(0.5)
        def body(i, _):
            rows = pl.ds(pl.multiple_of(i * 64, 64), 64)
            value = part_b[base, rows, :]
            if extra is not None:
                value = value + decode(ry[extra, rows, :])
            sy[out, rows, :] = encode(value)
            return 0
        lax.fori_loop(0, both // 64, body, 0)

    def gain(base, extra):
        work(0.5)
        def body(i, _):
            rows = pl.ds(pl.multiple_of(i * 64, 64), 64)
            part_b[base, rows, :] += decode(ry[extra, rows, :])
            return 0
        lax.fori_loop(0, both // 64, body, 0)

    done, last_y = [], []

    def post(first):
        to_b(first)
        if first:
            copies = []
            if first == 6:
                yield lambda: "far" in done
            for p, peer, link in ((first, up, "y+"), (first + 1, down, "y-")):
                code(p - 2, p, p - 4 if first == 6 else None)
                if first == 6:
                    last_y.extend(
                        send(sy.at[p - 2, rows], ry.at[p - 2, rows], peer, link) for rows in (other, own))
                else:
                    copies.append(send(sy.at[p - 2], ry.at[p - 2], peer, link))
            if first < 6:
                spawn(0, after_y(first, copies))
            yield []
        else:
            done.append("own")
        to_a(first)
        squares(first)

    def after_y(first, copies):
        yield copies
        if first == 4:
            done.append("far")
            return
        yield lambda: "own" in done
        gain(1, 0)
        gain(0, 1)

    def blocks():
        yield first
        second = [send(nb.at[3, :both], nb.at[4, :both], up, "y+"), send(nb.at[2, :both], nb.at[5, :both], down, "y-")]
        third = [send(nb.at[1, :both], nb.at[7, :both], up, "y+"), send(nb.at[0, :both], nb.at[6, :both], down, "y-")]
        correlate(2)
        group(RANKS[1], WAYS[1], 2, post(2))
        yield second
        correlate(4)
        group(RANKS[2], WAYS[2], 4, post(4))
        yield third
        correlate(6)
        group(RANKS[3], WAYS[3], 6, post(6))

    WAYS = [[one_way, other_way], [one_way], [other_way], [one_way]]
    RANKS = [4, 3, 2, 1]

    row_acc[...] = jnp.zeros_like(row_acc)
    arrive([swap_a])
    for i in range(width // 128):
        cols = pl.ds(i * 128, 128)
        nat[cols, :] = jnp.transpose(na[:both, cols].astype(f32)).astype(bf16)
    work(2.0)
    correlate(0)
    spawn(0, blocks())
    group(RANKS[0], WAYS[0], 0, post(0))
    spawn(2, diagonal())
    run()

    swap_back = send(back_a.at[other, :], recv_a, partner)

    scale = 1.0 / (2.0 * off_weight)
    corr_half = diag_f[c, 1, 0:1]
    loss_off = jnp.sum(sum(square[p] for p in range(count)), axis=1, keepdims=True)
    loss_diag = jnp.sum((1.0 - corr_half) ** 2, axis=1, keepdims=True)
    loss_row = jnp.broadcast_to(loss_off * (off_weight * scale * scale) + loss_diag, (1, half))
    for p in range(slots):
        block = extra_y.at[ny + p] if p else extra_y.at[m]
        left, right = PIECES.index((p, 0)), PIECES.index((p, 1))
        block[0:1, :piece] = part_b[left, both : both + 1, :]
        block[0:1, piece:] = part_b[right, both : both + 1, :]
        block[1:2, :piece] = square[left] * scale
        block[1:2, piece:] = square[right] * scale
        block[2:3, :] = loss_row
        block[3:4, :] = jnp.zeros((1, half), f32)
    share_y = [
        send(extra_y.at[ny + SLOT[k]], extra_y.at[m], peers_y[k - 1]) for k in range(1, ny)
    ]
    extra_a[c, 0:1, :] = back_a[both : both + 1, :]
    extra_a[c, 1:2, :] = jnp.sum(jnp.transpose(row_acc[...]), axis=0, keepdims=True) * scale
    share_a = send(extra_a.at[c], extra_a.at[c], partner)

    diag = jnp.concatenate([diag_f[0], diag_f[1]], axis=2)
    mean_a16, mean_own_b16 = diag[0, 0:1], diag[0, 1:2]
    corr_ii = diag[1, 0:1]
    cross_a, cross_b = diag[2, 0:1], diag[2, 1:2]
    slope_ii = (-2.0 * (1.0 - corr_ii)).astype(bf16).astype(f32)

    arrive([share_a])
    last_a = extra_a[0] + extra_a[1]
    mean_a = last_a[0:1] + mean_own_b16 * slope_ii
    inner_a = last_a[1:2] + cross_a * slope_ii
    arrive([swap_back])

    def finish_a(i, _):
        rows = pl.ds(pl.multiple_of(i * 32, 32), 32)
        wide = (a_ref[rows, :].astype(f32) - center_a) * inv_a
        back = back_a[rows, :] + recv_a[rows, :] + slope_ii * nb16[rows, :].astype(f32)
        ga_ref[rows, :] = (inv_a * (back - mean_a - wide * inner_a)).astype(bf16)
        return 0

    lax.fori_loop(0, frames // 32, finish_a, 0)

    arrive(share_y)
    extra_c[c] = sum(extra_y[i] for i in range(ny))
    share_c = send(extra_c.at[c], extra_c.at[c], partner)

    def add_last(base, dst, at):
        for side, got in ((0, 4), (1, 5)):
            cols = pl.ds(at if isinstance(at, int) else pl.multiple_of(at + side * piece, 128), piece)
            if isinstance(at, int):
                cols = pl.ds(side * piece, piece)
            def body(i, _, side=side, got=got, cols=cols):
                rows = pl.ds(pl.multiple_of(base + i * 64, 64), 64)
                here = pl.ds(pl.multiple_of(i * 64, 64), 64)
                dst[here, cols] = part_b[side, rows, :] + decode(ry[got, rows, :])
                return 0
            lax.fori_loop(0, frames // 64, body, 0)

    late = last_y + [swap_back, share_a, share_c] + share_y
    late = [id(copy) for copy in late]
    for copy in started:
        if id(copy) not in late:
            copy.wait_send()
    before = len(started)
    arrive(last_y[0::2])
    add_last(frames, sum_b, 0)
    swap_sum = [send(sum_b, full_b.at[:, own_half], partner)]
    arrive(last_y[1::2])
    add_last(0, full_b, c * half)

    arrive([share_c])
    mean_b = jnp.concatenate([extra_c[0, 0:1], extra_c[1, 0:1]], axis=1) + mean_a16 * slope_ii
    inner_b = jnp.concatenate([extra_c[0, 1:2], extra_c[1, 1:2]], axis=1) + cross_b * slope_ii
    loss_ref[...] = jnp.broadcast_to(extra_c[0, 2:3, :128] + extra_c[1, 2:3, :128], (8, 128))
    arrive(swap_sum)

    def finish_b(i, _):
        rows = pl.ds(pl.multiple_of(i * 32, 32), 32)
        wide = (b_ref[rows, :].astype(f32) - center_b) * inv_b
        back = full_b[rows, :] + slope_ii * na[rows, :].astype(f32)
        gb_ref[rows, :] = (inv_b * (back - mean_b - wide * inner_b)).astype(bf16)
        return 0

    lax.fori_loop(0, frames // 32, finish_b, 0)
    for at, copy in enumerate(started):
        if at >= before or id(copy) in late:
            copy.wait_send()


def solution(mesh):
    ny = mesh.shape["mp"]
    members = mesh.shape["dp"]
    nx = ny
    nz = members // (2 * nx)

    def per_device(view_a, view_b):
        frames, width = view_a.shape
        both, half = 2 * frames, width // 2
        rows_x, rows_z, rows_o = width // nx, width // nz, width // (nx * nz)
        vmem = pltpu.VMEM
        rings = []
        count, piece = 2 * ny, half // 2
        scratch = [
            vmem((frames, width), bf16),
            vmem((both + 16, width), bf16),
            vmem((width, both), bf16),
            vmem((count, both + 16, piece), bf16),
            vmem((count, width, piece), f32),
            vmem((count, width, piece), bf16),
            vmem((both + 16, width), f32),
            vmem((count, both + 16, piece), f32),
            vmem((frames, half), f32),
            vmem((frames, width), f32),
            vmem((2, 2, 2, width), f32),
            vmem((nx, 2, 2, width), f32),
            vmem((nz, 2, 2, width), f32),
            vmem((2, 3, 2, width), f32),
            vmem((nx, 3, 2, half), f32),
            vmem((nz, 3, 2, half), f32),
            vmem((2, 3, 2, half), f32),
            vmem((ny, 1, half), f32),
            vmem((count, 1, piece), f32),
            vmem((2 * ny, 4, half), f32),
            vmem((2, 4, half), f32),
            vmem((2, 2, width), f32),
            vmem((width, 128), f32),
        ]
        for rows, n in ((rows_x + rows_o, nx), (rows_z + rows_o, nz)):
            ring = [vmem((count, rows, piece // 2), bf16)] * 2
            rings.append(ring + [vmem((n // 2 - 1, count, rows, piece), bf16)] * 2)
        scratch += rings[0] + rings[1] + rings[0] + rings[1] + [vmem((count - 2, both, piece), bf16)] * 2 + [
            vmem((frames, width), f32),
            pltpu.SemaphoreType.DMA((256,)),
            pltpu.SemaphoreType.DMA((256,)),
        ]
        grad_a, grad_b, loss = pl.pallas_call(
            functools.partial(kernel, nx, nz, ny, float(frames * members)),
            out_shape=(
                jax.ShapeDtypeStruct((frames, width), bf16),
                jax.ShapeDtypeStruct((frames, width), bf16),
                jax.ShapeDtypeStruct((8, 128), f32),
            ),
            in_specs=[pl.BlockSpec(memory_space=vmem)] * 2,
            out_specs=[pl.BlockSpec(memory_space=vmem)] * 3,
            scratch_shapes=scratch,
            compiler_params=pltpu.CompilerParams(
                collective_id=0, has_side_effects=True, vmem_limit_bytes=56 * 1024 * 1024
            ),
            cost_estimate=pl.CostEstimate(
                flops=3 * 2 * both * width * half * ny, bytes_accessed=4 * frames * width * 2,
                transcendentals=0),
        )(view_a, view_b)
        return grad_a, grad_b, loss[0, 0]

    placed = P("dp", "mp")
    return jax.shard_map(
        per_device,
        mesh=mesh,
        in_specs=(placed, placed),
        out_specs=(placed, placed, P()),
        check_vma=False,
    )
```
